32 devices in a mesh: groups: 2 (over y), leaf: 4 (over z), sub: 4 (over x, core), pair: 1.
Axes of the slice: x: 2, y: 2, z: 4, core: 2. Of those that a mesh axis runs over, the one named last changes fastest.
Arguments:
- points: float32 [16, 65536], P(None, ('groups', 'leaf', 'sub')), parts along dimension 1, may hold values from -3 to 3
- vectors: float32 [32, 65536], P(None, ('groups', 'leaf', 'sub')), parts along dimension 1, may hold values from -6 to 6
- basis: float32 [64, 64, 1024], P(('groups', 'leaf', 'sub')), parts along dimension 0, may hold values from -0.1875 to 0.1875
- transfer: float32 [64, 64, 64], P(('groups', 'leaf', 'sub')), parts along dimension 0, may hold values from -0.75 to 0.75
- skeleton: float32 [64, 16, 64], P(('groups', 'leaf', 'sub')), parts along dimension 0, may hold values from -3 to 3
- parent_skel: float32 [8, 16, 64], P('groups'), parts along dimension 0, may hold values from -3 to 3
- near_list: int32 [64, 6], P(('groups', 'leaf')), parts along dimension 0, may hold values from 0 to 31, as said below
- near_count: int32 [64], P(('groups', 'leaf')), parts along dimension 0, may hold values from 1 to 6, as said below
- far_list: int32 [64, 8], P(('groups', 'leaf', 'sub')), parts along dimension 0, may hold values from 0 to 31, as said below
- parent_far: int32 [8, 3], P(('groups', 'leaf')), parts along dimension 0, may hold values from 0 to 3, as said below
Outputs:
- product: float32 [32, 65536], P(None, ('groups', 'leaf', 'sub')), parts along dimension 1
The draws below stay inside these ranges and needn't reach their ends.
There are 2 independent parts, one for each index of `groups`. The reference program is written for one: setup_inputs(seed, part) draws one part's arguments, and reference() takes and returns one part's arrays. A program takes and returns all parts, laid end to end along the dimension named above; each array names one. Nothing has to cross between parts.
Inputs may be any that keep to these rules, and one draw needn't show every extreme that they name: `near_list`: row i begins with i itself, followed by distinct other leaves of the same subtree (the 8 consecutive leaves holding i); only its first near_count[i] entries are used. `near_count`: every subtree has a leaf whose count is exactly 6. `far_list`: each row holds distinct leaves outside the row's own subtree. `parent_far`: each row holds distinct subtrees other than the row's own.
All inputs are finite; a program needn't handle non-finite values.
Results may differ from the reference program's by a relative error of at most 0.0001.
Values sent between devices are 32-bit elements; how exact they have to be, the bound alone decides.
No kernel may reach another device: no remote copies, remote signals or barrier semaphores. Data moves between devices by JAX's collectives and lax.ppermute only.
A program may use at most 64 MiB of HBM per device.

```python
import jax
import jax.numpy as jnp
from jax import lax

LP = 1024
DIM = 16
NV = 32
R = 64
FAR1 = 8
FAR2 = 3
SUBLEAF = 8
NLEAF = 32
NPAR = 4
NPTS = 32768
NEAR = 6


def draw_near_list(key, part):
    key = jax.random.fold_in(key, 11)
    scores = jax.random.randint(key, (NLEAF, SUBLEAF), 0, 1 << 20) * SUBLEAF + jnp.arange(SUBLEAF)[None, :]
    local_self = jnp.arange(NLEAF) % SUBLEAF
    scores = jnp.where(jnp.arange(SUBLEAF)[None, :] == local_self[:, None], -1, scores)
    order = jnp.argsort(scores, axis=1, stable=True)[:, :NEAR]
    first_leaf = jnp.arange(NLEAF) // SUBLEAF * SUBLEAF
    return (order + first_leaf[:, None]).astype(jnp.int32)


def draw_near_count(key, part):
    key = jax.random.fold_in(key, 12)
    draw_key, pick_key = jax.random.split(key)
    raw_value = jax.random.randint(draw_key, (NLEAF,), 0, NEAR)
    floor_count = max(NEAR // 3, 1)
    counts = jnp.minimum(floor_count + raw_value * raw_value * raw_value // (NEAR * NEAR), NEAR)
    chosen = jax.random.randint(pick_key, (NLEAF // SUBLEAF,), 0, SUBLEAF)
    local_index = jnp.arange(NLEAF) % SUBLEAF
    subtree = jnp.arange(NLEAF) // SUBLEAF
    counts = jnp.where(local_index == chosen[subtree], NEAR, counts)
    return counts.astype(jnp.int32)


def draw_far_list(key, part):
    key = jax.random.fold_in(key, 13)
    scores = jax.random.randint(key, (NLEAF, NLEAF), 0, 1 << 16) * NLEAF + jnp.arange(NLEAF)[None, :]
    subtree = jnp.arange(NLEAF) // SUBLEAF
    scores = jnp.where(subtree[None, :] == subtree[:, None], 1 << 30, scores)
    order = jnp.argsort(scores, axis=1, stable=True)[:, :FAR1]
    return order.astype(jnp.int32)


def draw_parent_far(key, part):
    key = jax.random.fold_in(key, 14)
    scores = jax.random.randint(key, (NPAR, NPAR), 0, 1 << 16) * NPAR + jnp.arange(NPAR)[None, :]
    scores = jnp.where(jnp.arange(NPAR)[None, :] == jnp.arange(NPAR)[:, None], 1 << 30, scores)
    order = jnp.argsort(scores, axis=1, stable=True)[:, :FAR2]
    return order.astype(jnp.int32)


def steps_of(rng, dims, cuts, least, high):
    factor_of = 1.0
    for dim, shards_of in cuts:
        heights = jax.random.uniform(jax.random.fold_in(jax.random.fold_in(rng, 6), dim), (shards_of,), jnp.float32, least / len(cuts), high / len(cuts))
        factor_of = factor_of * jnp.repeat(jnp.exp(heights), dims[dim] // shards_of).reshape((-1,) + (1,) * (len(dims) - 1 - dim))
    return factor_of


def bell_draw(own_key, extent, deviation, limit, cuts=(), kind=jnp.bfloat16):
    gain = steps_of(own_key, extent, cuts, -0.22, 0.18) if cuts else 1.0
    drawn = jax.random.normal(own_key, extent, jnp.float32) * deviation * gain
    return jnp.minimum(jnp.maximum(drawn, -limit), limit).astype(kind)


def setup_inputs(seed: int = 0, part: int = 0) -> dict:
    streams_of = jax.random.split(jax.random.key(seed), 11)
    part_keys = jax.random.split(jax.random.fold_in(streams_of[10], part), 11)
    points = bell_draw(part_keys[0], (DIM, NPTS), 0.5, 3.0, ((1, 16),), jnp.float32)
    vectors = bell_draw(part_keys[1], (NV, NPTS), 1.0, 6.0, ((1, 16),), jnp.float32)
    basis = bell_draw(part_keys[2], (NLEAF, R, LP), LP ** -0.5, 0.1875, ((0, 16),), jnp.float32)
    transfer = bell_draw(part_keys[3], (NLEAF, R, R), R ** -0.5, 0.75, ((0, 16),), jnp.float32)
    skeleton = bell_draw(part_keys[4], (NLEAF, DIM, R), 0.5, 3.0, ((0, 16),), jnp.float32)
    parent_skel = bell_draw(part_keys[5], (NPAR, DIM, R), 0.5, 3.0, (), jnp.float32)
    near_list = draw_near_list(jax.random.fold_in(jax.random.fold_in(streams_of[10], part), 71), part)
    near_count = draw_near_count(jax.random.fold_in(jax.random.fold_in(streams_of[10], part), 71), part)
    far_list = draw_far_list(jax.random.fold_in(jax.random.fold_in(streams_of[10], part), 71), part)
    parent_far = draw_parent_far(jax.random.fold_in(jax.random.fold_in(streams_of[10], part), 71), part)
    return {"points": points, "vectors": vectors, "basis": basis, "transfer": transfer, "skeleton": skeleton, "parent_skel": parent_skel, "near_list": near_list, "near_count": near_count, "far_list": far_list, "parent_far": parent_far}


WIDTH = 0.125
PRECISE = lax.Precision.HIGHEST


def kernel_block(source, target):
    cross_term = jnp.einsum("da,db->ab", source, target, precision=PRECISE)
    lengths = jnp.sum(source * source, axis=0)[:, None] + jnp.sum(target * target, axis=0)[None, :] - 2.0 * cross_term
    return jnp.exp(-WIDTH * lengths)


def tile_product(source, source_vectors, target):
    columns = target.shape[1]
    stride = min(512, columns)
    pieces = [jnp.dot(source_vectors, kernel_block(source, target[:, offset:offset + stride]), precision=PRECISE) for offset in range(0, columns, stride)]
    return jnp.concatenate(pieces, axis=1)


def couple(source, target):
    cross_term = jnp.einsum("...db,...da->...ba", source, target, precision=PRECISE)
    lengths = jnp.sum(source * source, axis=-2)[..., :, None] + jnp.sum(target * target, axis=-2)[..., None, :] - 2.0 * cross_term
    return jnp.exp(-WIDTH * lengths)


def reference(points, vectors, basis, transfer, skeleton, parent_skel, near_list, near_count, far_list, parent_far):
    def near_leaf(leaf_index):
        target = lax.dynamic_slice_in_dim(points, leaf_index * LP, LP, 1)

        def add_tile(position, summed):
            partner = near_list[leaf_index, position]
            source = lax.dynamic_slice_in_dim(points, partner * LP, LP, 1)
            source_vectors = lax.dynamic_slice_in_dim(vectors, partner * LP, LP, 1)
            return summed + tile_product(source, source_vectors, target)

        return lax.fori_loop(0, near_count[leaf_index], add_tile, jnp.zeros((NV, LP), jnp.float32))

    near_all = lax.map(near_leaf, jnp.arange(NLEAF, dtype=jnp.int32)) * (LP ** -0.5)
    leaf_vectors = vectors.reshape(NV, NLEAF, LP)
    coefs = jnp.einsum("nlp,lrp->lnr", leaf_vectors, basis, precision=PRECISE)
    couplings = couple(skeleton[far_list], skeleton[:, None])
    gathered = jnp.einsum("lhnb,lhba->lna", coefs[far_list], couplings, precision=PRECISE) * (R ** -0.5)
    far_part = jnp.einsum("lna,lap->lnp", gathered, basis, precision=PRECISE)
    lifted = jnp.einsum("lnr,lrs->lns", coefs, transfer, precision=PRECISE)
    parent_coef = lifted.reshape(NPAR, SUBLEAF, NV, R).sum(axis=1)
    links_upper = couple(parent_skel[parent_far], parent_skel[:, None])
    upper_field = jnp.einsum("phnb,phba->pna", parent_coef[parent_far], links_upper, precision=PRECISE) * (R ** -0.5)
    spread = jnp.repeat(upper_field, SUBLEAF, axis=0)
    downward = jnp.einsum("lna,lba->lnb", spread, transfer, precision=PRECISE)
    down_part = jnp.einsum("lnb,lbp->lnp", downward, basis, precision=PRECISE)
    mixed = (near_all + far_part) + down_part
    return jnp.transpose(mixed, (1, 0, 2)).reshape(NV, NLEAF * LP)
```

```python
import functools
import math

import jax
import jax.numpy as jnp
from jax import lax
from jax.experimental import pallas as pl
from jax.experimental.pallas import tpu as pltpu
from jax.sharding import PartitionSpec as P

RATE = 0.125 * math.log2(math.e)
STRIP = 256
F32, BF16 = jnp.float32, jnp.bfloat16
VMEM = pl.BlockSpec(memory_space=pltpu.VMEM)
SMEM = pl.BlockSpec(memory_space=pltpu.SMEM)
PARAMS = pltpu.CompilerParams(vmem_limit_bytes=40 * 1024 * 1024)
NN, NT = (((1,), (0,)), ((), ())), (((1,), (1,)), ((), ()))


def mxu(x, y, dims=NN):
    return lax.dot_general(x, y, dims, preferred_element_type=F32)


def split2(x):
    high = x.astype(BF16)
    return high, (x - high.astype(F32)).astype(BF16)


def split3(x):
    high = x.astype(BF16).astype(F32)
    rest = x - high
    middle = rest.astype(BF16).astype(F32)
    return high, middle, (rest - middle).astype(BF16).astype(F32)


def product(x, y, dims=NN):
    x1, x2 = split2(x)
    y1, y2 = split2(y)
    return mxu(x1, y1, dims) + (mxu(x2, y1, dims) + mxu(x1, y2, dims))


def source_rows(x):
    a1, a2, a3 = split3(x * (2.0 * RATE))
    return jnp.concatenate([a1, a1, a2, a2, a1, a3], axis=0).T.astype(BF16)


def target_columns(x):
    b1, b2, b3 = split3(x)
    return jnp.concatenate([b1, b2, b1, b2, b3, b1], axis=0).astype(BF16)


def damping(x):
    return jnp.exp2(-RATE * jnp.sum(x * x, axis=0, keepdims=True))


def coef_kernel(leaves, vectors, basis, transfer, skeleton, packed):
    dim, rank = skeleton.shape[1:]
    width = basis.shape[2]
    vecs = vectors.shape[0]
    lift = 0.0
    for leaf in range(leaves):
        lanes = pl.ds(leaf * rank, rank)
        coef = product(vectors[:, leaf * width : (leaf + 1) * width], basis[leaf], NT)
        packed[0:dim, lanes] = skeleton[leaf]
        packed[dim : dim + vecs, lanes] = coef
        lift = lift + product(coef, transfer[leaf])
    rows = vecs // leaves
    for piece in range(leaves):
        packed[dim + vecs :, pl.ds(piece * rank, rank)] = lift[piece * rows : (piece + 1) * rows]


def coefficients(vectors, basis, transfer, skeleton):
    leaves, dim, rank = skeleton.shape
    vecs = vectors.shape[0]
    return pl.pallas_call(
        functools.partial(coef_kernel, leaves),
        out_shape=jax.ShapeDtypeStruct((dim + vecs + vecs // leaves, leaves * rank), F32),
        in_specs=[VMEM] * 4,
        out_specs=VMEM,
        compiler_params=PARAMS,
        name="coefficients",
    )(vectors, basis, transfer, skeleton)


def near_kernel(config, near_list, near_count, points, vectors, *refs):
    source_xor, target_xors, leaves, sources, width, has_start = config
    count = len(target_xors)
    targets, refs = refs[:count], refs[count:]
    starts, refs = (refs[:count], refs[count:]) if has_start else (None, refs)
    outs, (work, left, coefs, right, totals) = refs[:count], refs[count:]
    vecs = vectors.shape[0]
    group = near_list.shape[0]
    first = lax.axis_index("leaf") * group
    me = lax.axis_index("sub")
    source_base = 0 if source_xor is None else (me ^ source_xor) * leaves
    pair_size, pair_at = lax.axis_size("pair"), lax.axis_index("pair")

    todo = jnp.int32(0)
    for index, target_xor in enumerate(target_xors):
        for leaf in range(leaves):
            place = (me ^ target_xor) * leaves + leaf
            limit = near_count[place]
            for turn in range(near_list.shape[1]):
                source = near_list[place, turn] - first - source_base
                wanted = (turn < limit) & (source >= 0) & (source < sources)
                if pair_size > 1:
                    wanted = wanted & (pair_at == turn % pair_size)
                work[todo] = (index * leaves + leaf) * sources + source
                todo = todo + wanted.astype(jnp.int32)

    for source in range(sources):
        span = slice(source * width, (source + 1) * width)
        here = points[:, span]
        left[source] = source_rows(here)
        high, low = split2(vectors[:, span] * damping(here))
        coefs[source, 0:vecs] = high
        coefs[source, vecs:] = low
    for index in range(count):
        for leaf in range(leaves):
            slot = index * leaves + leaf
            right[slot] = target_columns(targets[index][:, leaf * width : (leaf + 1) * width])
            totals[slot] = jnp.zeros((vecs, width), F32)

    def tile(step, carry):
        slot = work[step] // sources
        source = work[step] % sources
        rows = left[source]
        both = coefs[source]
        for offset in range(0, width, STRIP):
            kernel = jnp.exp2(mxu(rows, right[slot, :, offset : offset + STRIP]))
            high, low = split2(kernel)
            top = mxu(both, high)
            found = top[:vecs] + (top[vecs:] + mxu(both[:vecs], low))
            totals[slot, :, offset : offset + STRIP] += found
        return carry

    lax.fori_loop(0, todo, tile, 0)
    for index in range(count):
        for leaf in range(leaves):
            span = slice(leaf * width, (leaf + 1) * width)
            scale = damping(targets[index][:, span]) * width**-0.5
            found = totals[index * leaves + leaf] * scale
            if has_start:
                found = found + starts[index][:, span]
            outs[index][:, span] = found


def near_field(lists, source, targets, source_xor, target_xors, leaves, starts=()):
    points, vectors = source
    near_list, near_count = lists
    dim, vecs = points.shape[0], vectors.shape[0]
    width = targets[0].shape[1] // leaves
    sources = points.shape[1] // width
    count = len(target_xors)
    slots = count * leaves
    config = (source_xor, target_xors, leaves, sources, width, bool(starts))
    return pl.pallas_call(
        functools.partial(near_kernel, config),
        out_shape=[jax.ShapeDtypeStruct((vecs, leaves * width), F32)] * count,
        in_specs=[SMEM, SMEM] + [VMEM] * (2 + count + len(starts)),
        out_specs=[VMEM] * count,
        scratch_shapes=[
            pltpu.SMEM((slots * near_list.shape[1] + 1,), jnp.int32),
            pltpu.VMEM((sources, width, 6 * dim), BF16),
            pltpu.VMEM((sources, 2 * vecs, width), BF16),
            pltpu.VMEM((slots, 6 * dim, width), BF16),
            pltpu.VMEM((slots, vecs, width), F32),
        ],
        compiler_params=PARAMS,
        name="near_field",
    )(near_list, near_count, points, vectors, *targets, *starts)


def interact(source, coefs, target):
    kernel = jnp.exp2(mxu(source_rows(source), target_columns(target)))
    return product(coefs * damping(source), kernel) * damping(target)


def far_kernel(place_of, leaves, subs, far_list, parent_far, *refs):
    gathered, (skeleton, parent_skel, transfer, basis, out) = refs[:-5], refs[-5:]
    dim, rank = skeleton.shape[1:]
    width = basis.shape[2]
    vecs = out.shape[0]

    def block(device):
        which, index = place_of(device)
        found = gathered[0][index]
        for other in range(1, len(gathered)):
            found = jnp.where(which == other, gathered[other][index], found)
        return found

    def lanes(data, at):
        found = data[:, :rank]
        for other in range(1, leaves):
            found = jnp.where(at == other, data[:, other * rank : (other + 1) * rank], found)
        return found

    points, coefs = [], []
    for turn in range(parent_far.shape[1]):
        parent = parent_far[0, turn]
        lift = block(parent * subs)[dim + vecs :]
        for sub in range(1, subs):
            lift = lift + block(parent * subs + sub)[dim + vecs :]
        coefs.append(
            jnp.concatenate([lift[:, at * rank : (at + 1) * rank] for at in range(leaves)], axis=0)
        )
        points.append(parent_skel[parent])
    own = parent_skel[lax.axis_index("leaf")]
    upper = interact(
        jnp.concatenate(points, axis=1), jnp.concatenate(coefs, axis=1), own
    ) * (rank**-0.5)

    for leaf in range(leaves):
        points, coefs = [], []
        for turn in range(far_list.shape[1]):
            partner = far_list[leaf, turn]
            data = lanes(block(partner // leaves), partner % leaves)
            points.append(data[:dim])
            coefs.append(data[dim : dim + vecs])
        far = interact(
            jnp.concatenate(points, axis=1), jnp.concatenate(coefs, axis=1), skeleton[leaf]
        ) * (rank**-0.5)
        field = far + product(upper, transfer[leaf], NT)
        out[:, leaf * width : (leaf + 1) * width] = product(field, basis[leaf])


def far_field(place_of, subs, far_list, parent_far, gathered, skeleton, parent_skel, transfer, basis):
    leaves, rank, width = basis.shape
    vecs = gathered[0].shape[1] - skeleton.shape[1]
    vecs = vecs * leaves // (leaves + 1)
    return pl.pallas_call(
        functools.partial(far_kernel, place_of, leaves, subs),
        out_shape=jax.ShapeDtypeStruct((vecs, leaves * width), F32),
        in_specs=[SMEM, SMEM] + [VMEM] * (len(gathered) + 4),
        out_specs=VMEM,
        compiler_params=PARAMS,
        name="far_field",
    )(far_list, parent_far, *gathered, skeleton, parent_skel, transfer, basis)


def swap(x, bit):
    size = lax.axis_size("sub")
    return lax.ppermute(x, "sub", [(at, at ^ bit) for at in range(size)])


def local(
    points,
    vectors,
    basis,
    transfer,
    skeleton,
    parent_skel,
    near_list,
    near_count,
    far_list,
    parent_far,
):
    leaves = basis.shape[0]
    subs, groups = lax.axis_size("sub"), lax.axis_size("leaf")
    lists = (near_list, near_count)
    own = (points, vectors)
    packed = coefficients(vectors, basis, transfer, skeleton)
    if subs == 4 and lax.axis_size("pair") == 1:
        cross = (swap(points, 2), swap(vectors, 2))
        twin_points = swap(points, 1)
        targets = (twin_points, points)
        line = [packed] + [
            lax.ppermute(packed, "leaf", [(at, (at + step) % groups) for at in range(groups)])
            for step in range(1, groups)
        ]
        first = near_field(lists, own, targets, 0, (1, 0), leaves)
        line = jnp.stack(line)
        plane = jnp.concatenate([line, swap(line, 2)])
        gathered = (plane, swap(plane, 1))
        (twin_near,) = near_field(lists, cross, (twin_points,), 2, (1,), leaves, (first[0],))
        back = swap(twin_near, 1)
        (near,) = near_field(lists, cross, (points,), 2, (0,), leaves, (first[1],))

        def place_of(device):
            away = (device % subs) ^ lax.axis_index("sub")
            step = (lax.axis_index("leaf") - device // subs + groups) % groups
            return away % 2, (away // 2) * groups + step

        near = near + back
    else:
        gathered = (lax.all_gather(packed, ("leaf", "sub")),)
        everyone = tuple(lax.all_gather(x, "sub", axis=1, tiled=True) for x in own)
        (near,) = near_field(lists, everyone, (points,), None, (0,), leaves)
        near = lax.psum(near, "pair")

        def place_of(device):
            return 0, device

    far = far_field(
        place_of, subs, far_list, parent_far, gathered, skeleton, parent_skel, transfer, basis
    )
    return near + far


def solution(mesh):
    placed = (
        P(None, ("groups", "leaf", "sub")),
        P(None, ("groups", "leaf", "sub")),
        P(("groups", "leaf", "sub"), None, None),
        P(("groups", "leaf", "sub"), None, None),
        P(("groups", "leaf", "sub"), None, None),
        P("groups", None, None),
        P(("groups", "leaf"), None),
        P(("groups", "leaf")),
        P(("groups", "leaf", "sub"), None),
        P(("groups", "leaf"), None),
    )
    return jax.shard_map(
        local,
        mesh=mesh,
        in_specs=placed,
        out_specs=P(None, ("groups", "leaf", "sub")),
        check_vma=False,
    )
```

```python
import functools
import math

import jax
import jax.numpy as jnp
from jax import lax
from jax.experimental import pallas as pl
from jax.experimental.pallas import tpu as pltpu
from jax.sharding import PartitionSpec as P

RATE = 0.125 * math.log2(math.e)
STRIP = 256
F32, BF16 = jnp.float32, jnp.bfloat16
VMEM = pl.BlockSpec(memory_space=pltpu.VMEM)
HBM = pl.BlockSpec(memory_space=pltpu.HBM)
SMEM = pl.BlockSpec(memory_space=pltpu.SMEM)
PARAMS = pltpu.CompilerParams(vmem_limit_bytes=40 * 1024 * 1024)
NN, NT = (((1,), (0,)), ((), ())), (((1,), (1,)), ((), ()))


def lasts(microseconds):
    return pl.CostEstimate(
        flops=int(1e9 * microseconds), bytes_accessed=int(3e6 * microseconds), transcendentals=0
    )


def mxu(x, y, dims=NN):
    return lax.dot_general(x, y, dims, preferred_element_type=F32)


def split2(x):
    high = x.astype(BF16)
    return high, (x - high.astype(F32)).astype(BF16)


def split3(x):
    high = x.astype(BF16).astype(F32)
    rest = x - high
    middle = rest.astype(BF16).astype(F32)
    return high, middle, (rest - middle).astype(BF16).astype(F32)


def product(x, y, dims=NN):
    x1, x2 = split2(x)
    y1, y2 = split2(y)
    return mxu(x1, y1, dims) + (mxu(x2, y1, dims) + mxu(x1, y2, dims))


def source_rows(x):
    a1, a2, a3 = split3(x * (2.0 * RATE))
    return jnp.concatenate([a1, a1, a2, a2, a1, a3], axis=0).T.astype(BF16)


def target_columns(x):
    b1, b2, b3 = split3(x)
    return jnp.concatenate([b1, b2, b1, b2, b3, b1], axis=0).astype(BF16)


def damping(x):
    return jnp.exp2(-RATE * jnp.sum(x * x, axis=0, keepdims=True))


def prepare_kernel(leaves, points, vectors, basis, transfer, skeleton, *refs):
    packed, left, coefs, right, scale = refs[:5]
    here, held, bases, moves, skeletons, sems = refs[5:]
    pairs = [(points, here), (vectors, held), (transfer, moves), (skeleton, skeletons)]
    pairs += [(basis.at[leaf], bases.at[leaf]) for leaf in range(leaves)]
    loads = [pltpu.make_async_copy(src, dst, sems.at[at]) for at, (src, dst) in enumerate(pairs)]
    for load in loads:
        load.start()
    dim, rank = skeletons.shape[1:]
    width = bases.shape[2]
    vecs = held.shape[0]
    spans = [slice(leaf * width, (leaf + 1) * width) for leaf in range(leaves)]
    loads[0].wait()
    fade = damping(here[...])
    scale[...] = fade * width**-0.5
    for leaf, span in enumerate(spans):
        left[leaf] = source_rows(here[:, span])
        right[leaf] = target_columns(here[:, span])
    loads[1].wait()
    for leaf, span in enumerate(spans):
        high, low = split2(held[:, span] * fade[:, span])
        coefs[leaf, 0:vecs] = high
        coefs[leaf, vecs:] = low
    loads[2].wait()
    loads[3].wait()
    lift = 0.0
    for leaf, span in enumerate(spans):
        loads[4 + leaf].wait()
        lanes = slice(leaf * rank, (leaf + 1) * rank)
        coef = product(held[:, span], bases[leaf], NT)
        packed[0:dim, lanes] = skeletons[leaf]
        packed[dim : dim + vecs, lanes] = coef
        lift = lift + product(coef, moves[leaf])
    rows = vecs // leaves
    for piece in range(leaves):
        packed[dim + vecs :, piece * rank : (piece + 1) * rank] = lift[
            piece * rows : (piece + 1) * rows
        ]


def prepare(points, vectors, basis, transfer, skeleton):
    leaves, dim, rank = skeleton.shape
    vecs = vectors.shape[0]
    width = basis.shape[2]
    inputs = [
        pltpu.with_memory_space_constraint(x, pltpu.HBM)
        for x in (points, vectors, basis, transfer, skeleton)
    ]
    return pl.pallas_call(
        functools.partial(prepare_kernel, leaves),
        out_shape=[
            jax.ShapeDtypeStruct((dim + vecs + vecs // leaves, leaves * rank), F32),
            jax.ShapeDtypeStruct((leaves, width, 6 * dim), BF16),
            jax.ShapeDtypeStruct((leaves, 2 * vecs, width), BF16),
            jax.ShapeDtypeStruct((leaves, 6 * dim, width), BF16),
            jax.ShapeDtypeStruct((1, leaves * width), F32),
        ],
        in_specs=[HBM] * 5,
        out_specs=[VMEM] * 5,
        scratch_shapes=[pltpu.VMEM(x.shape, F32) for x in inputs]
        + [pltpu.SemaphoreType.DMA((4 + leaves,))],
        compiler_params=PARAMS,
        cost_estimate=lasts(0.5),
        name="prepare",
    )(*inputs)


def near_kernel(config, near_list, near_count, *refs):
    source_xor, target_xor, leaves, sources, width, fresh_source, fresh_target, begun, last = config
    refs = list(refs)
    take = lambda count: [refs.pop(0) for _ in range(count)]
    given_source, given_target = take(2), take(1 if fresh_target else 2)
    start = take(1)[0] if begun else None
    out = take(1)[0]
    left, coefs = take(2) if fresh_source else given_source
    right, scale = take(2) if fresh_target else given_target
    (work,) = take(1)
    totals = take(1)[0] if last else out
    vecs = coefs.shape[1] // 2
    group = near_list.shape[0]
    first = lax.axis_index("leaf") * group
    me = lax.axis_index("sub")
    source_base = 0 if source_xor is None else (me ^ source_xor) * leaves
    pair_size, pair_at = lax.axis_size("pair"), lax.axis_index("pair")

    todo = jnp.int32(0)
    for leaf in range(leaves):
        place = (me ^ target_xor) * leaves + leaf
        limit = near_count[place]
        for turn in range(near_list.shape[1]):
            source = near_list[place, turn] - first - source_base
            wanted = (turn < limit) & (source >= 0) & (source < sources)
            if pair_size > 1:
                wanted = wanted & (pair_at == turn % pair_size)
            work[todo] = leaf * sources + source
            todo = todo + wanted.astype(jnp.int32)

    if fresh_source:
        points, vectors = given_source
        for source in range(sources):
            span = slice(source * width, (source + 1) * width)
            here = points[:, span]
            left[source] = source_rows(here)
            high, low = split2(vectors[:, span] * damping(here))
            coefs[source, 0:vecs] = high
            coefs[source, vecs:] = low
    if fresh_target:
        here = given_target[0]
        scale[...] = damping(here[...]) * width**-0.5
        for leaf in range(leaves):
            right[leaf] = target_columns(here[:, leaf * width : (leaf + 1) * width])
    for leaf in range(leaves):
        totals[leaf] = start[leaf] if begun else jnp.zeros((vecs, width), F32)

    def tile(step, carry):
        slot = work[step] // sources
        source = work[step] % sources
        chunks = [(y, x) for y in range(0, width, STRIP) for x in range(0, width, STRIP)]

        def exponent(y, x):
            return mxu(left[source, x : x + STRIP], right[slot, :, y : y + STRIP])

        ahead = exponent(*chunks[0])
        for at, (y, x) in enumerate(chunks):
            power = ahead
            if at + 1 < len(chunks):
                ahead = exponent(*chunks[at + 1])
            high, low = split2(jnp.exp2(power))
            both = coefs[source, :, x : x + STRIP]
            top = mxu(both, high)
            found = top[:vecs] + (top[vecs:] + mxu(both[:vecs], low))
            strip = found if x == 0 else strip + found
            if x + STRIP == width:
                totals[slot, :, y : y + STRIP] += strip
        return carry

    lax.fori_loop(0, todo, tile, 0)
    if last:
        for leaf in range(leaves):
            span = slice(leaf * width, (leaf + 1) * width)
            out[:, span] = totals[leaf] * scale[:, span]


def near_field(lists, source, target, source_xor, target_xor, leaves, start=None, last=False):
    near_list, near_count = lists
    fresh_source, fresh_target = source[0].ndim == 2, len(target) == 1
    if fresh_source:
        dim, vecs = source[0].shape[0], source[1].shape[0]
    else:
        dim, vecs = source[0].shape[2] // 6, source[1].shape[1] // 2
    width = target[-1].shape[1] // leaves
    sources = source[0].shape[1] // width if fresh_source else source[0].shape[0]
    config = (
        source_xor, target_xor, leaves, sources, width, fresh_source, fresh_target,
        start is not None, last,
    )
    totals = (leaves, vecs, width)
    shapes = [jax.ShapeDtypeStruct((vecs, leaves * width) if last else totals, F32)]
    if fresh_source:
        shapes += [
            jax.ShapeDtypeStruct((sources, width, 6 * dim), BF16),
            jax.ShapeDtypeStruct((sources, 2 * vecs, width), BF16),
        ]
    if fresh_target:
        shapes += [
            jax.ShapeDtypeStruct((leaves, 6 * dim, width), BF16),
            jax.ShapeDtypeStruct((1, leaves * width), F32),
        ]
    inputs = (*source, *target) + (() if start is None else (start,))
    scratch = [pltpu.SMEM((leaves * near_list.shape[1] + 1,), jnp.int32)]
    return pl.pallas_call(
        functools.partial(near_kernel, config),
        out_shape=shapes,
        in_specs=[SMEM, SMEM] + [VMEM] * len(inputs),
        out_specs=[VMEM] * len(shapes),
        scratch_shapes=scratch + ([pltpu.VMEM(totals, F32)] if last else []),
        compiler_params=PARAMS,
        cost_estimate=lasts(0.5),
        name="near_field",
    )(near_list, near_count, *inputs)


def interact(source, coefs, target):
    kernel = jnp.exp2(mxu(source_rows(source), target_columns(target)))
    return product(coefs * damping(source), kernel) * damping(target)


def far_kernel(place_of, leaves, subs, far_list, parent_far, *refs):
    gathered, (skeleton, parent_skel, transfer, basis, out) = refs[:-5], refs[-5:]
    dim, rank = skeleton.shape[1:]
    width = basis.shape[2]
    vecs = out.shape[0]

    def block(device):
        which, *index = place_of(device)
        found = gathered[0][tuple(index)]
        for other in range(1, len(gathered)):
            found = jnp.where(which == other, gathered[other][tuple(index)], found)
        return found

    def lanes(data, at):
        found = data[:, :rank]
        for other in range(1, leaves):
            found = jnp.where(at == other, data[:, other * rank : (other + 1) * rank], found)
        return found

    points, coefs = [], []
    for turn in range(parent_far.shape[1]):
        parent = parent_far[0, turn]
        lift = block(parent * subs)[dim + vecs :]
        for sub in range(1, subs):
            lift = lift + block(parent * subs + sub)[dim + vecs :]
        coefs.append(
            jnp.concatenate([lift[:, at * rank : (at + 1) * rank] for at in range(leaves)], axis=0)
        )
        points.append(parent_skel[parent])
    own = parent_skel[lax.axis_index("leaf")]
    upper = interact(
        jnp.concatenate(points, axis=1), jnp.concatenate(coefs, axis=1), own
    ) * (rank**-0.5)

    for leaf in range(leaves):
        points, coefs = [], []
        for turn in range(far_list.shape[1]):
            partner = far_list[leaf, turn]
            data = lanes(block(partner // leaves), partner % leaves)
            points.append(data[:dim])
            coefs.append(data[dim : dim + vecs])
        far = interact(
            jnp.concatenate(points, axis=1), jnp.concatenate(coefs, axis=1), skeleton[leaf]
        ) * (rank**-0.5)
        field = far + product(upper, transfer[leaf], NT)
        out[:, leaf * width : (leaf + 1) * width] = product(field, basis[leaf])


def far_field(place_of, subs, far_list, parent_far, gathered, skeleton, parent_skel, transfer, basis):
    leaves, rank, width = basis.shape
    vecs = gathered[0].shape[-2] - skeleton.shape[1]
    vecs = vecs * leaves // (leaves + 1)
    return pl.pallas_call(
        functools.partial(far_kernel, place_of, leaves, subs),
        out_shape=jax.ShapeDtypeStruct((vecs, leaves * width), F32),
        in_specs=[SMEM, SMEM] + [VMEM] * (len(gathered) + 4),
        out_specs=VMEM,
        compiler_params=PARAMS,
        cost_estimate=lasts(0.5),
        name="far_field",
    )(far_list, parent_far, *gathered, skeleton, parent_skel, transfer, basis)


def swap(x, bit):
    size = lax.axis_size("sub")
    return lax.ppermute(x, "sub", [(at, at ^ bit) for at in range(size)])


def local(
    points,
    vectors,
    basis,
    transfer,
    skeleton,
    parent_skel,
    near_list,
    near_count,
    far_list,
    parent_far,
):
    leaves = basis.shape[0]
    subs, groups = lax.axis_size("sub"), lax.axis_size("leaf")
    lists = (near_list, near_count)
    packed, *factors = prepare(points, vectors, basis, transfer, skeleton)
    own, own_target = factors[:2], factors[2:]
    if subs == 4 and lax.axis_size("pair") == 1:
        cross_points = swap(points, 2)
        column = jnp.stack([packed, swap(packed, 2)])
        cross = (cross_points, swap(vectors, 2))
        twin = (swap(points, 1),)
        (near,) = near_field(lists, own, own_target, 0, 0, leaves)
        column, near, twin = lax.optimization_barrier((column, near, twin))
        line = [
            lax.ppermute(column, "leaf", [(at, (at + step) % groups) for at in range(groups)])
            for step in range(1, groups)
        ]
        twin_near, *twin = near_field(lists, own, twin, 0, 1, leaves)
        line, twin_near = lax.optimization_barrier((line, twin_near))
        plane = jnp.stack([column] + line)
        gathered = (plane, swap(plane, 1))
        twin_near, *cross = near_field(lists, cross, twin, 2, 1, leaves, twin_near, True)
        back = swap(twin_near, 1)
        (near,) = near_field(lists, cross, own_target, 2, 0, leaves, near, True)

        def place_of(device):
            away = (device % subs) ^ lax.axis_index("sub")
            step = (lax.axis_index("leaf") - device // subs + groups) % groups
            return away % 2, step, away // 2

        near = near + back
    else:
        gathered = (lax.all_gather(packed, ("leaf", "sub")),)
        everyone = tuple(
            lax.all_gather(x, "sub", axis=1, tiled=True) for x in (points, vectors)
        )
        near, *_ = near_field(lists, everyone, own_target, None, 0, leaves, None, True)
        near = lax.psum(near, "pair")

        def place_of(device):
            return 0, device

    far = far_field(
        place_of, subs, far_list, parent_far, gathered, skeleton, parent_skel, transfer, basis
    )
    return near + far


def solution(mesh):
    placed = (
        P(None, ("groups", "leaf", "sub")),
        P(None, ("groups", "leaf", "sub")),
        P(("groups", "leaf", "sub"), None, None),
        P(("groups", "leaf", "sub"), None, None),
        P(("groups", "leaf", "sub"), None, None),
        P("groups", None, None),
        P(("groups", "leaf"), None),
        P(("groups", "leaf")),
        P(("groups", "leaf", "sub"), None),
        P(("groups", "leaf"), None),
    )
    return jax.shard_map(
        local,
        mesh=mesh,
        in_specs=placed,
        out_specs=P(None, ("groups", "leaf", "sub")),
        check_vma=False,
    )
```

```python
import functools
import math

import jax
import jax.numpy as jnp
from jax import lax
from jax.experimental import pallas as pl
from jax.experimental.pallas import tpu as pltpu
from jax.sharding import PartitionSpec as P

RATE = 0.125 * math.log2(math.e)
ROWS, COLUMNS = 512, 256
F32, BF16 = jnp.float32, jnp.bfloat16
VMEM = pl.BlockSpec(memory_space=pltpu.VMEM)
HBM = pl.BlockSpec(memory_space=pltpu.HBM)
SMEM = pl.BlockSpec(memory_space=pltpu.SMEM)
PARAMS = pltpu.CompilerParams(vmem_limit_bytes=40 * 1024 * 1024)
NN, NT = (((1,), (0,)), ((), ())), (((1,), (1,)), ((), ()))


def lasts(microseconds):
    return pl.CostEstimate(
        flops=int(1e9 * microseconds), bytes_accessed=int(3e6 * microseconds), transcendentals=0
    )


def mxu(x, y, dims=NN):
    return lax.dot_general(x, y, dims, preferred_element_type=F32)


def split2(x):
    high = x.astype(BF16)
    return high, (x - high.astype(F32)).astype(BF16)


def split3(x):
    high = x.astype(BF16).astype(F32)
    rest = x - high
    middle = rest.astype(BF16).astype(F32)
    return high, middle, (rest - middle).astype(BF16).astype(F32)


def product(x, y, dims=NN):
    x1, x2 = split2(x)
    y1, y2 = split2(y)
    return mxu(x1, y1, dims) + (mxu(x2, y1, dims) + mxu(x1, y2, dims))


def source_rows(x):
    a1, a2, a3 = split3(x * (2.0 * RATE))
    return jnp.concatenate([a1, a1, a2, a2, a1, a3], axis=0).T.astype(BF16)


def target_columns(x):
    b1, b2, b3 = split3(x)
    return jnp.concatenate([b1, b2, b1, b2, b3, b1], axis=0).astype(BF16)


def damping(x):
    return jnp.exp2(-RATE * jnp.sum(x * x, axis=0, keepdims=True))


def coef_kernel(leaves, vectors, basis, transfer, skeleton, packed, *refs):
    held, bases, moves, skeletons, sems = refs
    pairs = [(vectors, held), (transfer, moves), (skeleton, skeletons)]
    pairs += [(basis.at[leaf], bases.at[leaf]) for leaf in range(leaves)]
    loads = [pltpu.make_async_copy(src, dst, sems.at[at]) for at, (src, dst) in enumerate(pairs)]
    for load in loads:
        load.start()
    for load in loads[:3]:
        load.wait()
    dim, rank = skeletons.shape[1:]
    width = bases.shape[2]
    vecs = held.shape[0]
    lift = 0.0
    for leaf in range(leaves):
        loads[3 + leaf].wait()
        lanes = slice(leaf * rank, (leaf + 1) * rank)
        coef = product(held[:, leaf * width : (leaf + 1) * width], bases[leaf], NT)
        packed[0:dim, lanes] = skeletons[leaf]
        packed[dim : dim + vecs, lanes] = coef
        lift = lift + product(coef, moves[leaf])
    rows = vecs // leaves
    for piece in range(leaves):
        packed[dim + vecs :, piece * rank : (piece + 1) * rank] = lift[
            piece * rows : (piece + 1) * rows
        ]


def coefficients(vectors, basis, transfer, skeleton):
    leaves, dim, rank = skeleton.shape
    vecs = vectors.shape[0]
    inputs = [
        pltpu.with_memory_space_constraint(x, pltpu.HBM)
        for x in (vectors, basis, transfer, skeleton)
    ]
    return pl.pallas_call(
        functools.partial(coef_kernel, leaves),
        out_shape=jax.ShapeDtypeStruct((dim + vecs + vecs // leaves, leaves * rank), F32),
        in_specs=[HBM] * 4,
        out_specs=VMEM,
        scratch_shapes=[pltpu.VMEM(x.shape, F32) for x in inputs]
        + [pltpu.SemaphoreType.DMA((3 + leaves,))],
        compiler_params=PARAMS,
        cost_estimate=lasts(0.5),
        name="coefficients",
    )(*inputs)


def write_source(points, vectors, left, coefs):
    vecs = vectors.shape[0]
    left[...] = source_rows(points)
    high, low = split2(vectors * damping(points))
    coefs[0:vecs] = high
    coefs[vecs:] = low


def prepare_kernel(width, bases_of, *refs):
    left, coefs, right, scale = refs[-4:]
    for at, base in enumerate(bases_of()):
        points, vectors = refs[2 * at], refs[2 * at + 1]
        for leaf in range(points.shape[1] // width):
            span = slice(leaf * width, (leaf + 1) * width)
            here = points[:, span]
            write_source(here, vectors[:, span], left.at[base + leaf], coefs.at[base + leaf])
            right[base + leaf] = target_columns(here)
            scale[base + leaf] = damping(here) * width**-0.5


def source_shapes(sources, dim, vecs, width):
    return [
        jax.ShapeDtypeStruct((sources, width, 6 * dim), BF16),
        jax.ShapeDtypeStruct((sources, 2 * vecs, width), BF16),
    ]


def prepare(pairs, width, bases_of):
    dim, vecs = pairs[0][0].shape[0], pairs[0][1].shape[0]
    count = sum(points.shape[1] for points, _ in pairs) // width
    inputs = [x for pair in pairs for x in pair]
    return pl.pallas_call(
        functools.partial(prepare_kernel, width, bases_of),
        out_shape=source_shapes(count, dim, vecs, width)
        + [
            jax.ShapeDtypeStruct((count, 6 * dim, width), BF16),
            jax.ShapeDtypeStruct((count, 1, width), F32),
        ],
        in_specs=[VMEM] * len(inputs),
        out_specs=[VMEM] * 4,
        compiler_params=PARAMS,
        cost_estimate=lasts(0.5),
        name="prepare",
    )(*inputs)


def run_tiles(todo, work, sources, left, coefs, right, right_base, totals, totals_base):
    vecs, width = totals.shape[1:]
    chunks = [(y, x) for y in range(0, width, COLUMNS) for x in range(0, width, ROWS)]

    def tile(step, carry):
        slot = work[step] // sources
        source = work[step] % sources

        def exponent(y, x):
            return mxu(left[source, x : x + ROWS], right[right_base + slot, :, y : y + COLUMNS])

        ahead = exponent(*chunks[0])
        for at, (y, x) in enumerate(chunks):
            power = ahead
            if at + 1 < len(chunks):
                ahead = exponent(*chunks[at + 1])
            high, low = split2(jnp.exp2(power))
            both = coefs[source, :, x : x + ROWS]
            top = mxu(both, high)
            found = top[:vecs] + (top[vecs:] + mxu(both[:vecs], low))
            strip = found if x == 0 else strip + found
            if x + ROWS == width:
                totals[totals_base + slot, :, y : y + COLUMNS] += strip
        return carry

    lax.fori_loop(*todo, tile, 0)


def chip_kernel(leaves, near_list, near_count, left, coefs, right, totals, work):
    first = lax.axis_index("leaf") * near_list.shape[0]
    me = lax.axis_index("sub")
    core, chip = me % 2, me // 2
    many = 2 * leaves
    base = chip * many

    inside, across = jnp.int32(0), [jnp.int32(0), jnp.int32(0)]
    for place in range(many):
        limit = near_count[base + place]
        for turn in range(near_list.shape[1]):
            source = near_list[base + place, turn] - first
            used = turn < limit
            here = (source // many) == chip
            work[inside] = place * many + (source - base)
            inside = inside + (used & here).astype(jnp.int32)
            for side in range(2):
                parity = (source // leaves) % 2 == side
                across[side] = across[side] + (used & ~here & parity).astype(jnp.int32)
    share = (inside + across[0] + across[1] + 1) // 2 - across[0]
    share = jnp.clip(share, 0, inside)
    start = jnp.where(core == 0, 0, share)
    stop = jnp.where(core == 0, share, inside)
    totals[...] = jnp.zeros(totals.shape, F32)
    run_tiles((start, stop), work, many, left, coefs, right, 0, totals, 0)


def on_chip(lists, factors, leaves):
    near_list, near_count = lists
    left, coefs, right, _ = factors
    vecs, width = coefs.shape[1] // 2, coefs.shape[2]
    return pl.pallas_call(
        functools.partial(chip_kernel, leaves),
        out_shape=jax.ShapeDtypeStruct((2 * leaves, vecs, width), F32),
        in_specs=[SMEM, SMEM] + [VMEM] * 3,
        out_specs=VMEM,
        scratch_shapes=[pltpu.SMEM((2 * leaves * near_list.shape[1] + 1,), jnp.int32)],
        compiler_params=PARAMS,
        cost_estimate=lasts(0.5),
        name="near_on_chip",
    )(near_list, near_count, left, coefs, right)


def list_tiles(near_list, near_count, leaves, target, source_base, sources, work):
    first = lax.axis_index("leaf") * near_list.shape[0]
    pair_size, pair_at = lax.axis_size("pair"), lax.axis_index("pair")
    todo = jnp.int32(0)
    for leaf in range(leaves):
        place = target * leaves + leaf
        limit = near_count[place]
        for turn in range(near_list.shape[1]):
            source = near_list[place, turn] - first - source_base
            wanted = (turn < limit) & (source >= 0) & (source < sources)
            if pair_size > 1:
                wanted = wanted & (pair_at == turn % pair_size)
            work[todo] = leaf * sources + source
            todo = todo + wanted.astype(jnp.int32)
    return todo


def cross_kernel(leaves, twin, near_list, near_count, *refs):
    given, (right, scale, begun, out, *rest) = refs[:2], refs[2:]
    totals, work = rest[-2:]
    me = lax.axis_index("sub")
    core = me % 2
    vecs, width = totals.shape[1:]
    todo = list_tiles(
        near_list, near_count, leaves, me ^ 1 if twin else me, (me ^ 2) * leaves, leaves, work
    )
    if twin:
        left, coefs = rest[:2]
        for leaf in range(leaves):
            span = slice(leaf * width, (leaf + 1) * width)
            write_source(given[0][:, span], given[1][:, span], left.at[leaf], coefs.at[leaf])
    else:
        left, coefs = given
    base = (1 - core if twin else core) * leaves
    for leaf in range(leaves):
        totals[leaf] = begun[base + leaf]
    run_tiles((0, todo), work, leaves, left, coefs, right, base, totals, 0)
    for leaf in range(leaves):
        out[:, leaf * width : (leaf + 1) * width] = totals[leaf] * scale[base + leaf]


def from_cross(lists, source, factors, begun, leaves, twin):
    near_list, near_count = lists
    _, coefs, right, scale = factors
    vecs, width = coefs.shape[1] // 2, coefs.shape[2]
    shapes = [jax.ShapeDtypeStruct((vecs, leaves * width), F32)]
    if twin:
        shapes += source_shapes(leaves, source[0].shape[0], vecs, width)
    return pl.pallas_call(
        functools.partial(cross_kernel, leaves, twin),
        out_shape=shapes,
        in_specs=[SMEM, SMEM] + [VMEM] * 5,
        out_specs=[VMEM] * len(shapes),
        scratch_shapes=[
            pltpu.VMEM((leaves, vecs, width), F32),
            pltpu.SMEM((leaves * near_list.shape[1] + 1,), jnp.int32),
        ],
        compiler_params=PARAMS,
        cost_estimate=lasts(0.5),
        name="near_cross_twin" if twin else "near_cross_own",
    )(near_list, near_count, *source, right, scale, begun)


def subtree_kernel(leaves, near_list, near_count, left, coefs, right, scale, out, totals, work):
    me = lax.axis_index("sub")
    vecs, width = totals.shape[1:]
    sources = left.shape[0]
    todo = list_tiles(near_list, near_count, leaves, me, 0, sources, work)
    totals[...] = jnp.zeros(totals.shape, F32)
    run_tiles((0, todo), work, sources, left, coefs, right, me * leaves, totals, 0)
    for leaf in range(leaves):
        out[:, leaf * width : (leaf + 1) * width] = totals[leaf] * scale[me * leaves + leaf]


def from_subtree(lists, factors, leaves):
    near_list, near_count = lists
    vecs, width = factors[1].shape[1] // 2, factors[1].shape[2]
    return pl.pallas_call(
        functools.partial(subtree_kernel, leaves),
        out_shape=jax.ShapeDtypeStruct((vecs, leaves * width), F32),
        in_specs=[SMEM, SMEM] + [VMEM] * 4,
        out_specs=VMEM,
        scratch_shapes=[
            pltpu.VMEM((leaves, vecs, width), F32),
            pltpu.SMEM((leaves * near_list.shape[1] + 1,), jnp.int32),
        ],
        compiler_params=PARAMS,
        name="near_subtree",
    )(near_list, near_count, *factors)


def interact(source, coefs, target):
    kernel = jnp.exp2(mxu(source_rows(source), target_columns(target)))
    return product(coefs * damping(source), kernel) * damping(target)


def far_kernel(place_of, leaves, subs, nears, far_list, parent_far, *refs):
    refs, (skeleton, parent_skel, transfer, basis, out) = refs[:-5], refs[-5:]
    near, gathered = refs[:nears], refs[nears:]
    dim, rank = skeleton.shape[1:]
    width = basis.shape[2]
    vecs = out.shape[0]

    def block(device):
        which, *index = place_of(device)
        found = gathered[0][tuple(index)]
        for other in range(1, len(gathered)):
            found = jnp.where(which == other, gathered[other][tuple(index)], found)
        return found

    def lanes(data, at):
        found = data[:, :rank]
        for other in range(1, leaves):
            found = jnp.where(at == other, data[:, other * rank : (other + 1) * rank], found)
        return found

    points, coefs = [], []
    for turn in range(parent_far.shape[1]):
        parent = parent_far[0, turn]
        lift = block(parent * subs)[dim + vecs :]
        for sub in range(1, subs):
            lift = lift + block(parent * subs + sub)[dim + vecs :]
        coefs.append(
            jnp.concatenate([lift[:, at * rank : (at + 1) * rank] for at in range(leaves)], axis=0)
        )
        points.append(parent_skel[parent])
    own = parent_skel[lax.axis_index("leaf")]
    upper = interact(
        jnp.concatenate(points, axis=1), jnp.concatenate(coefs, axis=1), own
    ) * (rank**-0.5)

    for leaf in range(leaves):
        points, coefs = [], []
        for turn in range(far_list.shape[1]):
            partner = far_list[leaf, turn]
            data = lanes(block(partner // leaves), partner % leaves)
            points.append(data[:dim])
            coefs.append(data[dim : dim + vecs])
        far = interact(
            jnp.concatenate(points, axis=1), jnp.concatenate(coefs, axis=1), skeleton[leaf]
        ) * (rank**-0.5)
        field = far + product(upper, transfer[leaf], NT)
        span = slice(leaf * width, (leaf + 1) * width)
        total = product(field, basis[leaf])
        for part in near:
            total = total + part[:, span]
        out[:, span] = total


def far_field(place_of, subs, far_list, parent_far, near, gathered, *held):
    skeleton, _, _, basis = held
    leaves, rank, width = basis.shape
    vecs = near[0].shape[0]
    return pl.pallas_call(
        functools.partial(far_kernel, place_of, leaves, subs, len(near)),
        out_shape=jax.ShapeDtypeStruct((vecs, leaves * width), F32),
        in_specs=[SMEM, SMEM] + [VMEM] * (len(near) + len(gathered) + 4),
        out_specs=VMEM,
        compiler_params=PARAMS,
        cost_estimate=lasts(0.5),
        name="far_field",
    )(far_list, parent_far, *near, *gathered, *held)


def swap(x, bit):
    size = lax.axis_size("sub")
    return lax.ppermute(x, "sub", [(at, at ^ bit) for at in range(size)])


def local(
    points,
    vectors,
    basis,
    transfer,
    skeleton,
    parent_skel,
    near_list,
    near_count,
    far_list,
    parent_far,
):
    leaves, _, width = basis.shape
    subs, groups = lax.axis_size("sub"), lax.axis_size("leaf")
    lists = (near_list, near_count)
    packed = coefficients(vectors, basis, transfer, skeleton)
    if subs == 4 and lax.axis_size("pair") == 1:

        def bases_of():
            core = lax.axis_index("sub") % 2
            return core * leaves, (1 - core) * leaves

        cross = (swap(points, 2), swap(vectors, 2))
        twin = (swap(points, 1), swap(vectors, 1))
        beside = swap(packed, 2)
        factors = prepare(((points, vectors), twin), width, bases_of)
        beside, factors = lax.optimization_barrier((beside, factors))
        column = jnp.stack([packed, beside])
        line = [
            lax.ppermute(column, "leaf", [(at, (at + step) % groups) for at in range(groups)])
            for step in range(1, groups)
        ]
        begun = on_chip(lists, factors, leaves)
        twin_near, *cross = from_cross(lists, cross, factors, begun, leaves, True)
        back = swap(twin_near, 1)
        line, twin_near = lax.optimization_barrier((line, twin_near))
        plane = jnp.stack([column] + line)
        gathered = (plane, swap(plane, 1))
        (own_near,) = from_cross(lists, cross, factors, begun, leaves, False)
        near = (own_near, back)

        def place_of(device):
            away = (device % subs) ^ lax.axis_index("sub")
            step = (lax.axis_index("leaf") - device // subs + groups) % groups
            return away % 2, step, away // 2

    else:

        def bases_of():
            return (0,)

        def place_of(device):
            return 0, device

        gathered = (lax.all_gather(packed, ("leaf", "sub")),)
        everyone = tuple(
            lax.all_gather(x, "sub", axis=1, tiled=True) for x in (points, vectors)
        )
        factors = prepare((everyone,), width, bases_of)
        near = (lax.psum(from_subtree(lists, factors, leaves), "pair"),)

    return far_field(
        place_of, subs, far_list, parent_far, near, gathered, skeleton, parent_skel, transfer, basis
    )


def solution(mesh):
    placed = (
        P(None, ("groups", "leaf", "sub")),
        P(None, ("groups", "leaf", "sub")),
        P(("groups", "leaf", "sub"), None, None),
        P(("groups", "leaf", "sub"), None, None),
        P(("groups", "leaf", "sub"), None, None),
        P("groups", None, None),
        P(("groups", "leaf"), None),
        P(("groups", "leaf")),
        P(("groups", "leaf", "sub"), None),
        P(("groups", "leaf"), None),
    )
    return jax.shard_map(
        local,
        mesh=mesh,
        in_specs=placed,
        out_specs=P(None, ("groups", "leaf", "sub")),
        check_vma=False,
    )
```

```python
import functools

import jax
import jax.numpy as jnp
from jax import lax
from jax.experimental import pallas as pl
from jax.experimental.pallas import tpu as pltpu
from jax.sharding import PartitionSpec as P

WIDTH = 0.125
ROWS, COLUMNS = 512, 256
F32, BF16 = jnp.float32, jnp.bfloat16
VMEM = pl.BlockSpec(memory_space=pltpu.VMEM)
HBM = pl.BlockSpec(memory_space=pltpu.HBM)
SMEM = pl.BlockSpec(memory_space=pltpu.SMEM)
PARAMS = pltpu.CompilerParams(vmem_limit_bytes=40 * 1024 * 1024)
NN, NT = (((1,), (0,)), ((), ())), (((1,), (1,)), ((), ()))


def lasts(microseconds):
    return pl.CostEstimate(
        flops=int(1e9 * microseconds), bytes_accessed=int(3e6 * microseconds), transcendentals=0
    )


def mxu(x, y, dims=NN):
    return lax.dot_general(x, y, dims, preferred_element_type=F32)


def split2(x):
    high = x.astype(BF16)
    return high, (x - high.astype(F32)).astype(BF16)


def split3(x):
    high = x.astype(BF16).astype(F32)
    rest = x - high
    middle = rest.astype(BF16).astype(F32)
    return high, middle, (rest - middle).astype(BF16).astype(F32)


def product(x, y, dims=NN):
    x1, x2 = split2(x)
    y1, y2 = split2(y)
    return mxu(x1, y1, dims) + (mxu(x2, y1, dims) + mxu(x1, y2, dims))


def source_rows(x):
    a1, a2, a3 = split3(x * (2.0 * WIDTH))
    return jnp.concatenate([a1, a1, a2, a2, a1, a3], axis=0).T.astype(BF16)


def target_columns(x):
    b1, b2, b3 = split3(x)
    return jnp.concatenate([b1, b2, b1, b2, b3, b1], axis=0).astype(BF16)


def damping(x):
    return jnp.exp(-WIDTH * jnp.sum(x * x, axis=0, keepdims=True))


def coef_kernel(leaves, vectors, basis, transfer, skeleton, packed, *refs):
    held, bases, moves, skeletons, sems = refs
    pairs = [(vectors, held), (transfer, moves), (skeleton, skeletons)]
    pairs += [(basis.at[leaf], bases.at[leaf]) for leaf in range(leaves)]
    loads = [pltpu.make_async_copy(src, dst, sems.at[at]) for at, (src, dst) in enumerate(pairs)]
    for load in loads:
        load.start()
    for load in loads[:3]:
        load.wait()
    dim, rank = skeletons.shape[1:]
    width = bases.shape[2]
    vecs = held.shape[0]
    lift = 0.0
    for leaf in range(leaves):
        loads[3 + leaf].wait()
        lanes = slice(leaf * rank, (leaf + 1) * rank)
        coef = product(held[:, leaf * width : (leaf + 1) * width], bases[leaf], NT)
        packed[0:dim, lanes] = skeletons[leaf]
        packed[dim : dim + vecs, lanes] = coef
        lift = lift + product(coef, moves[leaf])
    rows = vecs // leaves
    for piece in range(leaves):
        packed[dim + vecs : dim + vecs + rows, piece * rank : (piece + 1) * rank] = lift[
            piece * rows : (piece + 1) * rows
        ]
    used = dim + vecs + rows
    packed[used:] = jnp.zeros((packed.shape[0] - used, packed.shape[1]), F32)


def coefficients(vectors, basis, transfer, skeleton):
    leaves, dim, rank = skeleton.shape
    vecs = vectors.shape[0]
    inputs = [
        pltpu.with_memory_space_constraint(x, pltpu.HBM)
        for x in (vectors, basis, transfer, skeleton)
    ]
    return pl.pallas_call(
        functools.partial(coef_kernel, leaves),
        out_shape=jax.ShapeDtypeStruct((2 * (dim + vecs + vecs // leaves), leaves * rank), F32),
        in_specs=[HBM] * 4,
        out_specs=VMEM,
        scratch_shapes=[pltpu.VMEM(x.shape, F32) for x in inputs]
        + [pltpu.SemaphoreType.DMA((3 + leaves,))],
        compiler_params=PARAMS,
        cost_estimate=lasts(0.5),
        name="coefficients",
    )(*inputs)


def write_source(points, vectors, left, coefs):
    vecs = vectors.shape[0]
    left[...] = source_rows(points)
    high, low = split2(vectors * damping(points))
    coefs[0:vecs] = high
    coefs[vecs:] = low


def prepare_kernel(width, bases_of, *refs):
    left, coefs, right, scale = refs[-4:]
    for at, base in enumerate(bases_of()):
        points, vectors = refs[2 * at], refs[2 * at + 1]
        for leaf in range(points.shape[1] // width):
            span = slice(leaf * width, (leaf + 1) * width)
            here = points[:, span]
            write_source(here, vectors[:, span], left.at[base + leaf], coefs.at[base + leaf])
            right[base + leaf] = target_columns(here)
            scale[base + leaf] = damping(here) * width**-0.5


def source_shapes(sources, dim, vecs, width):
    return [
        jax.ShapeDtypeStruct((sources, width, 6 * dim), BF16),
        jax.ShapeDtypeStruct((sources, 2 * vecs, width), BF16),
    ]


def prepare(pairs, width, bases_of):
    dim, vecs = pairs[0][0].shape[0], pairs[0][1].shape[0]
    count = sum(points.shape[1] for points, _ in pairs) // width
    inputs = [x for pair in pairs for x in pair]
    return pl.pallas_call(
        functools.partial(prepare_kernel, width, bases_of),
        out_shape=source_shapes(count, dim, vecs, width)
        + [
            jax.ShapeDtypeStruct((count, 6 * dim, width), BF16),
            jax.ShapeDtypeStruct((count, 1, width), F32),
        ],
        in_specs=[VMEM] * len(inputs),
        out_specs=[VMEM] * 4,
        compiler_params=PARAMS,
        cost_estimate=lasts(0.5),
        name="prepare",
    )(*inputs)


def run_tiles(todo, work, sources, left, coefs, right, right_base, totals, totals_base):
    vecs, width = totals.shape[1:]
    chunks = [(y, x) for y in range(0, width, COLUMNS) for x in range(0, width, ROWS)]

    def tile(step, carry):
        slot = work[step] // sources
        source = work[step] % sources

        def exponent(y, x):
            return mxu(left[source, x : x + ROWS], right[right_base + slot, :, y : y + COLUMNS])

        ahead = exponent(*chunks[0])
        for at, (y, x) in enumerate(chunks):
            power = ahead
            if at + 1 < len(chunks):
                ahead = exponent(*chunks[at + 1])
            high, low = split2(jnp.exp(power))
            both = coefs[source, :, x : x + ROWS]
            top = mxu(both, high)
            found = top[:vecs] + (top[vecs:] + mxu(both[:vecs], low))
            strip = found if x == 0 else strip + found
            if x + ROWS == width:
                totals[totals_base + slot, :, y : y + COLUMNS] += strip
        return carry

    lax.fori_loop(*todo, tile, 0)


def chip_kernel(leaves, near_list, near_count, left, coefs, right, totals, work):
    first = lax.axis_index("leaf") * near_list.shape[0]
    me = lax.axis_index("sub")
    core, chip = me % 2, me // 2
    many = 2 * leaves
    base = chip * many

    inside, across = jnp.int32(0), [jnp.int32(0), jnp.int32(0)]
    for place in range(many):
        limit = near_count[base + place]
        for turn in range(near_list.shape[1]):
            source = near_list[base + place, turn] - first
            used = turn < limit
            here = (source // many) == chip
            work[inside] = place * many + (source - base)
            inside = inside + (used & here).astype(jnp.int32)
            for side in range(2):
                parity = (source // leaves) % 2 == side
                across[side] = across[side] + (used & ~here & parity).astype(jnp.int32)
    share = (inside + across[0] + across[1] + 1) // 2 - across[0]
    share = jnp.clip(share, 0, inside)
    start = jnp.where(core == 0, 0, share)
    stop = jnp.where(core == 0, share, inside)
    totals[...] = jnp.zeros(totals.shape, F32)
    run_tiles((start, stop), work, many, left, coefs, right, 0, totals, 0)


def on_chip(lists, factors, leaves):
    near_list, near_count = lists
    left, coefs, right, _ = factors
    vecs, width = coefs.shape[1] // 2, coefs.shape[2]
    return pl.pallas_call(
        functools.partial(chip_kernel, leaves),
        out_shape=jax.ShapeDtypeStruct((2 * leaves, vecs, width), F32),
        in_specs=[SMEM, SMEM] + [VMEM] * 3,
        out_specs=VMEM,
        scratch_shapes=[pltpu.SMEM((2 * leaves * near_list.shape[1] + 1,), jnp.int32)],
        compiler_params=PARAMS,
        cost_estimate=lasts(0.5),
        name="near_on_chip",
    )(near_list, near_count, left, coefs, right)


def list_tiles(near_list, near_count, leaves, target, source_base, sources, work):
    first = lax.axis_index("leaf") * near_list.shape[0]
    pair_size, pair_at = lax.axis_size("pair"), lax.axis_index("pair")
    todo = jnp.int32(0)
    for leaf in range(leaves):
        place = target * leaves + leaf
        limit = near_count[place]
        for turn in range(near_list.shape[1]):
            source = near_list[place, turn] - first - source_base
            wanted = (turn < limit) & (source >= 0) & (source < sources)
            if pair_size > 1:
                wanted = wanted & (pair_at == turn % pair_size)
            work[todo] = leaf * sources + source
            todo = todo + wanted.astype(jnp.int32)
    return todo


def cross_kernel(leaves, twin, near_list, near_count, *refs):
    given, (right, scale, begun, out, *rest) = refs[:2], refs[2:]
    totals, work = rest[-2:]
    me = lax.axis_index("sub")
    core = me % 2
    vecs, width = totals.shape[1:]
    todo = list_tiles(
        near_list, near_count, leaves, me ^ 1 if twin else me, (me ^ 2) * leaves, leaves, work
    )
    if twin:
        left, coefs = rest[:2]
        for leaf in range(leaves):
            span = slice(leaf * width, (leaf + 1) * width)
            write_source(given[0][:, span], given[1][:, span], left.at[leaf], coefs.at[leaf])
    else:
        left, coefs = given
    base = (1 - core if twin else core) * leaves
    for leaf in range(leaves):
        totals[leaf] = begun[base + leaf]
    run_tiles((0, todo), work, leaves, left, coefs, right, base, totals, 0)
    for leaf in range(leaves):
        out[:, leaf * width : (leaf + 1) * width] = totals[leaf] * scale[base + leaf]


def from_cross(lists, source, factors, begun, leaves, twin):
    near_list, near_count = lists
    _, coefs, right, scale = factors
    vecs, width = coefs.shape[1] // 2, coefs.shape[2]
    shapes = [jax.ShapeDtypeStruct((vecs, leaves * width), F32)]
    if twin:
        shapes += source_shapes(leaves, source[0].shape[0], vecs, width)
    return pl.pallas_call(
        functools.partial(cross_kernel, leaves, twin),
        out_shape=shapes,
        in_specs=[SMEM, SMEM] + [VMEM] * 5,
        out_specs=[VMEM] * len(shapes),
        scratch_shapes=[
            pltpu.VMEM((leaves, vecs, width), F32),
            pltpu.SMEM((leaves * near_list.shape[1] + 1,), jnp.int32),
        ],
        compiler_params=PARAMS,
        cost_estimate=lasts(0.5),
        name="near_cross_twin" if twin else "near_cross_own",
    )(near_list, near_count, *source, right, scale, begun)


def subtree_kernel(leaves, near_list, near_count, left, coefs, right, scale, out, totals, work):
    me = lax.axis_index("sub")
    vecs, width = totals.shape[1:]
    sources = left.shape[0]
    todo = list_tiles(near_list, near_count, leaves, me, 0, sources, work)
    totals[...] = jnp.zeros(totals.shape, F32)
    run_tiles((0, todo), work, sources, left, coefs, right, me * leaves, totals, 0)
    for leaf in range(leaves):
        out[:, leaf * width : (leaf + 1) * width] = totals[leaf] * scale[me * leaves + leaf]


def from_subtree(lists, factors, leaves):
    near_list, near_count = lists
    vecs, width = factors[1].shape[1] // 2, factors[1].shape[2]
    return pl.pallas_call(
        functools.partial(subtree_kernel, leaves),
        out_shape=jax.ShapeDtypeStruct((vecs, leaves * width), F32),
        in_specs=[SMEM, SMEM] + [VMEM] * 4,
        out_specs=VMEM,
        scratch_shapes=[
            pltpu.VMEM((leaves, vecs, width), F32),
            pltpu.SMEM((leaves * near_list.shape[1] + 1,), jnp.int32),
        ],
        compiler_params=PARAMS,
        name="near_subtree",
    )(near_list, near_count, *factors)


def interact(source, coefs, target):
    kernel = jnp.exp(mxu(source_rows(source), target_columns(target)))
    return product(coefs * damping(source), kernel) * damping(target)


def far_kernel(leaves, subs, nears, far_list, parent_far, *refs):
    near, (gathered, skeleton, parent_skel, transfer, basis, out) = refs[:nears], refs[nears:]
    dim, rank = skeleton.shape[1:]
    width = basis.shape[2]
    vecs = out.shape[0]
    lift_rows = slice(dim + vecs, dim + vecs + vecs // leaves)

    def lanes(data, at):
        found = data[:, :rank]
        for other in range(1, leaves):
            found = jnp.where(at == other, data[:, other * rank : (other + 1) * rank], found)
        return found

    points, coefs = [], []
    for turn in range(parent_far.shape[1]):
        parent = parent_far[0, turn]
        lift = gathered[parent * subs, lift_rows]
        for sub in range(1, subs):
            lift = lift + gathered[parent * subs + sub, lift_rows]
        coefs.append(
            jnp.concatenate([lift[:, at * rank : (at + 1) * rank] for at in range(leaves)], axis=0)
        )
        points.append(parent_skel[parent])
    own = parent_skel[lax.axis_index("leaf")]
    upper = interact(
        jnp.concatenate(points, axis=1), jnp.concatenate(coefs, axis=1), own
    ) * (rank**-0.5)

    for leaf in range(leaves):
        points, coefs = [], []
        for turn in range(far_list.shape[1]):
            partner = far_list[leaf, turn]
            data = lanes(gathered[partner // leaves, 0 : dim + vecs], partner % leaves)
            points.append(data[:dim])
            coefs.append(data[dim:])
        far = interact(
            jnp.concatenate(points, axis=1), jnp.concatenate(coefs, axis=1), skeleton[leaf]
        ) * (rank**-0.5)
        field = far + product(upper, transfer[leaf], NT)
        span = slice(leaf * width, (leaf + 1) * width)
        total = product(field, basis[leaf])
        for part in near:
            total = total + part[:, span]
        out[:, span] = total


def far_field(subs, far_list, parent_far, near, *held):
    basis = held[-1]
    leaves, rank, width = basis.shape
    vecs = near[0].shape[0]
    return pl.pallas_call(
        functools.partial(far_kernel, leaves, subs, len(near)),
        out_shape=jax.ShapeDtypeStruct((vecs, leaves * width), F32),
        in_specs=[SMEM, SMEM] + [VMEM] * (len(near) + 5),
        out_specs=VMEM,
        compiler_params=PARAMS,
        cost_estimate=lasts(0.5),
        name="far_field",
    )(far_list, parent_far, *near, *held)


def swap(x, bit):
    size = lax.axis_size("sub")
    return lax.ppermute(x, "sub", [(at, at ^ bit) for at in range(size)])


def local(
    points,
    vectors,
    basis,
    transfer,
    skeleton,
    parent_skel,
    near_list,
    near_count,
    far_list,
    parent_far,
):
    leaves, _, width = basis.shape
    subs = lax.axis_size("sub")
    lists = (near_list, near_count)
    packed = coefficients(vectors, basis, transfer, skeleton)
    gathered = lax.all_gather(packed, ("leaf", "sub"))
    if subs == 4 and lax.axis_size("pair") == 1:

        def bases_of():
            core = lax.axis_index("sub") % 2
            return core * leaves, (1 - core) * leaves

        cross = (swap(points, 2), swap(vectors, 2))
        twin = (swap(points, 1), swap(vectors, 1))
        factors = prepare(((points, vectors), twin), width, bases_of)
        begun = on_chip(lists, factors, leaves)
        twin_near, *cross = from_cross(lists, cross, factors, begun, leaves, True)
        back = swap(twin_near, 1)
        (own_near,) = from_cross(lists, cross, factors, begun, leaves, False)
        near = (own_near, back)
    else:
        everyone = tuple(
            lax.all_gather(x, "sub", axis=1, tiled=True) for x in (points, vectors)
        )
        factors = prepare((everyone,), width, lambda: (0,))
        near = (lax.psum(from_subtree(lists, factors, leaves), "pair"),)

    return far_field(
        subs, far_list, parent_far, near, gathered, skeleton, parent_skel, transfer, basis
    )


def solution(mesh):
    placed = (
        P(None, ("groups", "leaf", "sub")),
        P(None, ("groups", "leaf", "sub")),
        P(("groups", "leaf", "sub"), None, None),
        P(("groups", "leaf", "sub"), None, None),
        P(("groups", "leaf", "sub"), None, None),
        P("groups", None, None),
        P(("groups", "leaf"), None),
        P(("groups", "leaf")),
        P(("groups", "leaf", "sub"), None),
        P(("groups", "leaf"), None),
    )
    return jax.shard_map(
        local,
        mesh=mesh,
        in_specs=placed,
        out_specs=P(None, ("groups", "leaf", "sub")),
        check_vma=False,
    )
```

```python
import functools
import math

import jax
import jax.numpy as jnp
from jax import lax
from jax.experimental import pallas as pl
from jax.experimental.pallas import tpu as pltpu
from jax.sharding import PartitionSpec as P

RATE = 0.125 * math.log2(math.e)
ROWS, COLUMNS = 512, 256
F32, BF16 = jnp.float32, jnp.bfloat16
VMEM = pl.BlockSpec(memory_space=pltpu.VMEM)
HBM = pl.BlockSpec(memory_space=pltpu.HBM)
SMEM = pl.BlockSpec(memory_space=pltpu.SMEM)
PARAMS = pltpu.CompilerParams(vmem_limit_bytes=40 * 1024 * 1024)
NN, NT = (((1,), (0,)), ((), ())), (((1,), (1,)), ((), ()))


def lasts(microseconds):
    return pl.CostEstimate(
        flops=int(1e9 * microseconds), bytes_accessed=int(3e6 * microseconds), transcendentals=0
    )


def mxu(x, y, dims=NN):
    return lax.dot_general(x, y, dims, preferred_element_type=F32)


def split2(x):
    high = x.astype(BF16)
    return high, (x - high.astype(F32)).astype(BF16)


def split3(x):
    high = x.astype(BF16).astype(F32)
    rest = x - high
    middle = rest.astype(BF16).astype(F32)
    return high, middle, (rest - middle).astype(BF16).astype(F32)


def product(x, y, dims=NN):
    x1, x2 = split2(x)
    y1, y2 = split2(y)
    return mxu(x1, y1, dims) + (mxu(x2, y1, dims) + mxu(x1, y2, dims))


def source_rows(x):
    a1, a2, a3 = split3(x * (2.0 * RATE))
    return jnp.concatenate([a1, a1, a2, a2, a1, a3], axis=0).T.astype(BF16)


def target_columns(x):
    b1, b2, b3 = split3(x)
    return jnp.concatenate([b1, b2, b1, b2, b3, b1], axis=0).astype(BF16)


def damping(x):
    return jnp.exp2(-RATE * jnp.sum(x * x, axis=0, keepdims=True))


def coef_kernel(leaves, vectors, basis, transfer, skeleton, packed, *refs):
    held, bases, moves, skeletons, sems = refs
    pairs = [(vectors, held), (transfer, moves), (skeleton, skeletons)]
    pairs += [(basis.at[leaf], bases.at[leaf]) for leaf in range(leaves)]
    loads = [pltpu.make_async_copy(src, dst, sems.at[at]) for at, (src, dst) in enumerate(pairs)]
    for load in loads:
        load.start()
    for load in loads:
        load.wait()
    dim, rank = skeletons.shape[1:]
    width = bases.shape[2]
    vecs = held.shape[0]
    lift = 0.0
    for leaf in range(leaves):
        lanes = slice(leaf * rank, (leaf + 1) * rank)
        coef = product(held[:, leaf * width : (leaf + 1) * width], bases[leaf], NT)
        packed[0:dim, lanes] = skeletons[leaf]
        packed[dim : dim + vecs, lanes] = coef
        lift = lift + product(coef, moves[leaf])
    rows = vecs // leaves
    for piece in range(leaves):
        packed[dim + vecs :, piece * rank : (piece + 1) * rank] = lift[
            piece * rows : (piece + 1) * rows
        ]


def coefficients(vectors, basis, transfer, skeleton):
    leaves, dim, rank = skeleton.shape
    vecs = vectors.shape[0]
    inputs = [
        pltpu.with_memory_space_constraint(x, pltpu.HBM)
        for x in (vectors, basis, transfer, skeleton)
    ]
    return pl.pallas_call(
        functools.partial(coef_kernel, leaves),
        out_shape=jax.ShapeDtypeStruct((dim + vecs + vecs // leaves, leaves * rank), F32),
        in_specs=[HBM] * 4,
        out_specs=VMEM,
        scratch_shapes=[pltpu.VMEM(x.shape, F32) for x in inputs]
        + [pltpu.SemaphoreType.DMA((3 + leaves,))],
        compiler_params=PARAMS,
        cost_estimate=lasts(0.5),
        name="coefficients",
    )(*inputs)


def write_source(points, vectors, left, coefs):
    vecs = vectors.shape[0]
    left[...] = source_rows(points)
    high, low = split2(vectors * damping(points))
    coefs[0:vecs] = high
    coefs[vecs:] = low


def prepare_kernel(width, points, vectors, left, coefs, right, scale):
    for leaf in range(points.shape[1] // width):
        span = slice(leaf * width, (leaf + 1) * width)
        here = points[:, span]
        write_source(here, vectors[:, span], left.at[leaf], coefs.at[leaf])
        right[leaf] = target_columns(here)
        scale[leaf] = damping(here) * width**-0.5


def source_shapes(sources, dim, vecs, width):
    return [
        jax.ShapeDtypeStruct((sources, width, 6 * dim), BF16),
        jax.ShapeDtypeStruct((sources, 2 * vecs, width), BF16),
    ]


def target_shapes(targets, dim, width):
    return [
        jax.ShapeDtypeStruct((targets, 6 * dim, width), BF16),
        jax.ShapeDtypeStruct((targets, 1, width), F32),
    ]


def prepare(points, vectors, width):
    dim, vecs = points.shape[0], vectors.shape[0]
    count = points.shape[1] // width
    return pl.pallas_call(
        functools.partial(prepare_kernel, width),
        out_shape=source_shapes(count, dim, vecs, width) + target_shapes(count, dim, width),
        in_specs=[VMEM] * 2,
        out_specs=[VMEM] * 4,
        compiler_params=PARAMS,
        cost_estimate=lasts(0.5),
        name="prepare",
    )(points, vectors)


def run_tiles(todo, pick, left, coefs, right, right_base, totals, totals_base):
    vecs, width = totals.shape[1:]
    chunks = [(y, x) for y in range(0, width, COLUMNS) for x in range(0, width, ROWS)]

    def tile(step, carry):
        slot, source = pick(step)

        def exponent(y, x):
            return mxu(left[source, x : x + ROWS], right[right_base + slot, :, y : y + COLUMNS])

        ahead = exponent(*chunks[0])
        for at, (y, x) in enumerate(chunks):
            power = ahead
            if at + 1 < len(chunks):
                ahead = exponent(*chunks[at + 1])
            high, low = split2(jnp.exp2(power))
            both = coefs[source, :, x : x + ROWS]
            top = mxu(both, high)
            found = top[:vecs] + (top[vecs:] + mxu(both[:vecs], low))
            strip = found if x == 0 else strip + found
            if x + ROWS == width:
                totals[totals_base + slot, :, y : y + COLUMNS] += strip
        return carry

    lax.fori_loop(*todo, tile, 0)


def listed(work, sources):
    return lambda step: (work[step] // sources, work[step] % sources)


def self_kernel(points, vectors, left, coefs, right, scale, totals):
    leaves, _, width = totals.shape
    prepare_kernel(width, points, vectors, left, coefs, right, scale)
    totals[...] = jnp.zeros(totals.shape, F32)
    run_tiles((0, leaves), lambda step: (step, step), left, coefs, right, 0, totals, 0)


def with_self(points, vectors, leaves):
    dim, vecs = points.shape[0], vectors.shape[0]
    width = points.shape[1] // leaves
    return pl.pallas_call(
        self_kernel,
        out_shape=source_shapes(leaves, dim, vecs, width)
        + target_shapes(leaves, dim, width)
        + [jax.ShapeDtypeStruct((leaves, vecs, width), F32)],
        in_specs=[VMEM] * 2,
        out_specs=[VMEM] * 5,
        compiler_params=PARAMS,
        cost_estimate=lasts(0.5),
        name="near_self",
    )(points, vectors)


def chip_kernel(leaves, near_list, near_count, points, vectors, *refs):
    own, (right, scale, totals, left, coefs, work) = refs[:5], refs[5:]
    first = lax.axis_index("leaf") * near_list.shape[0]
    me = lax.axis_index("sub")
    core, chip = me % 2, me // 2
    many = 2 * leaves
    base = chip * many
    width = totals.shape[2]

    inside, across = jnp.int32(0), [jnp.int32(0), jnp.int32(0)]
    for place in range(many):
        limit = near_count[base + place]
        for turn in range(1, near_list.shape[1]):
            source = near_list[base + place, turn] - first
            used = turn < limit
            here = (source // many) == chip
            work[inside] = place * many + (source - base)
            inside = inside + (used & here).astype(jnp.int32)
            for side in range(2):
                parity = (source // leaves) % 2 == side
                across[side] = across[side] + (used & ~here & parity).astype(jnp.int32)
    share = (inside + across[0] + across[1] + 1) // 2 - across[0]
    share = jnp.clip(share, 0, inside)
    start = jnp.where(core == 0, 0, share)
    stop = jnp.where(core == 0, share, inside)

    twin = (1 - core) * leaves
    for leaf in range(leaves):
        for held, given in zip((left, coefs, right, scale, totals), own):
            held[core * leaves + leaf] = given[leaf]
        totals[twin + leaf] = jnp.zeros(totals.shape[1:], F32)
    prepare_kernel(
        width,
        points,
        vectors,
        *(held.at[pl.ds(twin, leaves)] for held in (left, coefs, right, scale)),
    )
    run_tiles((start, stop), listed(work, many), left, coefs, right, 0, totals, 0)


def on_chip(lists, twin, own, leaves):
    near_list, near_count = lists
    dim, vecs = twin[0].shape[0], twin[1].shape[0]
    width = twin[0].shape[1] // leaves
    return pl.pallas_call(
        functools.partial(chip_kernel, leaves),
        out_shape=target_shapes(2 * leaves, dim, width)
        + [jax.ShapeDtypeStruct((2 * leaves, vecs, width), F32)],
        in_specs=[SMEM, SMEM] + [VMEM] * 7,
        out_specs=[VMEM] * 3,
        scratch_shapes=[
            pltpu.VMEM((2 * leaves, width, 6 * dim), BF16),
            pltpu.VMEM((2 * leaves, 2 * vecs, width), BF16),
            pltpu.SMEM((2 * leaves * near_list.shape[1] + 1,), jnp.int32),
        ],
        compiler_params=PARAMS,
        cost_estimate=lasts(0.5),
        name="near_on_chip",
    )(near_list, near_count, *twin, *own)


def list_tiles(near_list, near_count, leaves, target, source_base, sources, work):
    first = lax.axis_index("leaf") * near_list.shape[0]
    pair_size, pair_at = lax.axis_size("pair"), lax.axis_index("pair")
    todo = jnp.int32(0)
    for leaf in range(leaves):
        place = target * leaves + leaf
        limit = near_count[place]
        for turn in range(near_list.shape[1]):
            source = near_list[place, turn] - first - source_base
            wanted = (turn < limit) & (source >= 0) & (source < sources)
            if pair_size > 1:
                wanted = wanted & (pair_at == turn % pair_size)
            work[todo] = leaf * sources + source
            todo = todo + wanted.astype(jnp.int32)
    return todo


def cross_kernel(leaves, twin, near_list, near_count, *refs):
    given, (right, scale, begun, out, *rest) = refs[:2], refs[2:]
    totals, work = rest[-2:]
    me = lax.axis_index("sub")
    core = me % 2
    vecs, width = totals.shape[1:]
    todo = list_tiles(
        near_list, near_count, leaves, me ^ 1 if twin else me, (me ^ 2) * leaves, leaves, work
    )
    if twin:
        left, coefs = rest[:2]
        for leaf in range(leaves):
            span = slice(leaf * width, (leaf + 1) * width)
            write_source(given[0][:, span], given[1][:, span], left.at[leaf], coefs.at[leaf])
    else:
        left, coefs = given
    base = (1 - core if twin else core) * leaves
    for leaf in range(leaves):
        totals[leaf] = begun[base + leaf]
    run_tiles((0, todo), listed(work, leaves), left, coefs, right, base, totals, 0)
    for leaf in range(leaves):
        out[:, leaf * width : (leaf + 1) * width] = totals[leaf] * scale[base + leaf]


def from_cross(lists, source, begun, leaves, twin):
    near_list, near_count = lists
    vecs, width = begun[-1].shape[1:]
    shapes = [jax.ShapeDtypeStruct((vecs, leaves * width), F32)]
    if twin:
        shapes += source_shapes(leaves, source[0].shape[0], vecs, width)
    return pl.pallas_call(
        functools.partial(cross_kernel, leaves, twin),
        out_shape=shapes,
        in_specs=[SMEM, SMEM] + [VMEM] * 5,
        out_specs=[VMEM] * len(shapes),
        scratch_shapes=[
            pltpu.VMEM((leaves, vecs, width), F32),
            pltpu.SMEM((leaves * near_list.shape[1] + 1,), jnp.int32),
        ],
        compiler_params=PARAMS,
        cost_estimate=lasts(0.5),
        name="near_cross_twin" if twin else "near_cross_own",
    )(near_list, near_count, *source, *begun)


def subtree_kernel(leaves, near_list, near_count, left, coefs, right, scale, out, totals, work):
    me = lax.axis_index("sub")
    vecs, width = totals.shape[1:]
    sources = left.shape[0]
    todo = list_tiles(near_list, near_count, leaves, me, 0, sources, work)
    totals[...] = jnp.zeros(totals.shape, F32)
    run_tiles((0, todo), listed(work, sources), left, coefs, right, me * leaves, totals, 0)
    for leaf in range(leaves):
        out[:, leaf * width : (leaf + 1) * width] = totals[leaf] * scale[me * leaves + leaf]


def from_subtree(lists, factors, leaves):
    near_list, near_count = lists
    vecs, width = factors[1].shape[1] // 2, factors[1].shape[2]
    return pl.pallas_call(
        functools.partial(subtree_kernel, leaves),
        out_shape=jax.ShapeDtypeStruct((vecs, leaves * width), F32),
        in_specs=[SMEM, SMEM] + [VMEM] * 4,
        out_specs=VMEM,
        scratch_shapes=[
            pltpu.VMEM((leaves, vecs, width), F32),
            pltpu.SMEM((leaves * near_list.shape[1] + 1,), jnp.int32),
        ],
        compiler_params=PARAMS,
        name="near_subtree",
    )(near_list, near_count, *factors)


def interact(source, coefs, target):
    kernel = jnp.exp2(mxu(source_rows(source), target_columns(target)))
    return product(coefs * damping(source), kernel) * damping(target)


def far_kernel(place_of, leaves, subs, nears, far_list, parent_far, *refs):
    refs, (skeleton, parent_skel, transfer, basis, out) = refs[:-5], refs[-5:]
    near, gathered = refs[:nears], refs[nears:]
    dim, rank = skeleton.shape[1:]
    width = basis.shape[2]
    vecs = out.shape[0]

    def block(device):
        which, *index = place_of(device)
        found = gathered[0][tuple(index)]
        for other in range(1, len(gathered)):
            found = jnp.where(which == other, gathered[other][tuple(index)], found)
        return found

    def lanes(data, at):
        found = data[:, :rank]
        for other in range(1, leaves):
            found = jnp.where(at == other, data[:, other * rank : (other + 1) * rank], found)
        return found

    points, coefs = [], []
    for turn in range(parent_far.shape[1]):
        parent = parent_far[0, turn]
        lift = block(parent * subs)[dim + vecs :]
        for sub in range(1, subs):
            lift = lift + block(parent * subs + sub)[dim + vecs :]
        coefs.append(
            jnp.concatenate([lift[:, at * rank : (at + 1) * rank] for at in range(leaves)], axis=0)
        )
        points.append(parent_skel[parent])
    own = parent_skel[lax.axis_index("leaf")]
    upper = interact(
        jnp.concatenate(points, axis=1), jnp.concatenate(coefs, axis=1), own
    ) * (rank**-0.5)

    for leaf in range(leaves):
        points, coefs = [], []
        for turn in range(far_list.shape[1]):
            partner = far_list[leaf, turn]
            data = lanes(block(partner // leaves), partner % leaves)
            points.append(data[:dim])
            coefs.append(data[dim : dim + vecs])
        far = interact(
            jnp.concatenate(points, axis=1), jnp.concatenate(coefs, axis=1), skeleton[leaf]
        ) * (rank**-0.5)
        field = far + product(upper, transfer[leaf], NT)
        span = slice(leaf * width, (leaf + 1) * width)
        total = product(field, basis[leaf])
        for part in near:
            total = total + part[:, span]
        out[:, span] = total


def far_field(place_of, subs, far_list, parent_far, near, gathered, *held):
    skeleton, _, _, basis = held
    leaves, rank, width = basis.shape
    vecs = near[0].shape[0]
    return pl.pallas_call(
        functools.partial(far_kernel, place_of, leaves, subs, len(near)),
        out_shape=jax.ShapeDtypeStruct((vecs, leaves * width), F32),
        in_specs=[SMEM, SMEM] + [VMEM] * (len(near) + len(gathered) + 4),
        out_specs=VMEM,
        compiler_params=PARAMS,
        cost_estimate=lasts(0.5),
        name="far_field",
    )(far_list, parent_far, *near, *gathered, *held)


def swap(x, bit):
    size = lax.axis_size("sub")
    return lax.ppermute(x, "sub", [(at, at ^ bit) for at in range(size)])


def local(
    points,
    vectors,
    basis,
    transfer,
    skeleton,
    parent_skel,
    near_list,
    near_count,
    far_list,
    parent_far,
):
    leaves, _, width = basis.shape
    subs, groups = lax.axis_size("sub"), lax.axis_size("leaf")
    lists = (near_list, near_count)
    packed = coefficients(vectors, basis, transfer, skeleton)
    if subs == 4 and lax.axis_size("pair") == 1:
        twin = (swap(points, 1), swap(vectors, 1))
        cross_vectors = swap(vectors, 2)
        beside = swap(packed, 2)
        late_points, packed = lax.optimization_barrier((points, packed))
        cross = (swap(late_points, 2), cross_vectors)
        own = with_self(points, vectors, leaves)
        beside, twin, own = lax.optimization_barrier((beside, twin, own))
        column = jnp.stack([packed, beside])
        line = [
            lax.ppermute(column, "leaf", [(at, (at + step) % groups) for at in range(groups)])
            for step in range(1, groups)
        ]
        begun = on_chip(lists, twin, own, leaves)
        twin_near, *cross = from_cross(lists, cross, begun, leaves, True)
        back = swap(twin_near, 1)
        line, twin_near = lax.optimization_barrier((line, twin_near))
        plane = jnp.stack([column] + line)
        gathered = (plane, swap(plane, 1))
        (own_near,) = from_cross(lists, cross, begun, leaves, False)
        near = (own_near, back)

        def place_of(device):
            away = (device % subs) ^ lax.axis_index("sub")
            step = (lax.axis_index("leaf") - device // subs + groups) % groups
            return away % 2, step, away // 2

    else:

        def place_of(device):
            return 0, device

        gathered = (lax.all_gather(packed, ("leaf", "sub")),)
        everyone = [lax.all_gather(x, "sub", axis=1, tiled=True) for x in (points, vectors)]
        factors = prepare(*everyone, width)
        near = (lax.psum(from_subtree(lists, factors, leaves), "pair"),)

    return far_field(
        place_of, subs, far_list, parent_far, near, gathered, skeleton, parent_skel, transfer, basis
    )


def solution(mesh):
    placed = (
        P(None, ("groups", "leaf", "sub")),
        P(None, ("groups", "leaf", "sub")),
        P(("groups", "leaf", "sub"), None, None),
        P(("groups", "leaf", "sub"), None, None),
        P(("groups", "leaf", "sub"), None, None),
        P("groups", None, None),
        P(("groups", "leaf"), None),
        P(("groups", "leaf")),
        P(("groups", "leaf", "sub"), None),
        P(("groups", "leaf"), None),
    )
    return jax.shard_map(
        local,
        mesh=mesh,
        in_specs=placed,
        out_specs=P(None, ("groups", "leaf", "sub")),
        check_vma=False,
    )
```

```python
import functools
import math

import jax
import jax.numpy as jnp
from jax import lax
from jax.experimental import pallas as pl
from jax.experimental.pallas import tpu as pltpu
from jax.sharding import PartitionSpec as P

RATE = 0.125 * math.log2(math.e)
ROWS, COLUMNS = 512, 256
F32, BF16 = jnp.float32, jnp.bfloat16
VMEM = pl.BlockSpec(memory_space=pltpu.VMEM)
HBM = pl.BlockSpec(memory_space=pltpu.HBM)
SMEM = pl.BlockSpec(memory_space=pltpu.SMEM)
PARAMS = pltpu.CompilerParams(vmem_limit_bytes=40 * 1024 * 1024)
NN, NT = (((1,), (0,)), ((), ())), (((1,), (1,)), ((), ()))


def lasts(microseconds):
    return pl.CostEstimate(
        flops=int(1e9 * microseconds), bytes_accessed=int(3e6 * microseconds), transcendentals=0
    )


def mxu(x, y, dims=NN):
    return lax.dot_general(x, y, dims, preferred_element_type=F32)


def split2(x):
    high = x.astype(BF16)
    return high, (x - high.astype(F32)).astype(BF16)


def split3(x):
    high = x.astype(BF16).astype(F32)
    rest = x - high
    middle = rest.astype(BF16).astype(F32)
    return high, middle, (rest - middle).astype(BF16).astype(F32)


def product(x, y, dims=NN):
    rows = x.shape[0]
    x1, x2 = split2(x)
    y1, y2 = split2(y)
    top = mxu(jnp.concatenate([x1, x2], axis=0), y1, dims)
    return top[:rows] + (top[rows:] + mxu(x1, y2, dims))


def source_rows(x):
    a1, a2, a3 = split3(x * (2.0 * RATE))
    return jnp.concatenate([a1, a1, a2, a2, a1, a3], axis=0).T.astype(BF16)


def target_columns(x):
    b1, b2, b3 = split3(x)
    return jnp.concatenate([b1, b2, b1, b2, b3, b1], axis=0).astype(BF16)


def damping(x):
    return jnp.exp2(-RATE * jnp.sum(x * x, axis=0, keepdims=True))


def share_tiles(near_list, near_count, leaves, tiles):
    first = lax.axis_index("leaf") * near_list.shape[0]
    me = lax.axis_index("sub")
    core, chip = me % 2, me // 2
    many = 2 * leaves
    base = chip * many
    zero = jnp.int32(0)

    def entries():
        for place in range(many):
            limit = near_count[base + place]
            for turn in range(1, near_list.shape[1]):
                source = near_list[base + place, turn] - first
                yield place, source, turn < limit, source // leaves

    inner = [zero, zero]
    outer = [[zero, zero], [zero, zero]]
    for place, source, used, device in entries():
        side = place // leaves
        here = device // 2 == chip
        inner[side] = inner[side] + (used & here).astype(jnp.int32)
        for of in range(2):
            out = used & ~here & (device % 2 == of)
            outer[side][of] = outer[side][of] + out.astype(jnp.int32)
    across = [outer[0][of] + outer[1][of] for of in range(2)]
    share = (inner[0] + inner[1] + across[0] + across[1] + 1) // 2 - across[0]
    share = jnp.clip(share, 0, inner[0] + inner[1])
    needed = [
        outer[1][0] + jnp.maximum(share - inner[0], 0),
        outer[0][1] + jnp.maximum(inner[0] - share, 0),
    ]
    total = [across[0] + share, across[1] + inner[0] + inner[1] - share]
    before = jnp.maximum(jnp.minimum(total[0], total[1]) - 1, jnp.maximum(*needed))

    done = zero
    for own in (False, True):
        inside = zero
        for place, source, used, device in entries():
            here = used & (device // 2 == chip)
            mine = here & ((inside < share) == (core == 0))
            across_here = used & (device == (me ^ 2))
            right_side = (core == place // leaves) == own
            tiles[2 + done] = place * (many + leaves) + jnp.where(
                here, source - base, many + source - (me ^ 2) * leaves
            )
            inside = inside + here.astype(jnp.int32)
            done = done + ((mine | across_here) & right_side).astype(jnp.int32)
    tiles[0] = jnp.minimum(before, done)
    tiles[1] = done


def coef_kernel(leaves, share, points, vectors, basis, transfer, skeleton, *refs):
    near_list, near_count, packed, stack, tiles = refs[:5]
    bases, moves, skeletons, lists, counts, sems = refs[5:]
    dim, rank = skeletons.shape[1:]
    width = bases.shape[2]
    vecs = vectors.shape[0]
    held = stack.at[dim:]
    pairs = [(near_list, lists), (near_count, counts), (vectors, held), (basis, bases)]
    pairs += [(transfer, moves), (skeleton, skeletons), (points, stack.at[:dim])]
    loads = [pltpu.make_async_copy(src, dst, sems.at[at]) for at, (src, dst) in enumerate(pairs)]
    for load in loads:
        load.start()
    for load in loads[:2]:
        load.wait()
    if share:
        share_tiles(lists, counts, leaves, tiles)
    else:
        tiles[0] = jnp.int32(0)
    for load in loads[2:]:
        load.wait()
    lift = 0.0
    for leaf in range(leaves):
        lanes = slice(leaf * rank, (leaf + 1) * rank)
        coef = product(held[:, leaf * width : (leaf + 1) * width], bases[leaf], NT)
        packed[0:dim, lanes] = skeletons[leaf]
        packed[dim : dim + vecs, lanes] = coef
        lift = lift + product(coef, moves[leaf])
    rows = vecs // leaves
    for piece in range(leaves):
        packed[dim + vecs :, piece * rank : (piece + 1) * rank] = lift[
            piece * rows : (piece + 1) * rows
        ]


def coefficients(share, lists, points, vectors, basis, transfer, skeleton):
    leaves, dim, rank = skeleton.shape
    vecs = vectors.shape[0]
    inputs = [
        pltpu.with_memory_space_constraint(x, pltpu.HBM)
        for x in (points, vectors, basis, transfer, skeleton, *lists)
    ]
    return pl.pallas_call(
        functools.partial(coef_kernel, leaves, share),
        out_shape=[
            jax.ShapeDtypeStruct((dim + vecs + vecs // leaves, leaves * rank), F32),
            jax.ShapeDtypeStruct((dim + vecs, vectors.shape[1]), F32),
            jax.ShapeDtypeStruct((2 * leaves * lists[0].shape[1] + 3,), jnp.int32),
        ],
        in_specs=[HBM] * 7,
        out_specs=[VMEM, VMEM, SMEM],
        scratch_shapes=[pltpu.VMEM(x.shape, F32) for x in (basis, transfer, skeleton)]
        + [pltpu.SMEM(x.shape, jnp.int32) for x in lists]
        + [pltpu.SemaphoreType.DMA((7,))],
        compiler_params=PARAMS,
        cost_estimate=lasts(0.5),
        name="coefficients",
    )(*inputs)


def write_source(points, vectors, left, coefs):
    vecs = vectors.shape[0]
    left[...] = source_rows(points)
    high, low = split2(vectors * damping(points))
    coefs[0:vecs] = high
    coefs[vecs:] = low


def write_target(points, right, scale):
    right[...] = target_columns(points)
    scale[...] = damping(points) * points.shape[1] ** -0.5


def leaf_of(stack, dim, width, leaf):
    span = slice(leaf * width, (leaf + 1) * width)
    return stack[:dim, span], stack[dim:, span]


def prepare_kernel(dim, width, stack, left, coefs, right, scale):
    for leaf in range(stack.shape[1] // width):
        points, vectors = leaf_of(stack, dim, width, leaf)
        write_source(points, vectors, left.at[leaf], coefs.at[leaf])
        write_target(points, right.at[leaf], scale.at[leaf])


def source_shapes(sources, dim, vecs, width):
    return [
        jax.ShapeDtypeStruct((sources, width, 6 * dim), BF16),
        jax.ShapeDtypeStruct((sources, 2 * vecs, width), BF16),
    ]


def target_shapes(targets, dim, width):
    return [
        jax.ShapeDtypeStruct((targets, 6 * dim, width), BF16),
        jax.ShapeDtypeStruct((targets, 1, width), F32),
    ]


def prepare(stack, dim, width):
    vecs = stack.shape[0] - dim
    count = stack.shape[1] // width
    return pl.pallas_call(
        functools.partial(prepare_kernel, dim, width),
        out_shape=source_shapes(count, dim, vecs, width) + target_shapes(count, dim, width),
        in_specs=[VMEM],
        out_specs=[VMEM] * 4,
        compiler_params=PARAMS,
        cost_estimate=lasts(0.5),
        name="prepare",
    )(stack)


def run_tiles(todo, pick, left, coefs, right, right_base, totals, totals_base):
    vecs, width = totals.shape[1:]
    chunks = [(y, x) for y in range(0, width, COLUMNS) for x in range(0, width, ROWS)]

    def tile(step, carry):
        slot, source = pick(step)

        def exponent(y, x):
            return mxu(left[source, x : x + ROWS], right[right_base + slot, :, y : y + COLUMNS])

        ahead = exponent(*chunks[0])
        for at, (y, x) in enumerate(chunks):
            power = ahead
            if at + 1 < len(chunks):
                ahead = exponent(*chunks[at + 1])
            high, low = split2(jnp.exp2(power))
            both = coefs[source, :, x : x + ROWS]
            top = mxu(both, high)
            found = top[:vecs] + (top[vecs:] + mxu(both[:vecs], low))
            strip = found if x == 0 else strip + found
            if x + ROWS == width:
                totals[totals_base + slot, :, y : y + COLUMNS] += strip
        return carry

    lax.fori_loop(*todo, tile, 0)


def listed(work, start, sources):
    return lambda step: (work[start + step] // sources, work[start + step] % sources)


def self_kernel(dim, stack, left, coefs, right, scale, totals):
    leaves, _, width = totals.shape
    prepare_kernel(dim, width, stack, left, coefs, right, scale)
    totals[...] = jnp.zeros(totals.shape, F32)
    run_tiles((0, leaves), lambda step: (step, step), left, coefs, right, 0, totals, 0)


def with_self(stack, dim, leaves):
    vecs = stack.shape[0] - dim
    width = stack.shape[1] // leaves
    return pl.pallas_call(
        functools.partial(self_kernel, dim),
        out_shape=source_shapes(leaves, dim, vecs, width)
        + target_shapes(leaves, dim, width)
        + [jax.ShapeDtypeStruct((leaves, vecs, width), F32)],
        in_specs=[VMEM],
        out_specs=[VMEM] * 5,
        compiler_params=PARAMS,
        cost_estimate=lasts(0.5),
        name="near_self",
    )(stack)


def before_kernel(leaves, dim, tiles, twin_stack, cross_stack, *refs):
    own_left, own_coefs, own_right, own_totals = refs[:4]
    twin_out, left, coefs, totals, right, scale = refs[4:]
    many, _, width = totals.shape
    core = lax.axis_index("sub") % 2
    own, twin = core * leaves, (1 - core) * leaves
    for leaf in range(leaves):
        left[own + leaf] = own_left[leaf]
        coefs[own + leaf] = own_coefs[leaf]
        right[own + leaf] = own_right[leaf]
        totals[own + leaf] = own_totals[leaf]
        totals[twin + leaf] = jnp.zeros(totals.shape[1:], F32)
        points, vectors = leaf_of(twin_stack, dim, width, leaf)
        write_source(points, vectors, left.at[twin + leaf], coefs.at[twin + leaf])
        write_target(points, right.at[twin + leaf], scale.at[leaf])
        points, vectors = leaf_of(cross_stack, dim, width, leaf)
        write_source(points, vectors, left.at[many + leaf], coefs.at[many + leaf])
    run_tiles((0, tiles[0]), listed(tiles, 2, many + leaves), left, coefs, right, 0, totals, 0)
    for leaf in range(leaves):
        twin_out[:, leaf * width : (leaf + 1) * width] = totals[twin + leaf] * scale[leaf]


def tiles_before(tiles, twin, cross, own, leaves):
    left, coefs, right, _, totals = own
    vecs, width = totals.shape[1:]
    dim = twin.shape[0] - vecs
    return pl.pallas_call(
        functools.partial(before_kernel, leaves, dim),
        out_shape=[jax.ShapeDtypeStruct((vecs, leaves * width), F32)]
        + source_shapes(3 * leaves, dim, vecs, width)
        + [jax.ShapeDtypeStruct((2 * leaves, vecs, width), F32)],
        in_specs=[SMEM] + [VMEM] * 6,
        out_specs=[VMEM] * 4,
        scratch_shapes=[
            pltpu.VMEM((2 * leaves, 6 * dim, width), BF16),
            pltpu.VMEM((leaves, 1, width), F32),
        ],
        compiler_params=PARAMS,
        cost_estimate=lasts(0.5),
        name="near_before",
    )(tiles, twin, cross, left, coefs, right, totals)


def after_kernel(leaves, tiles, left, coefs, right, scale, begun, out, totals):
    width = totals.shape[2]
    sources = left.shape[0]
    own = lax.axis_index("sub") % 2 * leaves
    for leaf in range(leaves):
        totals[leaf] = begun[own + leaf]

    def pick(step):
        code = tiles[2 + step]
        return code // sources - own, code % sources

    run_tiles((tiles[0], tiles[1]), pick, left, coefs, right, 0, totals, 0)
    for leaf in range(leaves):
        out[:, leaf * width : (leaf + 1) * width] = totals[leaf] * scale[leaf]


def tiles_after(tiles, left, coefs, right, scale, begun):
    leaves = right.shape[0]
    vecs, width = begun.shape[1:]
    return pl.pallas_call(
        functools.partial(after_kernel, leaves),
        out_shape=jax.ShapeDtypeStruct((vecs, leaves * width), F32),
        in_specs=[SMEM] + [VMEM] * 5,
        out_specs=VMEM,
        scratch_shapes=[pltpu.VMEM((leaves, vecs, width), F32)],
        compiler_params=PARAMS,
        cost_estimate=lasts(0.5),
        name="near_after",
    )(tiles, left, coefs, right, scale, begun)


def list_tiles(near_list, near_count, leaves, target, source_base, sources, work):
    first = lax.axis_index("leaf") * near_list.shape[0]
    pair_size, pair_at = lax.axis_size("pair"), lax.axis_index("pair")
    todo = jnp.int32(0)
    for leaf in range(leaves):
        place = target * leaves + leaf
        limit = near_count[place]
        for turn in range(near_list.shape[1]):
            source = near_list[place, turn] - first - source_base
            wanted = (turn < limit) & (source >= 0) & (source < sources)
            if pair_size > 1:
                wanted = wanted & (pair_at == turn % pair_size)
            work[todo] = leaf * sources + source
            todo = todo + wanted.astype(jnp.int32)
    return todo


def subtree_kernel(leaves, near_list, near_count, left, coefs, right, scale, out, totals, work):
    me = lax.axis_index("sub")
    vecs, width = totals.shape[1:]
    sources = left.shape[0]
    todo = list_tiles(near_list, near_count, leaves, me, 0, sources, work)
    totals[...] = jnp.zeros(totals.shape, F32)
    run_tiles((0, todo), listed(work, 0, sources), left, coefs, right, me * leaves, totals, 0)
    for leaf in range(leaves):
        out[:, leaf * width : (leaf + 1) * width] = totals[leaf] * scale[me * leaves + leaf]


def from_subtree(lists, factors, leaves):
    near_list, near_count = lists
    vecs, width = factors[1].shape[1] // 2, factors[1].shape[2]
    return pl.pallas_call(
        functools.partial(subtree_kernel, leaves),
        out_shape=jax.ShapeDtypeStruct((vecs, leaves * width), F32),
        in_specs=[SMEM, SMEM] + [VMEM] * 4,
        out_specs=VMEM,
        scratch_shapes=[
            pltpu.VMEM((leaves, vecs, width), F32),
            pltpu.SMEM((leaves * near_list.shape[1] + 1,), jnp.int32),
        ],
        compiler_params=PARAMS,
        name="near_subtree",
    )(near_list, near_count, *factors)


def interact(source, coefs, target):
    kernel = jnp.exp2(mxu(source_rows(source), target_columns(target)))
    return product(coefs * damping(source), kernel) * damping(target)


def far_kernel(place_of, leaves, subs, nears, far_list, parent_far, *refs):
    refs, (skeleton, parent_skel, transfer, basis, out) = refs[:-5], refs[-5:]
    near, gathered = refs[:nears], refs[nears:]
    dim, rank = skeleton.shape[1:]
    width = basis.shape[2]
    vecs = out.shape[0]

    def block(device):
        which, *index = place_of(device)
        found = gathered[0][tuple(index)]
        for other in range(1, len(gathered)):
            found = jnp.where(which == other, gathered[other][tuple(index)], found)
        return found

    def lanes(data, at):
        found = data[:, :rank]
        for other in range(1, leaves):
            found = jnp.where(at == other, data[:, other * rank : (other + 1) * rank], found)
        return found

    points, coefs = [], []
    for turn in range(parent_far.shape[1]):
        parent = parent_far[0, turn]
        lift = block(parent * subs)[dim + vecs :]
        for sub in range(1, subs):
            lift = lift + block(parent * subs + sub)[dim + vecs :]
        coefs.append(
            jnp.concatenate([lift[:, at * rank : (at + 1) * rank] for at in range(leaves)], axis=0)
        )
        points.append(parent_skel[parent])
    own = parent_skel[lax.axis_index("leaf")]
    upper = interact(
        jnp.concatenate(points, axis=1), jnp.concatenate(coefs, axis=1), own
    ) * (rank**-0.5)

    for leaf in range(leaves):
        points, coefs = [], []
        for turn in range(far_list.shape[1]):
            partner = far_list[leaf, turn]
            data = lanes(block(partner // leaves), partner % leaves)
            points.append(data[:dim])
            coefs.append(data[dim : dim + vecs])
        far = interact(
            jnp.concatenate(points, axis=1), jnp.concatenate(coefs, axis=1), skeleton[leaf]
        ) * (rank**-0.5)
        field = far + product(upper, transfer[leaf], NT)
        span = slice(leaf * width, (leaf + 1) * width)
        total = product(field, basis[leaf])
        for part in near:
            total = total + part[:, span]
        out[:, span] = total


def far_field(place_of, subs, far_list, parent_far, near, gathered, *held):
    skeleton, _, _, basis = held
    leaves, rank, width = basis.shape
    vecs = near[0].shape[0]
    return pl.pallas_call(
        functools.partial(far_kernel, place_of, leaves, subs, len(near)),
        out_shape=jax.ShapeDtypeStruct((vecs, leaves * width), F32),
        in_specs=[SMEM, SMEM] + [VMEM] * (len(near) + len(gathered) + 4),
        out_specs=VMEM,
        compiler_params=PARAMS,
        cost_estimate=lasts(0.5),
        name="far_field",
    )(far_list, parent_far, *near, *gathered, *held)


def swap(x, bit, axis="sub"):
    return lax.ppermute(x, axis, [(at, at ^ bit) for at in range(lax.axis_size(axis))])


def local(
    points,
    vectors,
    basis,
    transfer,
    skeleton,
    parent_skel,
    near_list,
    near_count,
    far_list,
    parent_far,
):
    leaves, _, width = basis.shape
    dim = points.shape[0]
    subs, groups = lax.axis_size("sub"), lax.axis_size("leaf")
    lists = (near_list, near_count)
    split = subs == 4 and lax.axis_size("pair") == 1 and groups & (groups - 1) == 0
    packed, stack, tiles = coefficients(split, lists, points, vectors, basis, transfer, skeleton)
    if split:
        twin, cross = swap(stack, 1), swap(stack, 2)
        line = [packed] + [swap(packed, step, "leaf") for step in range(1, groups)]
        own = with_self(stack, dim, leaves)
        line, own = lax.optimization_barrier((line, own))
        line = jnp.stack(line)
        beside = swap(line, 2)
        twin_near, *held, begun = tiles_before(tiles, twin, cross, own, leaves)
        back = swap(twin_near, 1)
        beside, twin_near = lax.optimization_barrier((beside, twin_near))
        plane = jnp.stack([line, beside])
        gathered = (plane, swap(plane, 1))
        near = (tiles_after(tiles, *held, *own[2:4], begun), back)

        def place_of(device):
            away = (device % subs) ^ lax.axis_index("sub")
            return away % 2, away // 2, (device // subs) ^ lax.axis_index("leaf")

    else:

        def place_of(device):
            return 0, device

        gathered = (lax.all_gather(packed, ("leaf", "sub")),)
        everyone = lax.all_gather(stack, "sub", axis=1, tiled=True)
        factors = prepare(everyone, dim, width)
        near = (lax.psum(from_subtree(lists, factors, leaves), "pair"),)

    return far_field(
        place_of, subs, far_list, parent_far, near, gathered, skeleton, parent_skel, transfer, basis
    )


def solution(mesh):
    placed = (
        P(None, ("groups", "leaf", "sub")),
        P(None, ("groups", "leaf", "sub")),
        P(("groups", "leaf", "sub"), None, None),
        P(("groups", "leaf", "sub"), None, None),
        P(("groups", "leaf", "sub"), None, None),
        P("groups", None, None),
        P(("groups", "leaf"), None),
        P(("groups", "leaf")),
        P(("groups", "leaf", "sub"), None),
        P(("groups", "leaf"), None),
    )
    return jax.shard_map(
        local,
        mesh=mesh,
        in_specs=placed,
        out_specs=P(None, ("groups", "leaf", "sub")),
        check_vma=False,
    )
```

```python
import functools
import math

import jax
import jax.numpy as jnp
from jax import lax
from jax.experimental import pallas as pl
from jax.experimental.pallas import tpu as pltpu
from jax.sharding import PartitionSpec as P

RATE = 0.125 * math.log2(math.e)
ROWS, COLUMNS = 256, 512
F32, BF16 = jnp.float32, jnp.bfloat16
VMEM = pl.BlockSpec(memory_space=pltpu.VMEM)
HBM = pl.BlockSpec(memory_space=pltpu.HBM)
SMEM = pl.BlockSpec(memory_space=pltpu.SMEM)
PARAMS = pltpu.CompilerParams(vmem_limit_bytes=40 * 1024 * 1024)
NN, NT = (((1,), (0,)), ((), ())), (((1,), (1,)), ((), ()))


def lasts(microseconds):
    return pl.CostEstimate(
        flops=int(1e9 * microseconds), bytes_accessed=int(3e6 * microseconds), transcendentals=0
    )


def mxu(x, y, dims=NN):
    return lax.dot_general(x, y, dims, preferred_element_type=F32)


def split2(x):
    high = x.astype(BF16)
    return high, (x - high.astype(F32)).astype(BF16)


def split3(x):
    high = x.astype(BF16).astype(F32)
    rest = x - high
    middle = rest.astype(BF16).astype(F32)
    return high, middle, (rest - middle).astype(BF16).astype(F32)


def product(x, y, dims=NN):
    rows = x.shape[0]
    x1, x2 = split2(x)
    y1, y2 = split2(y)
    top = mxu(jnp.concatenate([x1, x2], axis=0), y1, dims)
    return top[:rows] + (top[rows:] + mxu(x1, y2, dims))


def source_rows(x):
    a1, a2, a3 = split3(x * (2.0 * RATE))
    return jnp.concatenate([a1, a1, a2, a2, a1, a3], axis=0).T.astype(BF16)


def target_columns(x):
    b1, b2, b3 = split3(x)
    return jnp.concatenate([b1, b2, b1, b2, b3, b1], axis=0).astype(BF16)


def damping(x):
    return jnp.exp2(-RATE * jnp.sum(x * x, axis=0, keepdims=True))


def share_tiles(near_list, near_count, leaves, tiles):
    first = lax.axis_index("leaf") * near_list.shape[0]
    me = lax.axis_index("sub")
    core, chip = me % 2, me // 2
    many = 2 * leaves
    base = chip * many
    zero = jnp.int32(0)

    def entries():
        for place in range(many):
            limit = near_count[base + place]
            for turn in range(1, near_list.shape[1]):
                source = near_list[base + place, turn] - first
                yield place, source, turn < limit, source // leaves

    inner = [zero, zero]
    outer = [[zero, zero], [zero, zero]]
    for place, source, used, device in entries():
        side = place // leaves
        here = device // 2 == chip
        inner[side] = inner[side] + (used & here).astype(jnp.int32)
        for of in range(2):
            out = used & ~here & (device % 2 == of)
            outer[side][of] = outer[side][of] + out.astype(jnp.int32)
    across = [outer[0][of] + outer[1][of] for of in range(2)]
    share = (inner[0] + inner[1] + across[0] + across[1] + 1) // 2 - across[0]
    share = jnp.clip(share, 0, inner[0] + inner[1])
    needed = [
        outer[1][0] + jnp.maximum(share - inner[0], 0),
        outer[0][1] + jnp.maximum(inner[0] - share, 0),
    ]
    total = [across[0] + share, across[1] + inner[0] + inner[1] - share]
    before = jnp.maximum(jnp.minimum(total[0], total[1]) - 1, jnp.maximum(*needed))

    done = zero
    for local in (True, False):
        for own in (False, True):
            inside = zero
            for place, source, used, device in entries():
                here = used & (device // 2 == chip)
                if local:
                    wanted = here & ((inside < share) == (core == 0))
                    index = source - base
                else:
                    wanted = used & (device == (me ^ 2))
                    index = many + source - (me ^ 2) * leaves
                wanted = wanted & ((core == place // leaves) == own)
                tiles[3 + done] = place * (many + leaves) + index
                inside = inside + here.astype(jnp.int32)
                done = done + wanted.astype(jnp.int32)
        if local:
            tiles[0] = done
    spare = jnp.where(core == 0, outer[0][0], outer[1][1])
    tiles[1] = done - jnp.clip(done - before, 0, spare)
    tiles[2] = done


def coef_kernel(leaves, share, points, vectors, basis, transfer, skeleton, *refs):
    near_list, near_count, packed, stack, tiles = refs[:5]
    bases, moves, skeletons, lists, counts, sems = refs[5:]
    dim, rank = skeletons.shape[1:]
    width = bases.shape[2]
    vecs = vectors.shape[0]
    held = stack.at[dim:]
    pairs = [(near_list, lists), (near_count, counts), (vectors, held), (basis, bases)]
    pairs += [(transfer, moves), (skeleton, skeletons), (points, stack.at[:dim])]
    loads = [pltpu.make_async_copy(src, dst, sems.at[at]) for at, (src, dst) in enumerate(pairs)]
    for load in loads:
        load.start()
    for load in loads:
        load.wait()
    if share:
        share_tiles(lists, counts, leaves, tiles)
    else:
        tiles[0] = jnp.int32(0)
    lift = 0.0
    for leaf in range(leaves):
        lanes = slice(leaf * rank, (leaf + 1) * rank)
        coef = product(held[:, leaf * width : (leaf + 1) * width], bases[leaf], NT)
        packed[0:dim, lanes] = skeletons[leaf]
        packed[dim : dim + vecs, lanes] = coef
        lift = lift + product(coef, moves[leaf])
    rows = vecs // leaves
    for piece in range(leaves):
        packed[dim + vecs :, piece * rank : (piece + 1) * rank] = lift[
            piece * rows : (piece + 1) * rows
        ]


def coefficients(share, lists, points, vectors, basis, transfer, skeleton):
    leaves, dim, rank = skeleton.shape
    vecs = vectors.shape[0]
    inputs = [
        pltpu.with_memory_space_constraint(x, pltpu.HBM)
        for x in (points, vectors, basis, transfer, skeleton, *lists)
    ]
    return pl.pallas_call(
        functools.partial(coef_kernel, leaves, share),
        out_shape=[
            jax.ShapeDtypeStruct((dim + vecs + vecs // leaves, leaves * rank), F32),
            jax.ShapeDtypeStruct((dim + vecs, vectors.shape[1]), F32),
            jax.ShapeDtypeStruct((2 * leaves * lists[0].shape[1] + 4,), jnp.int32),
        ],
        in_specs=[HBM] * 7,
        out_specs=[VMEM, VMEM, SMEM],
        scratch_shapes=[pltpu.VMEM(x.shape, F32) for x in (basis, transfer, skeleton)]
        + [pltpu.SMEM(x.shape, jnp.int32) for x in lists]
        + [pltpu.SemaphoreType.DMA((7,))],
        compiler_params=PARAMS,
        cost_estimate=lasts(0.5),
        name="coefficients",
    )(*inputs)


def write_source(points, vectors, left, coefs):
    vecs = vectors.shape[0]
    left[...] = source_rows(points)
    high, low = split2(vectors * damping(points))
    coefs[0:vecs] = high
    coefs[vecs:] = low


def write_target(points, right, scale):
    right[...] = target_columns(points)
    scale[...] = damping(points) * points.shape[1] ** -0.5


def leaf_of(stack, dim, width, leaf):
    span = slice(leaf * width, (leaf + 1) * width)
    return stack[:dim, span], stack[dim:, span]


def prepare_kernel(dim, width, stack, left, coefs, right, scale):
    for leaf in range(stack.shape[1] // width):
        points, vectors = leaf_of(stack, dim, width, leaf)
        write_source(points, vectors, left.at[leaf], coefs.at[leaf])
        write_target(points, right.at[leaf], scale.at[leaf])


def source_shapes(sources, dim, vecs, width):
    return [
        jax.ShapeDtypeStruct((sources, width, 6 * dim), BF16),
        jax.ShapeDtypeStruct((sources, 2 * vecs, width), BF16),
    ]


def target_shapes(targets, dim, width):
    return [
        jax.ShapeDtypeStruct((targets, 6 * dim, width), BF16),
        jax.ShapeDtypeStruct((targets, 1, width), F32),
    ]


def prepare(stack, dim, width):
    vecs = stack.shape[0] - dim
    count = stack.shape[1] // width
    return pl.pallas_call(
        functools.partial(prepare_kernel, dim, width),
        out_shape=source_shapes(count, dim, vecs, width) + target_shapes(count, dim, width),
        in_specs=[VMEM],
        out_specs=[VMEM] * 4,
        compiler_params=PARAMS,
        cost_estimate=lasts(0.5),
        name="prepare",
    )(stack)


def run_tiles(todo, pick, left, coefs, right, right_base, totals, totals_base):
    vecs, width = totals.shape[1:]
    chunks = [(y, x) for y in range(0, width, COLUMNS) for x in range(0, width, ROWS)]

    def tile(step, carry):
        slot, source = pick(step)

        def exponent(y, x):
            return mxu(left[source, x : x + ROWS], right[right_base + slot, :, y : y + COLUMNS])

        ahead = exponent(*chunks[0])
        for at, (y, x) in enumerate(chunks):
            power = ahead
            if at + 1 < len(chunks):
                ahead = exponent(*chunks[at + 1])
            high, low = split2(jnp.exp2(power))
            both = coefs[source, :, x : x + ROWS]
            top = mxu(both, high)
            found = top[:vecs] + (top[vecs:] + mxu(both[:vecs], low))
            strip = found if x == 0 else strip + found
            if x + ROWS == width:
                totals[totals_base + slot, :, y : y + COLUMNS] += strip
        return carry

    lax.fori_loop(*todo, tile, 0)


def listed(work, start, sources):
    return lambda step: (work[start + step] // sources, work[start + step] % sources)


def self_kernel(dim, stack, left, coefs, right, scale, totals):
    leaves, _, width = totals.shape
    prepare_kernel(dim, width, stack, left, coefs, right, scale)
    totals[...] = jnp.zeros(totals.shape, F32)
    run_tiles((0, leaves), lambda step: (step, step), left, coefs, right, 0, totals, 0)


def with_self(stack, dim, leaves):
    vecs = stack.shape[0] - dim
    width = stack.shape[1] // leaves
    return pl.pallas_call(
        functools.partial(self_kernel, dim),
        out_shape=source_shapes(leaves, dim, vecs, width)
        + target_shapes(leaves, dim, width)
        + [jax.ShapeDtypeStruct((leaves, vecs, width), F32)],
        in_specs=[VMEM],
        out_specs=[VMEM] * 5,
        compiler_params=PARAMS,
        cost_estimate=lasts(0.5),
        name="near_self",
    )(stack)


def local_kernel(leaves, dim, tiles, twin_stack, *refs):
    own_left, own_coefs, own_right, own_totals = refs[:4]
    right, scale, totals, left, coefs = refs[4:]
    many, _, width = totals.shape
    core = lax.axis_index("sub") % 2
    own, twin = core * leaves, (1 - core) * leaves
    for leaf in range(leaves):
        left[own + leaf] = own_left[leaf]
        coefs[own + leaf] = own_coefs[leaf]
        right[own + leaf] = own_right[leaf]
        totals[own + leaf] = own_totals[leaf]
        totals[twin + leaf] = jnp.zeros(totals.shape[1:], F32)
        points, vectors = leaf_of(twin_stack, dim, width, leaf)
        write_source(points, vectors, left.at[twin + leaf], coefs.at[twin + leaf])
        write_target(points, right.at[twin + leaf], scale.at[leaf])
    run_tiles((0, tiles[0]), listed(tiles, 3, many + leaves), left, coefs, right, 0, totals, 0)


def tiles_local(tiles, twin, own, leaves):
    left, coefs, right, _, totals = own
    vecs, width = totals.shape[1:]
    dim = twin.shape[0] - vecs
    many = 2 * leaves
    return pl.pallas_call(
        functools.partial(local_kernel, leaves, dim),
        out_shape=[
            jax.ShapeDtypeStruct((many, 6 * dim, width), BF16),
            jax.ShapeDtypeStruct((leaves, 1, width), F32),
            jax.ShapeDtypeStruct((many, vecs, width), F32),
        ],
        in_specs=[SMEM] + [VMEM] * 5,
        out_specs=[VMEM] * 3,
        scratch_shapes=[
            pltpu.VMEM((many, width, 6 * dim), BF16),
            pltpu.VMEM((many, 2 * vecs, width), BF16),
        ],
        compiler_params=PARAMS,
        cost_estimate=lasts(0.5),
        name="near_local",
    )(tiles, twin, left, coefs, right, totals)


def from_neighbour(tiles, sources, many):
    def pick(step):
        code = tiles[3 + step]
        return code // sources, code % sources - many

    return pick


def cross_kernel(leaves, dim, tiles, cross_stack, right, scale, begun, *refs):
    twin_out, left, coefs, own_totals, totals = refs
    many, _, width = totals.shape
    core = lax.axis_index("sub") % 2
    own, twin = core * leaves, (1 - core) * leaves
    for leaf in range(leaves):
        points, vectors = leaf_of(cross_stack, dim, width, leaf)
        write_source(points, vectors, left.at[leaf], coefs.at[leaf])
    totals[...] = begun[...]
    pick = from_neighbour(tiles, many + leaves, many)
    run_tiles((tiles[0], tiles[1]), pick, left, coefs, right, 0, totals, 0)
    for leaf in range(leaves):
        twin_out[:, leaf * width : (leaf + 1) * width] = totals[twin + leaf] * scale[leaf]
        own_totals[leaf] = totals[own + leaf]


def tiles_cross(tiles, cross, right, scale, begun):
    many, vecs, width = begun.shape
    leaves = many // 2
    dim = cross.shape[0] - vecs
    return pl.pallas_call(
        functools.partial(cross_kernel, leaves, dim),
        out_shape=[jax.ShapeDtypeStruct((vecs, leaves * width), F32)]
        + source_shapes(leaves, dim, vecs, width)
        + [jax.ShapeDtypeStruct((leaves, vecs, width), F32)],
        in_specs=[SMEM] + [VMEM] * 4,
        out_specs=[VMEM] * 4,
        scratch_shapes=[pltpu.VMEM((many, vecs, width), F32)],
        compiler_params=PARAMS,
        cost_estimate=lasts(0.5),
        name="near_cross",
    )(tiles, cross, right, scale, begun)


def after_kernel(leaves, tiles, left, coefs, right, scale, begun, out, totals):
    width = totals.shape[2]
    own = lax.axis_index("sub") % 2 * leaves
    totals[...] = begun[...]
    pick = from_neighbour(tiles, 3 * leaves, 2 * leaves)

    def own_pick(step):
        place, source = pick(step)
        return place - own, source

    run_tiles((tiles[1], tiles[2]), own_pick, left, coefs, right, 0, totals, 0)
    for leaf in range(leaves):
        out[:, leaf * width : (leaf + 1) * width] = totals[leaf] * scale[leaf]


def tiles_after(tiles, left, coefs, right, scale, begun):
    leaves, vecs, width = begun.shape
    return pl.pallas_call(
        functools.partial(after_kernel, leaves),
        out_shape=jax.ShapeDtypeStruct((vecs, leaves * width), F32),
        in_specs=[SMEM] + [VMEM] * 5,
        out_specs=VMEM,
        scratch_shapes=[pltpu.VMEM((leaves, vecs, width), F32)],
        compiler_params=PARAMS,
        cost_estimate=lasts(0.5),
        name="near_after",
    )(tiles, left, coefs, right, scale, begun)


def list_tiles(near_list, near_count, leaves, target, source_base, sources, work):
    first = lax.axis_index("leaf") * near_list.shape[0]
    pair_size, pair_at = lax.axis_size("pair"), lax.axis_index("pair")
    todo = jnp.int32(0)
    for leaf in range(leaves):
        place = target * leaves + leaf
        limit = near_count[place]
        for turn in range(near_list.shape[1]):
            source = near_list[place, turn] - first - source_base
            wanted = (turn < limit) & (source >= 0) & (source < sources)
            if pair_size > 1:
                wanted = wanted & (pair_at == turn % pair_size)
            work[todo] = leaf * sources + source
            todo = todo + wanted.astype(jnp.int32)
    return todo


def subtree_kernel(leaves, near_list, near_count, left, coefs, right, scale, out, totals, work):
    me = lax.axis_index("sub")
    vecs, width = totals.shape[1:]
    sources = left.shape[0]
    todo = list_tiles(near_list, near_count, leaves, me, 0, sources, work)
    totals[...] = jnp.zeros(totals.shape, F32)
    run_tiles((0, todo), listed(work, 0, sources), left, coefs, right, me * leaves, totals, 0)
    for leaf in range(leaves):
        out[:, leaf * width : (leaf + 1) * width] = totals[leaf] * scale[me * leaves + leaf]


def from_subtree(lists, factors, leaves):
    near_list, near_count = lists
    vecs, width = factors[1].shape[1] // 2, factors[1].shape[2]
    return pl.pallas_call(
        functools.partial(subtree_kernel, leaves),
        out_shape=jax.ShapeDtypeStruct((vecs, leaves * width), F32),
        in_specs=[SMEM, SMEM] + [VMEM] * 4,
        out_specs=VMEM,
        scratch_shapes=[
            pltpu.VMEM((leaves, vecs, width), F32),
            pltpu.SMEM((leaves * near_list.shape[1] + 1,), jnp.int32),
        ],
        compiler_params=PARAMS,
        name="near_subtree",
    )(near_list, near_count, *factors)


def interact(source, coefs, target):
    kernel = jnp.exp2(mxu(source_rows(source), target_columns(target)))
    return product(coefs * damping(source), kernel) * damping(target)


def far_kernel(place_of, leaves, subs, nears, far_list, parent_far, *refs):
    refs, (skeleton, parent_skel, transfer, basis, out) = refs[:-5], refs[-5:]
    near, gathered = refs[:nears], refs[nears:]
    dim, rank = skeleton.shape[1:]
    width = basis.shape[2]
    vecs = out.shape[0]

    def block(device):
        which, *index = place_of(device)
        found = gathered[0][tuple(index)]
        for other in range(1, len(gathered)):
            found = jnp.where(which == other, gathered[other][tuple(index)], found)
        return found

    def lanes(data, at):
        found = data[:, :rank]
        for other in range(1, leaves):
            found = jnp.where(at == other, data[:, other * rank : (other + 1) * rank], found)
        return found

    points, coefs = [], []
    for turn in range(parent_far.shape[1]):
        parent = parent_far[0, turn]
        lift = block(parent * subs)[dim + vecs :]
        for sub in range(1, subs):
            lift = lift + block(parent * subs + sub)[dim + vecs :]
        coefs.append(
            jnp.concatenate([lift[:, at * rank : (at + 1) * rank] for at in range(leaves)], axis=0)
        )
        points.append(parent_skel[parent])
    own = parent_skel[lax.axis_index("leaf")]
    upper = interact(
        jnp.concatenate(points, axis=1), jnp.concatenate(coefs, axis=1), own
    ) * (rank**-0.5)

    for leaf in range(leaves):
        points, coefs = [], []
        for turn in range(far_list.shape[1]):
            partner = far_list[leaf, turn]
            data = lanes(block(partner // leaves), partner % leaves)
            points.append(data[:dim])
            coefs.append(data[dim : dim + vecs])
        far = interact(
            jnp.concatenate(points, axis=1), jnp.concatenate(coefs, axis=1), skeleton[leaf]
        ) * (rank**-0.5)
        field = far + product(upper, transfer[leaf], NT)
        span = slice(leaf * width, (leaf + 1) * width)
        total = product(field, basis[leaf])
        for part in near:
            total = total + part[:, span]
        out[:, span] = total


def far_field(place_of, subs, far_list, parent_far, near, gathered, *held):
    skeleton, _, _, basis = held
    leaves, rank, width = basis.shape
    vecs = near[0].shape[0]
    return pl.pallas_call(
        functools.partial(far_kernel, place_of, leaves, subs, len(near)),
        out_shape=jax.ShapeDtypeStruct((vecs, leaves * width), F32),
        in_specs=[SMEM, SMEM] + [VMEM] * (len(near) + len(gathered) + 4),
        out_specs=VMEM,
        compiler_params=PARAMS,
        cost_estimate=lasts(0.5),
        name="far_field",
    )(far_list, parent_far, *near, *gathered, *held)


def swap(x, bit, axis="sub"):
    return lax.ppermute(x, axis, [(at, at ^ bit) for at in range(lax.axis_size(axis))])


def local(
    points,
    vectors,
    basis,
    transfer,
    skeleton,
    parent_skel,
    near_list,
    near_count,
    far_list,
    parent_far,
):
    leaves, _, width = basis.shape
    dim = points.shape[0]
    subs, groups = lax.axis_size("sub"), lax.axis_size("leaf")
    lists = (near_list, near_count)
    split = subs == 4 and lax.axis_size("pair") == 1 and groups in (4, 8, 16)
    packed, stack, tiles = coefficients(split, lists, points, vectors, basis, transfer, skeleton)
    if split:
        twin, cross = swap(stack, 1), swap(stack, 2)
        line = packed[None]
        for bit in range(groups.bit_length() - 1):
            arrived = swap(line, 1 << bit, "leaf")
            if bit == 0:
                own = with_self(stack, dim, leaves)
                arrived, own = lax.optimization_barrier((arrived, own))
            elif bit == 1:
                right, scale, begun = tiles_local(tiles, twin, own, leaves)
                arrived, begun = lax.optimization_barrier((arrived, begun))
            line = jnp.concatenate([line, arrived])
        beside = swap(line, 2)
        twin_near, *held, begun = tiles_cross(tiles, cross, right, scale, begun)
        back = swap(twin_near, 1)
        beside, twin_near = lax.optimization_barrier((beside, twin_near))
        plane = jnp.stack([line, beside])
        gathered = (plane, swap(plane, 1))
        near = (tiles_after(tiles, *held, *own[2:4], begun), back)

        def place_of(device):
            away = (device % subs) ^ lax.axis_index("sub")
            return away % 2, away // 2, (device // subs) ^ lax.axis_index("leaf")

    else:

        def place_of(device):
            return 0, device

        gathered = (lax.all_gather(packed, ("leaf", "sub")),)
        everyone = lax.all_gather(stack, "sub", axis=1, tiled=True)
        factors = prepare(everyone, dim, width)
        near = (lax.psum(from_subtree(lists, factors, leaves), "pair"),)

    return far_field(
        place_of, subs, far_list, parent_far, near, gathered, skeleton, parent_skel, transfer, basis
    )


def solution(mesh):
    placed = (
        P(None, ("groups", "leaf", "sub")),
        P(None, ("groups", "leaf", "sub")),
        P(("groups", "leaf", "sub"), None, None),
        P(("groups", "leaf", "sub"), None, None),
        P(("groups", "leaf", "sub"), None, None),
        P("groups", None, None),
        P(("groups", "leaf"), None),
        P(("groups", "leaf")),
        P(("groups", "leaf", "sub"), None),
        P(("groups", "leaf"), None),
    )
    return jax.shard_map(
        local,
        mesh=mesh,
        in_specs=placed,
        out_specs=P(None, ("groups", "leaf", "sub")),
        check_vma=False,
    )
```

```python
import functools
import math

import jax
import jax.numpy as jnp
from jax import lax
from jax.experimental import pallas as pl
from jax.experimental.pallas import tpu as pltpu
from jax.sharding import PartitionSpec as P

RATE = 0.125 * math.log2(math.e)
ROWS, COLUMNS = 256, 1024
F32, BF16 = jnp.float32, jnp.bfloat16
VMEM = pl.BlockSpec(memory_space=pltpu.VMEM)
HBM = pl.BlockSpec(memory_space=pltpu.HBM)
SMEM = pl.BlockSpec(memory_space=pltpu.SMEM)
PARAMS = pltpu.CompilerParams(vmem_limit_bytes=40 * 1024 * 1024)
NN, NT = (((1,), (0,)), ((), ())), (((1,), (1,)), ((), ()))


def lasts(microseconds):
    return pl.CostEstimate(
        flops=int(1e9 * microseconds), bytes_accessed=int(3e6 * microseconds), transcendentals=0
    )


def mxu(x, y, dims=NN):
    return lax.dot_general(x, y, dims, preferred_element_type=F32)


def split2(x):
    high = x.astype(BF16)
    return high, (x - high.astype(F32)).astype(BF16)


def split3(x):
    high = x.astype(BF16).astype(F32)
    rest = x - high
    middle = rest.astype(BF16).astype(F32)
    return high, middle, (rest - middle).astype(BF16).astype(F32)


def product(x, y, dims=NN):
    rows = x.shape[0]
    x1, x2 = split2(x)
    y1, y2 = split2(y)
    top = mxu(jnp.concatenate([x1, x2], axis=0), y1, dims)
    return top[:rows] + (top[rows:] + mxu(x1, y2, dims))


def source_rows(x):
    a1, a2, a3 = split3(x * (2.0 * RATE))
    return jnp.concatenate([a1, a1, a2, a2, a1, a3], axis=0).T.astype(BF16)


def target_columns(x):
    b1, b2, b3 = split3(x)
    return jnp.concatenate([b1, b2, b1, b2, b3, b1], axis=0).astype(BF16)


def damping(x):
    return jnp.exp2(-RATE * jnp.sum(x * x, axis=0, keepdims=True))


HEAD = 7


def share_tiles(near_list, near_count, leaves, tiles):
    turns = near_list.shape[1]
    me = lax.axis_index("sub")
    core = me % 2
    many = 2 * leaves
    first = lax.axis_index("leaf") * near_list.shape[0]
    base = me // 2 * many
    beside = (me ^ 2) * leaves
    cross_at = HEAD + many * turns
    zero = jnp.int32(0)
    local, cross, used_all, marks = zero, zero, zero, []
    for index in range(many):
        side = 1 - core if index < leaves else core
        place = side * leaves + index % leaves
        limit = near_count[base + place]
        used_all = used_all + limit - 1
        for turn in range(1, turns):
            source = near_list[base + place, turn] - first
            used = turn < limit
            near = source - base
            away = source - beside
            tiles[HEAD + local] = place * many + near
            tiles[cross_at + cross] = place * leaves + away
            local = local + (used & (near >= 0) & (near < many)).astype(jnp.int32)
            cross = cross + (used & (away >= 0) & (away < leaves)).astype(jnp.int32)
        if index == leaves - 1:
            marks = [local, cross]
    other = used_all - local - cross
    own_local, own_cross = local - marks[0], cross - marks[1]
    mine = jnp.clip((used_all + 1 - core) // 2 - cross, 0, local)
    total, twin_total = mine + cross, local - mine + other
    after = total - jnp.minimum(total, twin_total) + 1
    after_cross = jnp.clip(after, 0, own_cross)
    after_local = jnp.clip(after - after_cross, 0, jnp.minimum(mine, own_local))
    tiles[0] = jnp.where(core == 0, marks[0] + mine - 1, local - mine)
    tiles[1] = jnp.where(core == 0, -1, 1)
    tiles[2] = local
    tiles[3] = mine - after_local
    tiles[4] = mine
    tiles[5] = cross - after_cross
    tiles[6] = cross


def walk(tiles, many):
    def pick(step):
        at = tiles[0] + tiles[1] * step
        code = tiles[HEAD + jnp.where(at >= tiles[2], at - tiles[2], at)]
        return code // many, code % many

    return pick


def walk_cross(tiles, leaves):
    cross_at = HEAD + (tiles.shape[0] - HEAD) // 2

    def pick(step):
        code = tiles[cross_at + step]
        return code // leaves, code % leaves

    return pick


def coef_kernel(leaves, share, points, vectors, basis, transfer, skeleton, *refs):
    near_list, near_count, packed, stack, tiles = refs[:5]
    bases, moves, skeletons, lists, counts, sems = refs[5:]
    dim, rank = skeletons.shape[1:]
    width = bases.shape[2]
    vecs = vectors.shape[0]
    held = stack.at[dim:]
    pairs = [(near_list, lists), (near_count, counts), (vectors, held), (basis, bases)]
    pairs += [(transfer, moves), (skeleton, skeletons), (points, stack.at[:dim])]
    loads = [pltpu.make_async_copy(src, dst, sems.at[at]) for at, (src, dst) in enumerate(pairs)]
    for load in loads:
        load.start()
    for load in loads[:2]:
        load.wait()
    if share:
        share_tiles(lists, counts, leaves, tiles)
    else:
        tiles[0] = jnp.int32(0)
    for load in loads[2:]:
        load.wait()
    lift = 0.0
    for leaf in range(leaves):
        lanes = slice(leaf * rank, (leaf + 1) * rank)
        coef = product(held[:, leaf * width : (leaf + 1) * width], bases[leaf], NT)
        packed[0:dim, lanes] = skeletons[leaf]
        packed[dim : dim + vecs, lanes] = coef
        lift = lift + product(coef, moves[leaf])
    rows = vecs // leaves
    for piece in range(leaves):
        packed[dim + vecs :, piece * rank : (piece + 1) * rank] = lift[
            piece * rows : (piece + 1) * rows
        ]


def coefficients(share, lists, points, vectors, basis, transfer, skeleton):
    leaves, dim, rank = skeleton.shape
    vecs = vectors.shape[0]
    inputs = [
        pltpu.with_memory_space_constraint(x, pltpu.HBM)
        for x in (points, vectors, basis, transfer, skeleton, *lists)
    ]
    return pl.pallas_call(
        functools.partial(coef_kernel, leaves, share),
        out_shape=[
            jax.ShapeDtypeStruct((dim + vecs + vecs // leaves, leaves * rank), F32),
            jax.ShapeDtypeStruct((dim + vecs, vectors.shape[1]), F32),
            jax.ShapeDtypeStruct((HEAD + 4 * leaves * lists[0].shape[1],), jnp.int32),
        ],
        in_specs=[HBM] * 7,
        out_specs=[VMEM, VMEM, SMEM],
        scratch_shapes=[pltpu.VMEM(x.shape, F32) for x in (basis, transfer, skeleton)]
        + [pltpu.SMEM(x.shape, jnp.int32) for x in lists]
        + [pltpu.SemaphoreType.DMA((7,))],
        compiler_params=PARAMS,
        cost_estimate=lasts(0.5),
        name="coefficients",
    )(*inputs)


def write_source(points, vectors, left, coefs):
    vecs = vectors.shape[0]
    left[...] = source_rows(points)
    high, low = split2(vectors * damping(points))
    coefs[0:vecs] = high
    coefs[vecs:] = low


def write_target(points, right, scale):
    right[...] = target_columns(points)
    scale[...] = damping(points) * points.shape[1] ** -0.5


def leaf_of(stack, dim, width, leaf):
    span = slice(leaf * width, (leaf + 1) * width)
    return stack[:dim, span], stack[dim:, span]


def prepare_kernel(dim, width, stack, left, coefs, right, scale):
    for leaf in range(stack.shape[1] // width):
        points, vectors = leaf_of(stack, dim, width, leaf)
        write_source(points, vectors, left.at[leaf], coefs.at[leaf])
        write_target(points, right.at[leaf], scale.at[leaf])


def source_shapes(sources, dim, vecs, width):
    return [
        jax.ShapeDtypeStruct((sources, width, 6 * dim), BF16),
        jax.ShapeDtypeStruct((sources, 2 * vecs, width), BF16),
    ]


def target_shapes(targets, dim, width):
    return [
        jax.ShapeDtypeStruct((targets, 6 * dim, width), BF16),
        jax.ShapeDtypeStruct((targets, 1, width), F32),
    ]


def prepare(stack, dim, width):
    vecs = stack.shape[0] - dim
    count = stack.shape[1] // width
    return pl.pallas_call(
        functools.partial(prepare_kernel, dim, width),
        out_shape=source_shapes(count, dim, vecs, width) + target_shapes(count, dim, width),
        in_specs=[VMEM],
        out_specs=[VMEM] * 4,
        compiler_params=PARAMS,
        cost_estimate=lasts(0.5),
        name="prepare",
    )(stack)


def run_tiles(todo, pick, left, coefs, right, right_base, totals, totals_base):
    vecs, width = totals.shape[1:]
    chunks = [(y, x) for y in range(0, width, COLUMNS) for x in range(0, width, ROWS)]

    def tile(step, carry):
        slot, source = pick(step)

        def exponent(y, x):
            return mxu(left[source, x : x + ROWS], right[right_base + slot, :, y : y + COLUMNS])

        ahead = exponent(*chunks[0])
        for at, (y, x) in enumerate(chunks):
            power = ahead
            if at + 1 < len(chunks):
                ahead = exponent(*chunks[at + 1])
            high, low = split2(jnp.exp2(power))
            both = coefs[source, :, x : x + ROWS]
            top = mxu(both, high)
            found = top[:vecs] + (top[vecs:] + mxu(both[:vecs], low))
            strip = found if x == 0 else strip + found
            if x + ROWS == width:
                totals[totals_base + slot, :, y : y + COLUMNS] += strip
        return carry

    lax.fori_loop(*todo, tile, 0)


def listed(work, start, sources):
    return lambda step: (work[start + step] // sources, work[start + step] % sources)


def self_kernel(dim, stack, left, coefs, right, scale, totals):
    leaves, _, width = totals.shape
    prepare_kernel(dim, width, stack, left, coefs, right, scale)
    totals[...] = jnp.zeros(totals.shape, F32)
    run_tiles((0, leaves), lambda step: (step, step), left, coefs, right, 0, totals, 0)


def with_self(stack, dim, leaves):
    vecs = stack.shape[0] - dim
    width = stack.shape[1] // leaves
    return pl.pallas_call(
        functools.partial(self_kernel, dim),
        out_shape=source_shapes(leaves, dim, vecs, width)
        + target_shapes(leaves, dim, width)
        + [jax.ShapeDtypeStruct((leaves, vecs, width), F32)],
        in_specs=[VMEM],
        out_specs=[VMEM] * 5,
        compiler_params=PARAMS,
        cost_estimate=lasts(0.5),
        name="near_self",
    )(stack)


def local_kernel(leaves, dim, tiles, twin_stack, *refs):
    own_left, own_coefs, own_right, own_totals = refs[:4]
    right, scale, totals, left, coefs = refs[4:]
    many, _, width = totals.shape
    core = lax.axis_index("sub") % 2
    own, twin = core * leaves, (1 - core) * leaves
    for leaf in range(leaves):
        left[own + leaf] = own_left[leaf]
        coefs[own + leaf] = own_coefs[leaf]
        right[own + leaf] = own_right[leaf]
        totals[own + leaf] = own_totals[leaf]
        totals[twin + leaf] = jnp.zeros(totals.shape[1:], F32)
        points, vectors = leaf_of(twin_stack, dim, width, leaf)
        write_source(points, vectors, left.at[twin + leaf], coefs.at[twin + leaf])
        write_target(points, right.at[twin + leaf], scale.at[leaf])
    run_tiles((0, tiles[3]), walk(tiles, many), left, coefs, right, 0, totals, 0)


def tiles_local(tiles, twin, own, leaves):
    left, coefs, right, _, totals = own
    vecs, width = totals.shape[1:]
    dim = twin.shape[0] - vecs
    many = 2 * leaves
    return pl.pallas_call(
        functools.partial(local_kernel, leaves, dim),
        out_shape=[
            jax.ShapeDtypeStruct((many, 6 * dim, width), BF16),
            jax.ShapeDtypeStruct((leaves, 1, width), F32),
            jax.ShapeDtypeStruct((many, vecs, width), F32),
        ]
        + source_shapes(many, dim, vecs, width),
        in_specs=[SMEM] + [VMEM] * 5,
        out_specs=[VMEM] * 5,
        compiler_params=PARAMS,
        cost_estimate=lasts(0.5),
        name="near_local",
    )(tiles, twin, left, coefs, right, totals)


def cross_kernel(leaves, dim, tiles, cross_stack, right, scale, begun, *refs):
    twin_out, left, coefs, own_totals, totals = refs
    many, _, width = totals.shape
    core = lax.axis_index("sub") % 2
    own, twin = core * leaves, (1 - core) * leaves
    for leaf in range(leaves):
        points, vectors = leaf_of(cross_stack, dim, width, leaf)
        write_source(points, vectors, left.at[leaf], coefs.at[leaf])
    totals[...] = begun[...]
    run_tiles((0, tiles[5]), walk_cross(tiles, leaves), left, coefs, right, 0, totals, 0)
    for leaf in range(leaves):
        twin_out[:, leaf * width : (leaf + 1) * width] = totals[twin + leaf] * scale[leaf]
        own_totals[leaf] = totals[own + leaf]


def tiles_cross(tiles, cross, right, scale, begun):
    many, vecs, width = begun.shape
    leaves = many // 2
    dim = cross.shape[0] - vecs
    return pl.pallas_call(
        functools.partial(cross_kernel, leaves, dim),
        out_shape=[jax.ShapeDtypeStruct((vecs, leaves * width), F32)]
        + source_shapes(leaves, dim, vecs, width)
        + [jax.ShapeDtypeStruct((leaves, vecs, width), F32)],
        in_specs=[SMEM] + [VMEM] * 4,
        out_specs=[VMEM] * 4,
        scratch_shapes=[pltpu.VMEM((many, vecs, width), F32)],
        compiler_params=PARAMS,
        cost_estimate=lasts(0.5),
        name="near_cross",
    )(tiles, cross, right, scale, begun)


def after_kernel(leaves, tiles, left, coefs, cross_left, cross_coefs, right, scale, begun, *refs):
    out, totals = refs
    width = totals.shape[2]
    own = lax.axis_index("sub") % 2 * leaves
    totals[...] = begun[...]

    def own_place(pick):
        def picked(step):
            place, source = pick(step)
            return place - own, source

        return picked

    local, cross = own_place(walk(tiles, 2 * leaves)), own_place(walk_cross(tiles, leaves))
    run_tiles((tiles[3], tiles[4]), local, left, coefs, right, 0, totals, 0)
    run_tiles((tiles[5], tiles[6]), cross, cross_left, cross_coefs, right, 0, totals, 0)
    for leaf in range(leaves):
        out[:, leaf * width : (leaf + 1) * width] = totals[leaf] * scale[leaf]


def tiles_after(tiles, local, cross, right, scale, begun):
    leaves, vecs, width = begun.shape
    return pl.pallas_call(
        functools.partial(after_kernel, leaves),
        out_shape=jax.ShapeDtypeStruct((vecs, leaves * width), F32),
        in_specs=[SMEM] + [VMEM] * 7,
        out_specs=VMEM,
        scratch_shapes=[pltpu.VMEM((leaves, vecs, width), F32)],
        compiler_params=PARAMS,
        cost_estimate=lasts(0.5),
        name="near_after",
    )(tiles, *local, *cross, right, scale, begun)


def list_tiles(near_list, near_count, leaves, target, source_base, sources, work):
    first = lax.axis_index("leaf") * near_list.shape[0]
    pair_size, pair_at = lax.axis_size("pair"), lax.axis_index("pair")
    todo = jnp.int32(0)
    for leaf in range(leaves):
        place = target * leaves + leaf
        limit = near_count[place]
        for turn in range(near_list.shape[1]):
            source = near_list[place, turn] - first - source_base
            wanted = (turn < limit) & (source >= 0) & (source < sources)
            if pair_size > 1:
                wanted = wanted & (pair_at == turn % pair_size)
            work[todo] = leaf * sources + source
            todo = todo + wanted.astype(jnp.int32)
    return todo


def subtree_kernel(leaves, near_list, near_count, left, coefs, right, scale, out, totals, work):
    me = lax.axis_index("sub")
    vecs, width = totals.shape[1:]
    sources = left.shape[0]
    todo = list_tiles(near_list, near_count, leaves, me, 0, sources, work)
    totals[...] = jnp.zeros(totals.shape, F32)
    run_tiles((0, todo), listed(work, 0, sources), left, coefs, right, me * leaves, totals, 0)
    for leaf in range(leaves):
        out[:, leaf * width : (leaf + 1) * width] = totals[leaf] * scale[me * leaves + leaf]


def from_subtree(lists, factors, leaves):
    near_list, near_count = lists
    vecs, width = factors[1].shape[1] // 2, factors[1].shape[2]
    return pl.pallas_call(
        functools.partial(subtree_kernel, leaves),
        out_shape=jax.ShapeDtypeStruct((vecs, leaves * width), F32),
        in_specs=[SMEM, SMEM] + [VMEM] * 4,
        out_specs=VMEM,
        scratch_shapes=[
            pltpu.VMEM((leaves, vecs, width), F32),
            pltpu.SMEM((leaves * near_list.shape[1] + 1,), jnp.int32),
        ],
        compiler_params=PARAMS,
        name="near_subtree",
    )(near_list, near_count, *factors)


def interact(source, coefs, target):
    kernel = jnp.exp2(mxu(source_rows(source), target_columns(target)))
    return product(coefs * damping(source), kernel) * damping(target)


def far_kernel(place_of, leaves, subs, nears, far_list, parent_far, *refs):
    refs, (skeleton, parent_skel, transfer, basis, out) = refs[:-5], refs[-5:]
    near, gathered = refs[:nears], refs[nears:]
    dim, rank = skeleton.shape[1:]
    width = basis.shape[2]
    vecs = out.shape[0]

    def block(device):
        which, *index = place_of(device)
        found = gathered[0][tuple(index)]
        for other in range(1, len(gathered)):
            found = jnp.where(which == other, gathered[other][tuple(index)], found)
        return found

    def lanes(data, at):
        found = data[:, :rank]
        for other in range(1, leaves):
            found = jnp.where(at == other, data[:, other * rank : (other + 1) * rank], found)
        return found

    points, coefs = [], []
    for turn in range(parent_far.shape[1]):
        parent = parent_far[0, turn]
        lift = block(parent * subs)[dim + vecs :]
        for sub in range(1, subs):
            lift = lift + block(parent * subs + sub)[dim + vecs :]
        coefs.append(
            jnp.concatenate([lift[:, at * rank : (at + 1) * rank] for at in range(leaves)], axis=0)
        )
        points.append(parent_skel[parent])
    own = parent_skel[lax.axis_index("leaf")]
    upper = interact(
        jnp.concatenate(points, axis=1), jnp.concatenate(coefs, axis=1), own
    ) * (rank**-0.5)

    for leaf in range(leaves):
        points, coefs = [], []
        for turn in range(far_list.shape[1]):
            partner = far_list[leaf, turn]
            data = lanes(block(partner // leaves), partner % leaves)
            points.append(data[:dim])
            coefs.append(data[dim : dim + vecs])
        far = interact(
            jnp.concatenate(points, axis=1), jnp.concatenate(coefs, axis=1), skeleton[leaf]
        ) * (rank**-0.5)
        field = far + product(upper, transfer[leaf], NT)
        span = slice(leaf * width, (leaf + 1) * width)
        total = product(field, basis[leaf])
        for part in near:
            total = total + part[:, span]
        out[:, span] = total


def far_field(place_of, subs, far_list, parent_far, near, gathered, *held):
    skeleton, _, _, basis = held
    leaves, rank, width = basis.shape
    vecs = near[0].shape[0]
    return pl.pallas_call(
        functools.partial(far_kernel, place_of, leaves, subs, len(near)),
        out_shape=jax.ShapeDtypeStruct((vecs, leaves * width), F32),
        in_specs=[SMEM, SMEM] + [VMEM] * (len(near) + len(gathered) + 4),
        out_specs=VMEM,
        compiler_params=PARAMS,
        cost_estimate=lasts(0.5),
        name="far_field",
    )(far_list, parent_far, *near, *gathered, *held)


def swap(x, bit, axis="sub"):
    return lax.ppermute(x, axis, [(at, at ^ bit) for at in range(lax.axis_size(axis))])


def local(
    points,
    vectors,
    basis,
    transfer,
    skeleton,
    parent_skel,
    near_list,
    near_count,
    far_list,
    parent_far,
):
    leaves, _, width = basis.shape
    dim = points.shape[0]
    subs, groups = lax.axis_size("sub"), lax.axis_size("leaf")
    lists = (near_list, near_count)
    split = subs == 4 and lax.axis_size("pair") == 1 and groups in (4, 8, 16)
    packed, stack, tiles = coefficients(split, lists, points, vectors, basis, transfer, skeleton)
    if split:
        twin, cross = swap(stack, 1), swap(stack, 2)
        line = packed[None]
        for bit in range(groups.bit_length() - 1):
            arrived = swap(line, 1 << bit, "leaf")
            if bit == 0:
                own = with_self(stack, dim, leaves)
                arrived, own = lax.optimization_barrier((arrived, own))
            elif bit == 1:
                right, scale, begun, *inner = tiles_local(tiles, twin, own, leaves)
                arrived, begun = lax.optimization_barrier((arrived, begun))
            line = jnp.concatenate([line, arrived])
        beside = swap(line, 2)
        twin_near, *held, begun = tiles_cross(tiles, cross, right, scale, begun)
        back = swap(twin_near, 1)
        beside, twin_near = lax.optimization_barrier((beside, twin_near))
        plane = jnp.stack([line, beside])
        gathered = (plane, swap(plane, 1))
        near = (tiles_after(tiles, inner, held, *own[2:4], begun), back)

        def place_of(device):
            away = (device % subs) ^ lax.axis_index("sub")
            return away % 2, away // 2, (device // subs) ^ lax.axis_index("leaf")

    else:

        def place_of(device):
            return 0, device

        gathered = (lax.all_gather(packed, ("leaf", "sub")),)
        everyone = lax.all_gather(stack, "sub", axis=1, tiled=True)
        factors = prepare(everyone, dim, width)
        near = (lax.psum(from_subtree(lists, factors, leaves), "pair"),)

    return far_field(
        place_of, subs, far_list, parent_far, near, gathered, skeleton, parent_skel, transfer, basis
    )


def solution(mesh):
    placed = (
        P(None, ("groups", "leaf", "sub")),
        P(None, ("groups", "leaf", "sub")),
        P(("groups", "leaf", "sub"), None, None),
        P(("groups", "leaf", "sub"), None, None),
        P(("groups", "leaf", "sub"), None, None),
        P("groups", None, None),
        P(("groups", "leaf"), None),
        P(("groups", "leaf")),
        P(("groups", "leaf", "sub"), None),
        P(("groups", "leaf"), None),
    )
    return jax.shard_map(
        local,
        mesh=mesh,
        in_specs=placed,
        out_specs=P(None, ("groups", "leaf", "sub")),
        check_vma=False,
    )
```

```python
import functools
import math

import jax
import jax.numpy as jnp
from jax import lax
from jax.experimental import pallas as pl
from jax.experimental.pallas import tpu as pltpu
from jax.sharding import PartitionSpec as P

RATE = 0.125 * math.log2(math.e)
ROWS, COLUMNS = 512, 1024
F32, BF16 = jnp.float32, jnp.bfloat16
VMEM = pl.BlockSpec(memory_space=pltpu.VMEM)
HBM = pl.BlockSpec(memory_space=pltpu.HBM)
SMEM = pl.BlockSpec(memory_space=pltpu.SMEM)
PARAMS = pltpu.CompilerParams(vmem_limit_bytes=40 * 1024 * 1024)
NN, NT = (((1,), (0,)), ((), ())), (((1,), (1,)), ((), ()))


def lasts(microseconds):
    return pl.CostEstimate(
        flops=int(1e9 * microseconds), bytes_accessed=int(3e6 * microseconds), transcendentals=0
    )


def mxu(x, y, dims=NN):
    return lax.dot_general(x, y, dims, preferred_element_type=F32)


def split2(x):
    high = x.astype(BF16)
    return high, (x - high.astype(F32)).astype(BF16)


def split3(x):
    high = x.astype(BF16).astype(F32)
    rest = x - high
    middle = rest.astype(BF16).astype(F32)
    return high, middle, (rest - middle).astype(BF16).astype(F32)


def product(x, y, dims=NN):
    rows = x.shape[0]
    x1, x2 = split2(x)
    y1, y2 = split2(y)
    top = mxu(jnp.concatenate([x1, x2], axis=0), y1, dims)
    return top[:rows] + (top[rows:] + mxu(x1, y2, dims))


def source_rows(x):
    a1, a2, a3 = split3(x * (2.0 * RATE))
    return jnp.concatenate([a1, a1, a2, a2, a1, a3], axis=0).T.astype(BF16)


def target_columns(x):
    b1, b2, b3 = split3(x)
    return jnp.concatenate([b1, b2, b1, b2, b3, b1], axis=0).astype(BF16)


def damping(x):
    return jnp.exp2(-RATE * jnp.sum(x * x, axis=0, keepdims=True))


HEAD = 7


def share_tiles(near_list, near_count, leaves, tiles):
    turns = near_list.shape[1]
    me = lax.axis_index("sub")
    core = me % 2
    many = 2 * leaves
    first = lax.axis_index("leaf") * near_list.shape[0]
    base = me // 2 * many
    beside = (me ^ 2) * leaves
    cross_at = HEAD + many * turns
    zero = jnp.int32(0)
    local, cross, used_all, marks = zero, zero, zero, []
    for index in range(many):
        side = 1 - core if index < leaves else core
        place = side * leaves + index % leaves
        limit = near_count[base + place]
        used_all = used_all + limit - 1
        for turn in range(1, turns):
            source = near_list[base + place, turn] - first
            used = turn < limit
            near = source - base
            away = source - beside
            tiles[HEAD + local] = place * many + near
            tiles[cross_at + cross] = place * leaves + away
            local = local + (used & (near >= 0) & (near < many)).astype(jnp.int32)
            cross = cross + (used & (away >= 0) & (away < leaves)).astype(jnp.int32)
        if index == leaves - 1:
            marks = [local, cross]
    other = used_all - local - cross
    own_local, own_cross = local - marks[0], cross - marks[1]
    mine = jnp.clip((used_all + 1 - core) // 2 - cross, 0, local)
    total, twin_total = mine + cross, local - mine + other
    after = total - jnp.minimum(total, twin_total) + 1
    after_cross = jnp.clip(after, 0, own_cross)
    after_local = jnp.clip(after - after_cross, 0, jnp.minimum(mine, own_local))
    tiles[0] = jnp.where(core == 0, marks[0] + mine - 1, local - mine)
    tiles[1] = jnp.where(core == 0, -1, 1)
    tiles[2] = local
    tiles[3] = mine - after_local
    tiles[4] = mine
    tiles[5] = cross - after_cross
    tiles[6] = cross


def walk(tiles, many):
    def pick(step):
        at = tiles[0] + tiles[1] * step
        code = tiles[HEAD + jnp.where(at >= tiles[2], at - tiles[2], at)]
        return code // many, code % many

    return pick


def walk_cross(tiles, leaves):
    cross_at = HEAD + (tiles.shape[0] - HEAD) // 2

    def pick(step):
        code = tiles[cross_at + step]
        return code // leaves, code % leaves

    return pick


def coef_kernel(leaves, share, points, vectors, basis, transfer, skeleton, *refs):
    near_list, near_count, packed, stack, tiles = refs[:5]
    bases, moves, skeletons, lists, counts, sems = refs[5:]
    dim, rank = skeletons.shape[1:]
    width = bases.shape[2]
    vecs = vectors.shape[0]
    held = stack.at[dim:]
    pairs = [(near_list, lists), (near_count, counts), (vectors, held), (basis, bases)]
    pairs += [(transfer, moves), (skeleton, skeletons), (points, stack.at[:dim])]
    loads = [pltpu.make_async_copy(src, dst, sems.at[at]) for at, (src, dst) in enumerate(pairs)]
    for load in loads:
        load.start()
    for load in loads[:2]:
        load.wait()
    if share:
        share_tiles(lists, counts, leaves, tiles)
    else:
        tiles[0] = jnp.int32(0)
    for load in loads[2:]:
        load.wait()
    lift = 0.0
    for leaf in range(leaves):
        lanes = slice(leaf * rank, (leaf + 1) * rank)
        coef = product(held[:, leaf * width : (leaf + 1) * width], bases[leaf], NT)
        packed[0:dim, lanes] = skeletons[leaf]
        packed[dim : dim + vecs, lanes] = coef
        lift = lift + product(coef, moves[leaf])
    rows = vecs // leaves
    for piece in range(leaves):
        packed[dim + vecs :, piece * rank : (piece + 1) * rank] = lift[
            piece * rows : (piece + 1) * rows
        ]


def coefficients(share, lists, points, vectors, basis, transfer, skeleton):
    leaves, dim, rank = skeleton.shape
    vecs = vectors.shape[0]
    inputs = [
        pltpu.with_memory_space_constraint(x, pltpu.HBM)
        for x in (points, vectors, basis, transfer, skeleton, *lists)
    ]
    return pl.pallas_call(
        functools.partial(coef_kernel, leaves, share),
        out_shape=[
            jax.ShapeDtypeStruct((dim + vecs + vecs // leaves, leaves * rank), F32),
            jax.ShapeDtypeStruct((dim + vecs, vectors.shape[1]), F32),
            jax.ShapeDtypeStruct((HEAD + 4 * leaves * lists[0].shape[1],), jnp.int32),
        ],
        in_specs=[HBM] * 7,
        out_specs=[VMEM, VMEM, SMEM],
        scratch_shapes=[pltpu.VMEM(x.shape, F32) for x in (basis, transfer, skeleton)]
        + [pltpu.SMEM(x.shape, jnp.int32) for x in lists]
        + [pltpu.SemaphoreType.DMA((7,))],
        compiler_params=PARAMS,
        cost_estimate=lasts(0.5),
        name="coefficients",
    )(*inputs)


def write_source(points, vectors, left, coefs):
    vecs = vectors.shape[0]
    left[...] = source_rows(points)
    high, low = split2(vectors * damping(points))
    coefs[0:vecs] = high
    coefs[vecs:] = low


def write_target(points, right, scale):
    right[...] = target_columns(points)
    scale[...] = damping(points) * points.shape[1] ** -0.5


def leaf_of(stack, dim, width, leaf):
    span = slice(leaf * width, (leaf + 1) * width)
    return stack[:dim, span], stack[dim:, span]


def prepare_kernel(dim, width, stack, left, coefs, right, scale):
    for leaf in range(stack.shape[1] // width):
        points, vectors = leaf_of(stack, dim, width, leaf)
        write_source(points, vectors, left.at[leaf], coefs.at[leaf])
        write_target(points, right.at[leaf], scale.at[leaf])


def source_shapes(sources, dim, vecs, width):
    return [
        jax.ShapeDtypeStruct((sources, width, 6 * dim), BF16),
        jax.ShapeDtypeStruct((sources, 2 * vecs, width), BF16),
    ]


def target_shapes(targets, dim, width):
    return [
        jax.ShapeDtypeStruct((targets, 6 * dim, width), BF16),
        jax.ShapeDtypeStruct((targets, 1, width), F32),
    ]


def prepare(stack, dim, width):
    vecs = stack.shape[0] - dim
    count = stack.shape[1] // width
    return pl.pallas_call(
        functools.partial(prepare_kernel, dim, width),
        out_shape=source_shapes(count, dim, vecs, width) + target_shapes(count, dim, width),
        in_specs=[VMEM],
        out_specs=[VMEM] * 4,
        compiler_params=PARAMS,
        cost_estimate=lasts(0.5),
        name="prepare",
    )(stack)


def run_tiles(todo, pick, left, coefs, right, right_base, totals, totals_base):
    vecs, width = totals.shape[1:]
    chunks = [(y, x) for y in range(0, width, COLUMNS) for x in range(0, width, ROWS)]

    def tile(step, carry):
        slot, source = pick(step)

        def exponent(y, x):
            return mxu(left[source, x : x + ROWS], right[right_base + slot, :, y : y + COLUMNS])

        ahead = exponent(*chunks[0])
        for at, (y, x) in enumerate(chunks):
            power = ahead
            if at + 1 < len(chunks):
                ahead = exponent(*chunks[at + 1])
            high, low = split2(jnp.exp2(power))
            both = coefs[source, :, x : x + ROWS]
            top = mxu(both, high)
            found = top[:vecs] + (top[vecs:] + mxu(both[:vecs], low))
            strip = found if x == 0 else strip + found
            if x + ROWS == width:
                totals[totals_base + slot, :, y : y + COLUMNS] += strip
        return carry

    lax.fori_loop(*todo, tile, 0)


def listed(work, start, sources):
    return lambda step: (work[start + step] // sources, work[start + step] % sources)


def self_kernel(dim, stack, left, coefs, right, scale, totals):
    leaves, _, width = totals.shape
    prepare_kernel(dim, width, stack, left, coefs, right, scale)
    totals[...] = jnp.zeros(totals.shape, F32)
    run_tiles((0, 1), lambda step: (step, step), left, coefs, right, 0, totals, 0)


def with_self(stack, dim, leaves):
    vecs = stack.shape[0] - dim
    width = stack.shape[1] // leaves
    return pl.pallas_call(
        functools.partial(self_kernel, dim),
        out_shape=source_shapes(leaves, dim, vecs, width)
        + target_shapes(leaves, dim, width)
        + [jax.ShapeDtypeStruct((leaves, vecs, width), F32)],
        in_specs=[VMEM],
        out_specs=[VMEM] * 5,
        compiler_params=PARAMS,
        cost_estimate=lasts(0.5),
        name="near_self",
    )(stack)


def twin_kernel(leaves, dim, twin_stack, *refs):
    own_left, own_coefs, own_right, own_totals = refs[:4]
    right, scale, totals, left, coefs = refs[4:]
    width = totals.shape[2]
    core = lax.axis_index("sub") % 2
    own, twin = core * leaves, (1 - core) * leaves
    for leaf in range(leaves):
        left[own + leaf] = own_left[leaf]
        coefs[own + leaf] = own_coefs[leaf]
        right[own + leaf] = own_right[leaf]
        totals[own + leaf] = own_totals[leaf]
        totals[twin + leaf] = jnp.zeros(totals.shape[1:], F32)
        points, vectors = leaf_of(twin_stack, dim, width, leaf)
        write_source(points, vectors, left.at[twin + leaf], coefs.at[twin + leaf])
        write_target(points, right.at[twin + leaf], scale.at[leaf])
    run_tiles((own + 1, own + leaves), lambda at: (at, at), left, coefs, right, 0, totals, 0)


def with_twin(twin, own):
    left, coefs, right, _, totals = own
    leaves, vecs, width = totals.shape
    dim = twin.shape[0] - vecs
    many = 2 * leaves
    return pl.pallas_call(
        functools.partial(twin_kernel, leaves, dim),
        out_shape=[
            jax.ShapeDtypeStruct((many, 6 * dim, width), BF16),
            jax.ShapeDtypeStruct((leaves, 1, width), F32),
            jax.ShapeDtypeStruct((many, vecs, width), F32),
        ]
        + source_shapes(many, dim, vecs, width),
        in_specs=[VMEM] * 5,
        out_specs=[VMEM] * 5,
        compiler_params=PARAMS,
        cost_estimate=lasts(0.5),
        name="near_twin",
    )(twin, left, coefs, right, totals)


def local_kernel(tiles, left, coefs, right, begun, totals):
    totals[...] = begun[...]
    run_tiles((0, tiles[3]), walk(tiles, totals.shape[0]), left, coefs, right, 0, totals, 0)


def tiles_local(tiles, left, coefs, right, begun):
    return pl.pallas_call(
        local_kernel,
        out_shape=jax.ShapeDtypeStruct(begun.shape, F32),
        in_specs=[SMEM] + [VMEM] * 4,
        out_specs=VMEM,
        compiler_params=PARAMS,
        cost_estimate=lasts(0.5),
        name="near_local",
    )(tiles, left, coefs, right, begun)


def cross_kernel(leaves, dim, tiles, cross_stack, right, scale, begun, *refs):
    twin_out, left, coefs, own_totals, totals = refs
    many, _, width = totals.shape
    core = lax.axis_index("sub") % 2
    own, twin = core * leaves, (1 - core) * leaves
    for leaf in range(leaves):
        points, vectors = leaf_of(cross_stack, dim, width, leaf)
        write_source(points, vectors, left.at[leaf], coefs.at[leaf])
    totals[...] = begun[...]
    run_tiles((0, tiles[5]), walk_cross(tiles, leaves), left, coefs, right, 0, totals, 0)
    for leaf in range(leaves):
        twin_out[:, leaf * width : (leaf + 1) * width] = totals[twin + leaf] * scale[leaf]
        own_totals[leaf] = totals[own + leaf]


def tiles_cross(tiles, cross, right, scale, begun):
    many, vecs, width = begun.shape
    leaves = many // 2
    dim = cross.shape[0] - vecs
    return pl.pallas_call(
        functools.partial(cross_kernel, leaves, dim),
        out_shape=[jax.ShapeDtypeStruct((vecs, leaves * width), F32)]
        + source_shapes(leaves, dim, vecs, width)
        + [jax.ShapeDtypeStruct((leaves, vecs, width), F32)],
        in_specs=[SMEM] + [VMEM] * 4,
        out_specs=[VMEM] * 4,
        scratch_shapes=[pltpu.VMEM((many, vecs, width), F32)],
        compiler_params=PARAMS,
        cost_estimate=lasts(0.5),
        name="near_cross",
    )(tiles, cross, right, scale, begun)


def after_kernel(leaves, tiles, left, coefs, cross_left, cross_coefs, right, scale, begun, *refs):
    out, totals = refs
    width = totals.shape[2]
    own = lax.axis_index("sub") % 2 * leaves
    totals[...] = begun[...]

    def own_place(pick):
        def picked(step):
            place, source = pick(step)
            return place - own, source

        return picked

    local, cross = own_place(walk(tiles, 2 * leaves)), own_place(walk_cross(tiles, leaves))
    run_tiles((tiles[3], tiles[4]), local, left, coefs, right, 0, totals, 0)
    run_tiles((tiles[5], tiles[6]), cross, cross_left, cross_coefs, right, 0, totals, 0)
    for leaf in range(leaves):
        out[:, leaf * width : (leaf + 1) * width] = totals[leaf] * scale[leaf]


def tiles_after(tiles, local, cross, right, scale, begun):
    leaves, vecs, width = begun.shape
    return pl.pallas_call(
        functools.partial(after_kernel, leaves),
        out_shape=jax.ShapeDtypeStruct((vecs, leaves * width), F32),
        in_specs=[SMEM] + [VMEM] * 7,
        out_specs=VMEM,
        scratch_shapes=[pltpu.VMEM((leaves, vecs, width), F32)],
        compiler_params=PARAMS,
        cost_estimate=lasts(0.5),
        name="near_after",
    )(tiles, *local, *cross, right, scale, begun)


def list_tiles(near_list, near_count, leaves, target, source_base, sources, work):
    first = lax.axis_index("leaf") * near_list.shape[0]
    pair_size, pair_at = lax.axis_size("pair"), lax.axis_index("pair")
    todo = jnp.int32(0)
    for leaf in range(leaves):
        place = target * leaves + leaf
        limit = near_count[place]
        for turn in range(near_list.shape[1]):
            source = near_list[place, turn] - first - source_base
            wanted = (turn < limit) & (source >= 0) & (source < sources)
            if pair_size > 1:
                wanted = wanted & (pair_at == turn % pair_size)
            work[todo] = leaf * sources + source
            todo = todo + wanted.astype(jnp.int32)
    return todo


def subtree_kernel(leaves, near_list, near_count, left, coefs, right, scale, out, totals, work):
    me = lax.axis_index("sub")
    vecs, width = totals.shape[1:]
    sources = left.shape[0]
    todo = list_tiles(near_list, near_count, leaves, me, 0, sources, work)
    totals[...] = jnp.zeros(totals.shape, F32)
    run_tiles((0, todo), listed(work, 0, sources), left, coefs, right, me * leaves, totals, 0)
    for leaf in range(leaves):
        out[:, leaf * width : (leaf + 1) * width] = totals[leaf] * scale[me * leaves + leaf]


def from_subtree(lists, factors, leaves):
    near_list, near_count = lists
    vecs, width = factors[1].shape[1] // 2, factors[1].shape[2]
    return pl.pallas_call(
        functools.partial(subtree_kernel, leaves),
        out_shape=jax.ShapeDtypeStruct((vecs, leaves * width), F32),
        in_specs=[SMEM, SMEM] + [VMEM] * 4,
        out_specs=VMEM,
        scratch_shapes=[
            pltpu.VMEM((leaves, vecs, width), F32),
            pltpu.SMEM((leaves * near_list.shape[1] + 1,), jnp.int32),
        ],
        compiler_params=PARAMS,
        name="near_subtree",
    )(near_list, near_count, *factors)


def interact(source, coefs, target):
    kernel = jnp.exp2(mxu(source_rows(source), target_columns(target)))
    return product(coefs * damping(source), kernel) * damping(target)


def far_kernel(place_of, leaves, subs, nears, far_list, parent_far, *refs):
    refs, (skeleton, parent_skel, transfer, basis, out) = refs[:-5], refs[-5:]
    near, gathered = refs[:nears], refs[nears:]
    dim, rank = skeleton.shape[1:]
    width = basis.shape[2]
    vecs = out.shape[0]

    def block(device):
        which, *index = place_of(device)
        found = gathered[0][tuple(index)]
        for other in range(1, len(gathered)):
            found = jnp.where(which == other, gathered[other][tuple(index)], found)
        return found

    def lanes(data, at):
        found = data[:, :rank]
        for other in range(1, leaves):
            found = jnp.where(at == other, data[:, other * rank : (other + 1) * rank], found)
        return found

    points, coefs = [], []
    for turn in range(parent_far.shape[1]):
        parent = parent_far[0, turn]
        lift = block(parent * subs)[dim + vecs :]
        for sub in range(1, subs):
            lift = lift + block(parent * subs + sub)[dim + vecs :]
        coefs.append(
            jnp.concatenate([lift[:, at * rank : (at + 1) * rank] for at in range(leaves)], axis=0)
        )
        points.append(parent_skel[parent])
    own = parent_skel[lax.axis_index("leaf")]
    upper = interact(
        jnp.concatenate(points, axis=1), jnp.concatenate(coefs, axis=1), own
    ) * (rank**-0.5)

    for leaf in range(leaves):
        points, coefs = [], []
        for turn in range(far_list.shape[1]):
            partner = far_list[leaf, turn]
            data = lanes(block(partner // leaves), partner % leaves)
            points.append(data[:dim])
            coefs.append(data[dim : dim + vecs])
        far = interact(
            jnp.concatenate(points, axis=1), jnp.concatenate(coefs, axis=1), skeleton[leaf]
        ) * (rank**-0.5)
        field = far + product(upper, transfer[leaf], NT)
        span = slice(leaf * width, (leaf + 1) * width)
        total = product(field, basis[leaf])
        for part in near:
            total = total + part[:, span]
        out[:, span] = total


def far_field(place_of, subs, far_list, parent_far, near, gathered, *held):
    skeleton, _, _, basis = held
    leaves, rank, width = basis.shape
    vecs = near[0].shape[0]
    return pl.pallas_call(
        functools.partial(far_kernel, place_of, leaves, subs, len(near)),
        out_shape=jax.ShapeDtypeStruct((vecs, leaves * width), F32),
        in_specs=[SMEM, SMEM] + [VMEM] * (len(near) + len(gathered) + 4),
        out_specs=VMEM,
        compiler_params=PARAMS,
        cost_estimate=lasts(0.5),
        name="far_field",
    )(far_list, parent_far, *near, *gathered, *held)


def swap(x, bit, axis="sub"):
    return lax.ppermute(x, axis, [(at, at ^ bit) for at in range(lax.axis_size(axis))])


def local(
    points,
    vectors,
    basis,
    transfer,
    skeleton,
    parent_skel,
    near_list,
    near_count,
    far_list,
    parent_far,
):
    leaves, _, width = basis.shape
    dim = points.shape[0]
    subs, groups = lax.axis_size("sub"), lax.axis_size("leaf")
    lists = (near_list, near_count)
    split = subs == 4 and lax.axis_size("pair") == 1 and groups in (4, 8, 16)
    packed, stack, tiles = coefficients(split, lists, points, vectors, basis, transfer, skeleton)
    if split:
        twin, cross = swap(stack, 1), swap(stack, 2)
        line = packed[None]
        for bit in range(groups.bit_length() - 1):
            arrived = swap(line, 1 << bit, "leaf")
            if bit == 0:
                own = with_self(stack, dim, leaves)
                arrived, own = lax.optimization_barrier((arrived, own))
            elif bit == 1:
                right, scale, begun, *inner = with_twin(twin, own)
                arrived, begun = lax.optimization_barrier((arrived, begun))
            line = jnp.concatenate([line, arrived])
        beside = swap(line, 2)
        begun = tiles_local(tiles, *inner, right, begun)
        twin_near, *held, begun = tiles_cross(tiles, cross, right, scale, begun)
        back = swap(twin_near, 1)
        beside, twin_near = lax.optimization_barrier((beside, twin_near))
        plane = jnp.stack([line, beside])
        gathered = (plane, swap(plane, 1))
        near = (tiles_after(tiles, inner, held, *own[2:4], begun), back)

        def place_of(device):
            away = (device % subs) ^ lax.axis_index("sub")
            return away % 2, away // 2, (device // subs) ^ lax.axis_index("leaf")

    else:

        def place_of(device):
            return 0, device

        gathered = (lax.all_gather(packed, ("leaf", "sub")),)
        everyone = lax.all_gather(stack, "sub", axis=1, tiled=True)
        factors = prepare(everyone, dim, width)
        near = (lax.psum(from_subtree(lists, factors, leaves), "pair"),)

    return far_field(
        place_of, subs, far_list, parent_far, near, gathered, skeleton, parent_skel, transfer, basis
    )


def solution(mesh):
    placed = (
        P(None, ("groups", "leaf", "sub")),
        P(None, ("groups", "leaf", "sub")),
        P(("groups", "leaf", "sub"), None, None),
        P(("groups", "leaf", "sub"), None, None),
        P(("groups", "leaf", "sub"), None, None),
        P("groups", None, None),
        P(("groups", "leaf"), None),
        P(("groups", "leaf")),
        P(("groups", "leaf", "sub"), None),
        P(("groups", "leaf"), None),
    )
    return jax.shard_map(
        local,
        mesh=mesh,
        in_specs=placed,
        out_specs=P(None, ("groups", "leaf", "sub")),
        check_vma=False,
    )
```

```python
import functools
import math

import jax
import jax.numpy as jnp
from jax import lax
from jax.experimental import pallas as pl
from jax.experimental.pallas import tpu as pltpu
from jax.sharding import PartitionSpec as P

RATE = 0.125 * math.log2(math.e)
ROWS, COLUMNS = 256, 1024
F32, BF16 = jnp.float32, jnp.bfloat16
VMEM = pl.BlockSpec(memory_space=pltpu.VMEM)
ANY = pl.BlockSpec(memory_space=pl.ANY)
HBM = pl.BlockSpec(memory_space=pltpu.HBM)
SMEM = pl.BlockSpec(memory_space=pltpu.SMEM)
PARAMS = pltpu.CompilerParams(vmem_limit_bytes=40 * 1024 * 1024)
NN, NT = (((1,), (0,)), ((), ())), (((1,), (1,)), ((), ()))


def lasts(microseconds):
    return pl.CostEstimate(
        flops=int(1e9 * microseconds), bytes_accessed=int(3e6 * microseconds), transcendentals=0
    )


def mxu(x, y, dims=NN):
    return lax.dot_general(x, y, dims, preferred_element_type=F32)


def split2(x):
    high = x.astype(BF16)
    return high, (x - high.astype(F32)).astype(BF16)


def split3(x):
    high = x.astype(BF16).astype(F32)
    rest = x - high
    middle = rest.astype(BF16).astype(F32)
    return high, middle, (rest - middle).astype(BF16).astype(F32)


def product(x, y, dims=NN):
    rows = x.shape[0]
    x1, x2 = split2(x)
    y1, y2 = split2(y)
    top = mxu(jnp.concatenate([x1, x2], axis=0), y1, dims)
    return top[:rows] + (top[rows:] + mxu(x1, y2, dims))


def source_rows(x):
    a1, a2, a3 = split3(x * (2.0 * RATE))
    return jnp.concatenate([a1, a1, a2, a2, a1, a3], axis=0).T.astype(BF16)


def target_columns(x):
    b1, b2, b3 = split3(x)
    return jnp.concatenate([b1, b2, b1, b2, b3, b1], axis=0).astype(BF16)


def damping(x):
    return jnp.exp2(-RATE * jnp.sum(x * x, axis=0, keepdims=True))


HEAD = 7
EARLY = 2


def share_tiles(near_list, near_count, leaves, tiles):
    turns = near_list.shape[1]
    me = lax.axis_index("sub")
    core = me % 2
    many = 2 * leaves
    first = lax.axis_index("leaf") * near_list.shape[0]
    base = me // 2 * many
    beside = (me ^ 2) * leaves
    cross_at = HEAD + many * turns
    zero = jnp.int32(0)
    local, cross, used_all, marks = zero, zero, zero, []
    for index in range(many):
        side = 1 - core if index < leaves else core
        place = side * leaves + index % leaves
        limit = near_count[base + place]
        used_all = used_all + limit - 1
        for turn in range(1, turns):
            source = near_list[base + place, turn] - first
            used = turn < limit
            near = source - base
            away = source - beside
            tiles[HEAD + local] = place * many + near
            tiles[cross_at + cross] = place * leaves + away
            local = local + (used & (near >= 0) & (near < many)).astype(jnp.int32)
            cross = cross + (used & (away >= 0) & (away < leaves)).astype(jnp.int32)
        if index == leaves - 1:
            marks = [local, cross]
    other = used_all - local - cross
    own_local, own_cross = local - marks[0], cross - marks[1]
    mine = jnp.clip((used_all + 1 - core) // 2 - cross, 0, local)
    total, twin_total = mine + cross, local - mine + other
    after = total - jnp.minimum(total, twin_total) + 1
    after_cross = jnp.clip(after, 0, own_cross)
    after_local = jnp.clip(after - after_cross, 0, jnp.minimum(mine, own_local))
    tiles[0] = jnp.where(core == 0, marks[0] + mine - 1, local - mine)
    tiles[1] = jnp.where(core == 0, -1, 1)
    tiles[2] = local
    tiles[3] = mine - after_local
    tiles[4] = mine
    tiles[5] = cross - after_cross
    tiles[6] = cross


def walk(tiles, many):
    def pick(step):
        at = tiles[0] + tiles[1] * step
        code = tiles[HEAD + jnp.where(at >= tiles[2], at - tiles[2], at)]
        return code // many, code % many

    return pick


def walk_cross(tiles, leaves):
    cross_at = HEAD + (tiles.shape[0] - HEAD) // 2

    def pick(step):
        code = tiles[cross_at + step]
        return code // leaves, code % leaves

    return pick


def coef_kernel(leaves, share, points, vectors, basis, transfer, skeleton, *refs):
    near_list, near_count, packed, stack, tiles = refs[:5]
    bases, moves, skeletons, lists, counts, sems = refs[5:]
    dim, rank = skeletons.shape[1:]
    width = bases.shape[2]
    vecs = vectors.shape[0]
    held = stack.at[dim:]
    pairs = [(near_list, lists), (near_count, counts), (vectors, held), (basis, bases)]
    pairs += [(transfer, moves), (skeleton, skeletons), (points, stack.at[:dim])]
    loads = [pltpu.make_async_copy(src, dst, sems.at[at]) for at, (src, dst) in enumerate(pairs)]
    for load in loads:
        load.start()
    for load in loads[:2]:
        load.wait()
    if share:
        share_tiles(lists, counts, leaves, tiles)
    else:
        tiles[0] = jnp.int32(0)
    for load in loads[2:]:
        load.wait()
    lift = 0.0
    for leaf in range(leaves):
        lanes = slice(leaf * rank, (leaf + 1) * rank)
        coef = product(held[:, leaf * width : (leaf + 1) * width], bases[leaf], NT)
        packed[0:dim, lanes] = skeletons[leaf]
        packed[dim : dim + vecs, lanes] = coef
        lift = lift + product(coef, moves[leaf])
    rows = vecs // leaves
    for piece in range(leaves):
        packed[dim + vecs :, piece * rank : (piece + 1) * rank] = lift[
            piece * rows : (piece + 1) * rows
        ]


def coefficients(share, lists, points, vectors, basis, transfer, skeleton):
    leaves, dim, rank = skeleton.shape
    vecs = vectors.shape[0]
    inputs = [
        pltpu.with_memory_space_constraint(x, pltpu.HBM)
        for x in (points, vectors, basis, transfer, skeleton, *lists)
    ]
    return pl.pallas_call(
        functools.partial(coef_kernel, leaves, share),
        out_shape=[
            jax.ShapeDtypeStruct((dim + vecs + vecs // leaves, leaves * rank), F32),
            jax.ShapeDtypeStruct((dim + vecs, vectors.shape[1]), F32),
            jax.ShapeDtypeStruct((HEAD + 4 * leaves * lists[0].shape[1],), jnp.int32),
        ],
        in_specs=[HBM] * 7,
        out_specs=[VMEM, VMEM, SMEM],
        scratch_shapes=[pltpu.VMEM(x.shape, F32) for x in (basis, transfer, skeleton)]
        + [pltpu.SMEM(x.shape, jnp.int32) for x in lists]
        + [pltpu.SemaphoreType.DMA((7,))],
        compiler_params=PARAMS,
        cost_estimate=lasts(0.5),
        name="coefficients",
    )(*inputs)


def write_source(points, vectors, left, coefs):
    vecs = vectors.shape[0]
    left[...] = source_rows(points)
    high, low = split2(vectors * damping(points))
    coefs[0:vecs] = high
    coefs[vecs:] = low


def write_target(points, right, scale):
    right[...] = target_columns(points)
    scale[...] = damping(points) * points.shape[1] ** -0.5


def leaf_of(stack, dim, width, leaf):
    span = slice(leaf * width, (leaf + 1) * width)
    return stack[:dim, span], stack[dim:, span]


def prepare_kernel(dim, width, stack, left, coefs, right, scale):
    for leaf in range(stack.shape[1] // width):
        points, vectors = leaf_of(stack, dim, width, leaf)
        write_source(points, vectors, left.at[leaf], coefs.at[leaf])
        write_target(points, right.at[leaf], scale.at[leaf])


def source_shapes(sources, dim, vecs, width):
    return [
        jax.ShapeDtypeStruct((sources, width, 6 * dim), BF16),
        jax.ShapeDtypeStruct((sources, 2 * vecs, width), BF16),
    ]


def target_shapes(targets, dim, width):
    return [
        jax.ShapeDtypeStruct((targets, 6 * dim, width), BF16),
        jax.ShapeDtypeStruct((targets, 1, width), F32),
    ]


def prepare(stack, dim, width):
    vecs = stack.shape[0] - dim
    count = stack.shape[1] // width
    return pl.pallas_call(
        functools.partial(prepare_kernel, dim, width),
        out_shape=source_shapes(count, dim, vecs, width) + target_shapes(count, dim, width),
        in_specs=[VMEM],
        out_specs=[VMEM] * 4,
        compiler_params=PARAMS,
        cost_estimate=lasts(0.5),
        name="prepare",
    )(stack)


def run_tiles(todo, pick, left, coefs, right, right_base, totals, totals_base):
    vecs, width = totals.shape[1:]
    chunks = [(y, x) for y in range(0, width, COLUMNS) for x in range(0, width, ROWS)]

    def tile(step, carry):
        slot, source = pick(step)

        def exponent(y, x):
            return mxu(left[source, x : x + ROWS], right[right_base + slot, :, y : y + COLUMNS])

        ahead = exponent(*chunks[0])
        for at, (y, x) in enumerate(chunks):
            power = ahead
            if at + 1 < len(chunks):
                ahead = exponent(*chunks[at + 1])
            high, low = split2(jnp.exp2(power))
            both = coefs[source, :, x : x + ROWS]
            top = mxu(both, high)
            found = top[:vecs] + (top[vecs:] + mxu(both[:vecs], low))
            strip = found if x == 0 else strip + found
            if x + ROWS == width:
                totals[totals_base + slot, :, y : y + COLUMNS] += strip
        return carry

    lax.fori_loop(*todo, tile, 0)


def listed(work, start, sources):
    return lambda step: (work[start + step] // sources, work[start + step] % sources)


def self_kernel(dim, stack, left, coefs, right, scale, totals):
    leaves, _, width = totals.shape
    prepare_kernel(dim, width, stack, left, coefs, right, scale)
    totals[...] = jnp.zeros(totals.shape, F32)
    run_tiles((0, leaves), lambda step: (step, step), left, coefs, right, 0, totals, 0)


def with_self(stack, dim, leaves):
    vecs = stack.shape[0] - dim
    width = stack.shape[1] // leaves
    return pl.pallas_call(
        functools.partial(self_kernel, dim),
        out_shape=source_shapes(leaves, dim, vecs, width)
        + target_shapes(leaves, dim, width)
        + [jax.ShapeDtypeStruct((leaves, vecs, width), F32)],
        in_specs=[VMEM],
        out_specs=[VMEM] * 5,
        compiler_params=PARAMS,
        cost_estimate=lasts(0.5),
        name="near_self",
    )(stack)


def fetch(tiles, held, sem):
    copy = pltpu.make_async_copy(tiles, held, sem)
    copy.start()
    return copy


def list_scratch(tiles):
    return [pltpu.SMEM(tiles.shape, jnp.int32), pltpu.SemaphoreType.DMA]


def local_kernel(leaves, dim, given_tiles, twin_stack, *refs):
    own_left, own_coefs, own_right, own_totals = refs[:4]
    right, scale, totals, left, coefs, tiles, sem = refs[4:]
    lists = fetch(given_tiles, tiles, sem)
    many, _, width = totals.shape
    core = lax.axis_index("sub") % 2
    own, twin = core * leaves, (1 - core) * leaves
    for leaf in range(leaves):
        left[own + leaf] = own_left[leaf]
        coefs[own + leaf] = own_coefs[leaf]
        right[own + leaf] = own_right[leaf]
        totals[own + leaf] = own_totals[leaf]
        totals[twin + leaf] = jnp.zeros(totals.shape[1:], F32)
        points, vectors = leaf_of(twin_stack, dim, width, leaf)
        write_source(points, vectors, left.at[twin + leaf], coefs.at[twin + leaf])
        write_target(points, right.at[twin + leaf], scale.at[leaf])
    lists.wait()
    stop = jnp.minimum(tiles[3], EARLY)
    run_tiles((0, stop), walk(tiles, many), left, coefs, right, 0, totals, 0)


def tiles_local(tiles, twin, own, leaves):
    left, coefs, right, _, totals = own
    vecs, width = totals.shape[1:]
    dim = twin.shape[0] - vecs
    many = 2 * leaves
    return pl.pallas_call(
        functools.partial(local_kernel, leaves, dim),
        out_shape=[
            jax.ShapeDtypeStruct((many, 6 * dim, width), BF16),
            jax.ShapeDtypeStruct((leaves, 1, width), F32),
            jax.ShapeDtypeStruct((many, vecs, width), F32),
        ]
        + source_shapes(many, dim, vecs, width),
        in_specs=[ANY] + [VMEM] * 5,
        out_specs=[VMEM] * 5,
        scratch_shapes=list_scratch(tiles),
        compiler_params=PARAMS,
        cost_estimate=lasts(0.5),
        name="near_local",
    )(tiles, twin, left, coefs, right, totals)


def cross_kernel(leaves, dim, given_tiles, cross_stack, right, scale, begun, *refs):
    local_left, local_coefs, twin_out, left, coefs, own_totals, totals, tiles, sem = refs
    lists = fetch(given_tiles, tiles, sem)
    many, _, width = totals.shape
    core = lax.axis_index("sub") % 2
    own, twin = core * leaves, (1 - core) * leaves
    for leaf in range(leaves):
        points, vectors = leaf_of(cross_stack, dim, width, leaf)
        write_source(points, vectors, left.at[leaf], coefs.at[leaf])
    totals[...] = begun[...]
    lists.wait()
    rest = (jnp.minimum(tiles[3], EARLY), tiles[3])
    run_tiles(rest, walk(tiles, many), local_left, local_coefs, right, 0, totals, 0)
    run_tiles((0, tiles[5]), walk_cross(tiles, leaves), left, coefs, right, 0, totals, 0)
    for leaf in range(leaves):
        twin_out[:, leaf * width : (leaf + 1) * width] = totals[twin + leaf] * scale[leaf]
        own_totals[leaf] = totals[own + leaf]


def tiles_cross(tiles, cross, right, scale, begun, inner):
    many, vecs, width = begun.shape
    leaves = many // 2
    dim = cross.shape[0] - vecs
    return pl.pallas_call(
        functools.partial(cross_kernel, leaves, dim),
        out_shape=[jax.ShapeDtypeStruct((vecs, leaves * width), F32)]
        + source_shapes(leaves, dim, vecs, width)
        + [jax.ShapeDtypeStruct((leaves, vecs, width), F32)],
        in_specs=[ANY] + [VMEM] * 6,
        out_specs=[VMEM] * 4,
        scratch_shapes=[pltpu.VMEM((many, vecs, width), F32)] + list_scratch(tiles),
        compiler_params=PARAMS,
        cost_estimate=lasts(0.5),
        name="near_cross",
    )(tiles, cross, right, scale, begun, *inner)


def after_kernel(leaves, given_tiles, left, coefs, cross_left, cross_coefs, *refs):
    right, scale, begun, out, totals, tiles, sem = refs
    lists = fetch(given_tiles, tiles, sem)
    width = totals.shape[2]
    own = lax.axis_index("sub") % 2 * leaves
    totals[...] = begun[...]

    def own_place(pick):
        def picked(step):
            place, source = pick(step)
            return place - own, source

        return picked

    lists.wait()
    local, cross = own_place(walk(tiles, 2 * leaves)), own_place(walk_cross(tiles, leaves))
    run_tiles((tiles[3], tiles[4]), local, left, coefs, right, 0, totals, 0)
    run_tiles((tiles[5], tiles[6]), cross, cross_left, cross_coefs, right, 0, totals, 0)
    for leaf in range(leaves):
        out[:, leaf * width : (leaf + 1) * width] = totals[leaf] * scale[leaf]


def tiles_after(tiles, local, cross, right, scale, begun):
    leaves, vecs, width = begun.shape
    return pl.pallas_call(
        functools.partial(after_kernel, leaves),
        out_shape=jax.ShapeDtypeStruct((vecs, leaves * width), F32),
        in_specs=[ANY] + [VMEM] * 7,
        out_specs=VMEM,
        scratch_shapes=[pltpu.VMEM((leaves, vecs, width), F32)] + list_scratch(tiles),
        compiler_params=PARAMS,
        cost_estimate=lasts(0.5),
        name="near_after",
    )(tiles, *local, *cross, right, scale, begun)


def list_tiles(near_list, near_count, leaves, target, source_base, sources, work):
    first = lax.axis_index("leaf") * near_list.shape[0]
    pair_size, pair_at = lax.axis_size("pair"), lax.axis_index("pair")
    todo = jnp.int32(0)
    for leaf in range(leaves):
        place = target * leaves + leaf
        limit = near_count[place]
        for turn in range(near_list.shape[1]):
            source = near_list[place, turn] - first - source_base
            wanted = (turn < limit) & (source >= 0) & (source < sources)
            if pair_size > 1:
                wanted = wanted & (pair_at == turn % pair_size)
            work[todo] = leaf * sources + source
            todo = todo + wanted.astype(jnp.int32)
    return todo


def subtree_kernel(leaves, near_list, near_count, left, coefs, right, scale, out, totals, work):
    me = lax.axis_index("sub")
    vecs, width = totals.shape[1:]
    sources = left.shape[0]
    todo = list_tiles(near_list, near_count, leaves, me, 0, sources, work)
    totals[...] = jnp.zeros(totals.shape, F32)
    run_tiles((0, todo), listed(work, 0, sources), left, coefs, right, me * leaves, totals, 0)
    for leaf in range(leaves):
        out[:, leaf * width : (leaf + 1) * width] = totals[leaf] * scale[me * leaves + leaf]


def from_subtree(lists, factors, leaves):
    near_list, near_count = lists
    vecs, width = factors[1].shape[1] // 2, factors[1].shape[2]
    return pl.pallas_call(
        functools.partial(subtree_kernel, leaves),
        out_shape=jax.ShapeDtypeStruct((vecs, leaves * width), F32),
        in_specs=[SMEM, SMEM] + [VMEM] * 4,
        out_specs=VMEM,
        scratch_shapes=[
            pltpu.VMEM((leaves, vecs, width), F32),
            pltpu.SMEM((leaves * near_list.shape[1] + 1,), jnp.int32),
        ],
        compiler_params=PARAMS,
        name="near_subtree",
    )(near_list, near_count, *factors)


def interact(source, coefs, columns, target_damping):
    kernel = jnp.exp2(mxu(source_rows(source), columns))
    return product(coefs * damping(source), kernel) * target_damping


def far_kernel(place_of, leaves, subs, nears, given_far, given_parents, *refs):
    refs, (out, far_list, parent_far, found, sems) = refs[:-5], refs[-5:]
    near, refs = refs[:nears], refs[nears:]
    gathered, (skeleton, parent_skel, transfer, basis) = refs[:-4], refs[-4:]
    copies = [
        fetch(given_far, far_list, sems.at[0]),
        fetch(given_parents, parent_far, sems.at[1]),
    ]
    dim, rank = skeleton.shape[1:]
    width = basis.shape[2]
    vecs = found.shape[1]
    targets = [skeleton[leaf] for leaf in range(leaves)]
    targets.append(parent_skel[lax.axis_index("leaf")])
    columns = [(target_columns(x), damping(x) * rank**-0.5) for x in targets]
    for copy in copies:
        copy.wait()

    def block(device):
        which, *index = place_of(device)
        data = gathered[0][tuple(index)]
        for other in range(1, len(gathered)):
            data = jnp.where(which == other, gathered[other][tuple(index)], data)
        return data

    def lanes(data, at):
        part = data[:, :rank]
        for other in range(1, leaves):
            part = jnp.where(at == other, data[:, other * rank : (other + 1) * rank], part)
        return part

    def joined(parts):
        return [jnp.concatenate(part, axis=1) for part in zip(*parts)]

    parts = []
    for turn in range(parent_far.shape[1]):
        parent = parent_far[0, turn]
        lift = block(parent * subs)[dim + vecs :]
        for sub in range(1, subs):
            lift = lift + block(parent * subs + sub)[dim + vecs :]
        pieces = [lift[:, at * rank : (at + 1) * rank] for at in range(leaves)]
        parts.append((parent_skel[parent], jnp.concatenate(pieces, axis=0)))
    upper = interact(*joined(parts), *columns[leaves])

    fields = []
    for leaf in range(leaves):
        parts = []
        for turn in range(far_list.shape[1]):
            partner = far_list[leaf, turn]
            data = lanes(block(partner // leaves), partner % leaves)
            parts.append((data[:dim], data[dim : dim + vecs]))
        far = interact(*joined(parts), *columns[leaf])
        fields.append(far + product(upper, transfer[leaf], NT))

    copies = []
    for leaf in range(leaves):
        span = slice(leaf * width, (leaf + 1) * width)
        total = product(fields[leaf], basis[leaf])
        for part in near:
            total = total + part[:, span]
        found[leaf] = total
        copies.append(
            pltpu.make_async_copy(found.at[leaf], out.at[:, pl.ds(leaf * width, width)], sems.at[leaf])
        )
        copies[-1].start()
    for copy in copies:
        copy.wait()


def far_field(place_of, subs, far_list, parent_far, near, gathered, *held):
    basis = held[-1]
    leaves, rank, width = basis.shape
    vecs = near[0].shape[0]
    return pl.pallas_call(
        functools.partial(far_kernel, place_of, leaves, subs, len(near)),
        out_shape=jax.ShapeDtypeStruct((vecs, leaves * width), F32),
        in_specs=[ANY, ANY] + [VMEM] * (len(near) + len(gathered) + 4),
        out_specs=ANY,
        scratch_shapes=[
            pltpu.SMEM(far_list.shape, jnp.int32),
            pltpu.SMEM(parent_far.shape, jnp.int32),
            pltpu.VMEM((leaves, vecs, width), F32),
            pltpu.SemaphoreType.DMA((max(2, leaves),)),
        ],
        compiler_params=PARAMS,
        cost_estimate=lasts(0.5),
        name="far_field",
    )(far_list, parent_far, *near, *gathered, *held)


def swap(x, bit, axis="sub"):
    return lax.ppermute(x, axis, [(at, at ^ bit) for at in range(lax.axis_size(axis))])


def local(
    points,
    vectors,
    basis,
    transfer,
    skeleton,
    parent_skel,
    near_list,
    near_count,
    far_list,
    parent_far,
):
    leaves, _, width = basis.shape
    dim = points.shape[0]
    subs, groups = lax.axis_size("sub"), lax.axis_size("leaf")
    lists = (near_list, near_count)
    split = subs == 4 and lax.axis_size("pair") == 1 and groups in (4, 8, 16)
    packed, stack, tiles = coefficients(split, lists, points, vectors, basis, transfer, skeleton)
    if split:
        twin, cross = swap(stack, 1), swap(stack, 2)
        line = packed[None]
        for bit in range(groups.bit_length() - 1):
            arrived = swap(line, 1 << bit, "leaf")
            if bit == 0:
                own = with_self(stack, dim, leaves)
                arrived, own = lax.optimization_barrier((arrived, own))
            elif bit == 1:
                right, scale, begun, *inner = tiles_local(tiles, twin, own, leaves)
                arrived, begun = lax.optimization_barrier((arrived, begun))
            line = jnp.concatenate([line, arrived])
        beside = swap(line, 2)
        twin_near, *held, begun = tiles_cross(tiles, cross, right, scale, begun, inner)
        back = swap(twin_near, 1)
        beside, twin_near = lax.optimization_barrier((beside, twin_near))
        plane = jnp.stack([line, beside])
        gathered = (plane, swap(plane, 1))
        near = (tiles_after(tiles, inner, held, *own[2:4], begun), back)

        def place_of(device):
            away = (device % subs) ^ lax.axis_index("sub")
            return away % 2, away // 2, (device // subs) ^ lax.axis_index("leaf")

    else:

        def place_of(device):
            return 0, device

        gathered = (lax.all_gather(packed, ("leaf", "sub")),)
        everyone = lax.all_gather(stack, "sub", axis=1, tiled=True)
        factors = prepare(everyone, dim, width)
        near = (lax.psum(from_subtree(lists, factors, leaves), "pair"),)

    return far_field(
        place_of, subs, far_list, parent_far, near, gathered, skeleton, parent_skel, transfer, basis
    )


def solution(mesh):
    placed = (
        P(None, ("groups", "leaf", "sub")),
        P(None, ("groups", "leaf", "sub")),
        P(("groups", "leaf", "sub"), None, None),
        P(("groups", "leaf", "sub"), None, None),
        P(("groups", "leaf", "sub"), None, None),
        P("groups", None, None),
        P(("groups", "leaf"), None),
        P(("groups", "leaf")),
        P(("groups", "leaf", "sub"), None),
        P(("groups", "leaf"), None),
    )
    return jax.shard_map(
        local,
        mesh=mesh,
        in_specs=placed,
        out_specs=P(None, ("groups", "leaf", "sub")),
        check_vma=False,
    )
```

```python
import functools
import math

import jax
import jax.numpy as jnp
from jax import lax
from jax.experimental import pallas as pl
from jax.experimental.pallas import tpu as pltpu
from jax.sharding import PartitionSpec as P

RATE = 0.125 * math.log2(math.e)
ROWS, COLUMNS = 256, 1024
F32, BF16 = jnp.float32, jnp.bfloat16
VMEM = pl.BlockSpec(memory_space=pltpu.VMEM)
ANY = pl.BlockSpec(memory_space=pl.ANY)
HBM = pl.BlockSpec(memory_space=pltpu.HBM)
SMEM = pl.BlockSpec(memory_space=pltpu.SMEM)
PARAMS = pltpu.CompilerParams(vmem_limit_bytes=40 * 1024 * 1024)
NN, NT = (((1,), (0,)), ((), ())), (((1,), (1,)), ((), ()))


def lasts(microseconds):
    return pl.CostEstimate(
        flops=int(1e9 * microseconds), bytes_accessed=int(3e6 * microseconds), transcendentals=0
    )


def mxu(x, y, dims=NN):
    return lax.dot_general(x, y, dims, preferred_element_type=F32)


def split2(x):
    high = x.astype(BF16)
    return high, (x - high.astype(F32)).astype(BF16)


def split3(x):
    high = x.astype(BF16).astype(F32)
    rest = x - high
    middle = rest.astype(BF16).astype(F32)
    return high, middle, (rest - middle).astype(BF16).astype(F32)


def product(x, y, dims=NN):
    rows = x.shape[0]
    x1, x2 = split2(x)
    y1, y2 = split2(y)
    top = mxu(jnp.concatenate([x1, x2], axis=0), y1, dims)
    return top[:rows] + (top[rows:] + mxu(x1, y2, dims))


def source_rows(x):
    a1, a2, a3 = split3(x * (2.0 * RATE))
    return jnp.concatenate([a1, a1, a2, a2, a1, a3], axis=0).T.astype(BF16)


def target_columns(x):
    b1, b2, b3 = split3(x)
    return jnp.concatenate([b1, b2, b1, b2, b3, b1], axis=0).astype(BF16)


def damping(x):
    return jnp.exp2(-RATE * jnp.sum(x * x, axis=0, keepdims=True))


HEAD = 7
EARLY = 2


def share_tiles(near_list, near_count, leaves, tiles):
    turns = near_list.shape[1]
    me = lax.axis_index("sub")
    core = me % 2
    many = 2 * leaves
    first = lax.axis_index("leaf") * near_list.shape[0]
    base = me // 2 * many
    beside = (me ^ 2) * leaves
    cross_at = HEAD + many * turns
    zero = jnp.int32(0)
    local, cross, used_all, marks = zero, zero, zero, []
    for index in range(many):
        side = 1 - core if index < leaves else core
        place = side * leaves + index % leaves
        limit = near_count[base + place]
        used_all = used_all + limit - 1
        for turn in range(1, turns):
            source = near_list[base + place, turn] - first
            used = turn < limit
            near = source - base
            away = source - beside
            tiles[HEAD + local] = place * many + near
            tiles[cross_at + cross] = place * leaves + away
            local = local + (used & (near >= 0) & (near < many)).astype(jnp.int32)
            cross = cross + (used & (away >= 0) & (away < leaves)).astype(jnp.int32)
        if index == leaves - 1:
            marks = [local, cross]
    other = used_all - local - cross
    own_local, own_cross = local - marks[0], cross - marks[1]
    mine = jnp.clip((used_all + 1 - core) // 2 - cross, 0, local)
    total, twin_total = mine + cross, local - mine + other
    after = total - jnp.minimum(total, twin_total) + 1
    after_cross = jnp.clip(after, 0, own_cross)
    after_local = jnp.clip(after - after_cross, 0, jnp.minimum(mine, own_local))
    tiles[0] = jnp.where(core == 0, marks[0] + mine - 1, local - mine)
    tiles[1] = jnp.where(core == 0, -1, 1)
    tiles[2] = local
    tiles[3] = mine - after_local
    tiles[4] = mine
    tiles[5] = cross - after_cross
    tiles[6] = cross


def walk(tiles, many):
    def pick(step):
        at = tiles[0] + tiles[1] * step
        code = tiles[HEAD + jnp.where(at >= tiles[2], at - tiles[2], at)]
        return code // many, code % many

    return pick


def walk_cross(tiles, leaves):
    cross_at = HEAD + (tiles.shape[0] - HEAD) // 2

    def pick(step):
        code = tiles[cross_at + step]
        return code // leaves, code % leaves

    return pick


def coef_kernel(leaves, share, points, vectors, basis, transfer, skeleton, *refs):
    near_list, near_count, packed, stack, tiles = refs[:5]
    bases, moves, skeletons, lists, counts, sems = refs[5:]
    dim, rank = skeletons.shape[1:]
    width = bases.shape[2]
    vecs = vectors.shape[0]
    held = stack.at[dim:]
    pairs = [(near_list, lists), (near_count, counts), (vectors, held), (basis, bases)]
    pairs += [(transfer, moves), (skeleton, skeletons), (points, stack.at[:dim])]
    loads = [pltpu.make_async_copy(src, dst, sems.at[at]) for at, (src, dst) in enumerate(pairs)]
    for load in loads:
        load.start()
    for load in loads[:2]:
        load.wait()
    if share:
        share_tiles(lists, counts, leaves, tiles)
    else:
        tiles[0] = jnp.int32(0)
    for load in loads[2:]:
        load.wait()
    lift = 0.0
    for leaf in range(leaves):
        lanes = slice(leaf * rank, (leaf + 1) * rank)
        coef = product(held[:, leaf * width : (leaf + 1) * width], bases[leaf], NT)
        packed[0:dim, lanes] = skeletons[leaf]
        packed[dim : dim + vecs, lanes] = coef
        lift = lift + product(coef, moves[leaf])
    rows = vecs // leaves
    for piece in range(leaves):
        packed[dim + vecs :, piece * rank : (piece + 1) * rank] = lift[
            piece * rows : (piece + 1) * rows
        ]


def coefficients(share, lists, points, vectors, basis, transfer, skeleton):
    leaves, dim, rank = skeleton.shape
    vecs = vectors.shape[0]
    inputs = [
        pltpu.with_memory_space_constraint(x, pltpu.HBM)
        for x in (points, vectors, basis, transfer, skeleton, *lists)
    ]
    return pl.pallas_call(
        functools.partial(coef_kernel, leaves, share),
        out_shape=[
            jax.ShapeDtypeStruct((dim + vecs + vecs // leaves, leaves * rank), F32),
            jax.ShapeDtypeStruct((dim + vecs, vectors.shape[1]), F32),
            jax.ShapeDtypeStruct((HEAD + 4 * leaves * lists[0].shape[1],), jnp.int32),
        ],
        in_specs=[HBM] * 7,
        out_specs=[VMEM, VMEM, SMEM],
        scratch_shapes=[pltpu.VMEM(x.shape, F32) for x in (basis, transfer, skeleton)]
        + [pltpu.SMEM(x.shape, jnp.int32) for x in lists]
        + [pltpu.SemaphoreType.DMA((7,))],
        compiler_params=PARAMS,
        cost_estimate=lasts(0.5),
        name="coefficients",
    )(*inputs)


def write_source(points, vectors, left, coefs):
    vecs = vectors.shape[0]
    left[...] = source_rows(points)
    high, low = split2(vectors * damping(points))
    coefs[0:vecs] = high
    coefs[vecs:] = low


def write_target(points, right, scale):
    right[...] = target_columns(points)
    scale[...] = damping(points) * points.shape[1] ** -0.5


def leaf_of(stack, dim, width, leaf):
    span = slice(leaf * width, (leaf + 1) * width)
    return stack[:dim, span], stack[dim:, span]


def prepare_kernel(dim, width, stack, left, coefs, right, scale):
    for leaf in range(stack.shape[1] // width):
        points, vectors = leaf_of(stack, dim, width, leaf)
        write_source(points, vectors, left.at[leaf], coefs.at[leaf])
        write_target(points, right.at[leaf], scale.at[leaf])


def source_shapes(sources, dim, vecs, width):
    return [
        jax.ShapeDtypeStruct((sources, width, 6 * dim), BF16),
        jax.ShapeDtypeStruct((sources, 2 * vecs, width), BF16),
    ]


def target_shapes(targets, dim, width):
    return [
        jax.ShapeDtypeStruct((targets, 6 * dim, width), BF16),
        jax.ShapeDtypeStruct((targets, 1, width), F32),
    ]


def prepare(stack, dim, width):
    vecs = stack.shape[0] - dim
    count = stack.shape[1] // width
    return pl.pallas_call(
        functools.partial(prepare_kernel, dim, width),
        out_shape=source_shapes(count, dim, vecs, width) + target_shapes(count, dim, width),
        in_specs=[VMEM],
        out_specs=[VMEM] * 4,
        compiler_params=PARAMS,
        cost_estimate=lasts(0.5),
        name="prepare",
    )(stack)


def run_tiles(todo, pick, left, coefs, right, right_base, totals, totals_base):
    vecs, width = totals.shape[1:]
    chunks = [(y, x) for y in range(0, width, COLUMNS) for x in range(0, width, ROWS)]

    def tile(step, carry):
        slot, source = pick(step)

        def exponent(y, x):
            return mxu(left[source, x : x + ROWS], right[right_base + slot, :, y : y + COLUMNS])

        ahead = exponent(*chunks[0])
        for at, (y, x) in enumerate(chunks):
            power = ahead
            if at + 1 < len(chunks):
                ahead = exponent(*chunks[at + 1])
            high, low = split2(jnp.exp2(power))
            both = coefs[source, :, x : x + ROWS]
            top = mxu(both, high)
            found = top[:vecs] + (top[vecs:] + mxu(both[:vecs], low))
            strip = found if x == 0 else strip + found
            if x + ROWS == width:
                totals[totals_base + slot, :, y : y + COLUMNS] += strip
        return carry

    lax.fori_loop(*todo, tile, 0)


def listed(work, start, sources):
    return lambda step: (work[start + step] // sources, work[start + step] % sources)


def self_kernel(dim, stack, left, coefs, right, scale, totals):
    leaves, _, width = totals.shape
    prepare_kernel(dim, width, stack, left, coefs, right, scale)
    totals[...] = jnp.zeros(totals.shape, F32)
    run_tiles((0, leaves), lambda step: (step, step), left, coefs, right, 0, totals, 0)


def with_self(stack, dim, leaves):
    vecs = stack.shape[0] - dim
    width = stack.shape[1] // leaves
    return pl.pallas_call(
        functools.partial(self_kernel, dim),
        out_shape=source_shapes(leaves, dim, vecs, width)
        + target_shapes(leaves, dim, width)
        + [jax.ShapeDtypeStruct((leaves, vecs, width), F32)],
        in_specs=[VMEM],
        out_specs=[VMEM] * 5,
        compiler_params=PARAMS,
        cost_estimate=lasts(0.5),
        name="near_self",
    )(stack)


def fetch(tiles, held, sem):
    copy = pltpu.make_async_copy(tiles, held, sem)
    copy.start()
    return copy


def list_scratch(tiles):
    return [pltpu.SMEM(tiles.shape, jnp.int32), pltpu.SemaphoreType.DMA]


def local_kernel(leaves, dim, given_tiles, twin_stack, *refs):
    own_left, own_coefs, own_right, own_totals = refs[:4]
    right, scale, totals, left, coefs, tiles, sem = refs[4:]
    lists = fetch(given_tiles, tiles, sem)
    many, _, width = totals.shape
    core = lax.axis_index("sub") % 2
    own, twin = core * leaves, (1 - core) * leaves
    for leaf in range(leaves):
        left[own + leaf] = own_left[leaf]
        coefs[own + leaf] = own_coefs[leaf]
        right[own + leaf] = own_right[leaf]
        totals[own + leaf] = own_totals[leaf]
        totals[twin + leaf] = jnp.zeros(totals.shape[1:], F32)
        points, vectors = leaf_of(twin_stack, dim, width, leaf)
        write_source(points, vectors, left.at[twin + leaf], coefs.at[twin + leaf])
        write_target(points, right.at[twin + leaf], scale.at[leaf])
    lists.wait()
    stop = jnp.minimum(tiles[3], EARLY)
    run_tiles((0, stop), walk(tiles, many), left, coefs, right, 0, totals, 0)


def tiles_local(tiles, twin, own, leaves):
    left, coefs, right, _, totals = own
    vecs, width = totals.shape[1:]
    dim = twin.shape[0] - vecs
    many = 2 * leaves
    return pl.pallas_call(
        functools.partial(local_kernel, leaves, dim),
        out_shape=[
            jax.ShapeDtypeStruct((many, 6 * dim, width), BF16),
            jax.ShapeDtypeStruct((leaves, 1, width), F32),
            jax.ShapeDtypeStruct((many, vecs, width), F32),
        ]
        + source_shapes(many, dim, vecs, width),
        in_specs=[ANY] + [VMEM] * 5,
        out_specs=[VMEM] * 5,
        scratch_shapes=list_scratch(tiles),
        compiler_params=PARAMS,
        cost_estimate=lasts(0.5),
        name="near_local",
    )(tiles, twin, left, coefs, right, totals)


def cross_kernel(leaves, dim, given_tiles, cross_stack, right, scale, begun, *refs):
    local_left, local_coefs, twin_out, left, coefs, own_totals, totals, tiles, sem = refs
    lists = fetch(given_tiles, tiles, sem)
    many, _, width = totals.shape
    core = lax.axis_index("sub") % 2
    own, twin = core * leaves, (1 - core) * leaves
    for leaf in range(leaves):
        points, vectors = leaf_of(cross_stack, dim, width, leaf)
        write_source(points, vectors, left.at[leaf], coefs.at[leaf])
    totals[...] = begun[...]
    lists.wait()
    rest = (jnp.minimum(tiles[3], EARLY), tiles[3])
    run_tiles(rest, walk(tiles, many), local_left, local_coefs, right, 0, totals, 0)
    run_tiles((0, tiles[5]), walk_cross(tiles, leaves), left, coefs, right, 0, totals, 0)
    for leaf in range(leaves):
        twin_out[:, leaf * width : (leaf + 1) * width] = totals[twin + leaf] * scale[leaf]
        own_totals[leaf] = totals[own + leaf]


def tiles_cross(tiles, cross, right, scale, begun, inner):
    many, vecs, width = begun.shape
    leaves = many // 2
    dim = cross.shape[0] - vecs
    return pl.pallas_call(
        functools.partial(cross_kernel, leaves, dim),
        out_shape=[jax.ShapeDtypeStruct((vecs, leaves * width), F32)]
        + source_shapes(leaves, dim, vecs, width)
        + [jax.ShapeDtypeStruct((leaves, vecs, width), F32)],
        in_specs=[ANY] + [VMEM] * 6,
        out_specs=[VMEM] * 4,
        scratch_shapes=[pltpu.VMEM((many, vecs, width), F32)] + list_scratch(tiles),
        compiler_params=PARAMS,
        cost_estimate=lasts(0.5),
        name="near_cross",
    )(tiles, cross, right, scale, begun, *inner)


def after_kernel(leaves, given_tiles, left, coefs, cross_left, cross_coefs, *refs):
    right, scale, begun, out, totals, tiles, sem = refs
    lists = fetch(given_tiles, tiles, sem)
    width = totals.shape[2]
    own = lax.axis_index("sub") % 2 * leaves
    totals[...] = begun[...]

    def own_place(pick):
        def picked(step):
            place, source = pick(step)
            return place - own, source

        return picked

    lists.wait()
    local, cross = own_place(walk(tiles, 2 * leaves)), own_place(walk_cross(tiles, leaves))
    run_tiles((tiles[3], tiles[4]), local, left, coefs, right, 0, totals, 0)
    run_tiles((tiles[5], tiles[6]), cross, cross_left, cross_coefs, right, 0, totals, 0)
    for leaf in range(leaves):
        out[:, leaf * width : (leaf + 1) * width] = totals[leaf] * scale[leaf]


def tiles_after(tiles, local, cross, right, scale, begun):
    leaves, vecs, width = begun.shape
    return pl.pallas_call(
        functools.partial(after_kernel, leaves),
        out_shape=jax.ShapeDtypeStruct((vecs, leaves * width), F32),
        in_specs=[ANY] + [VMEM] * 7,
        out_specs=VMEM,
        scratch_shapes=[pltpu.VMEM((leaves, vecs, width), F32)] + list_scratch(tiles),
        compiler_params=PARAMS,
        cost_estimate=lasts(0.5),
        name="near_after",
    )(tiles, *local, *cross, right, scale, begun)


def list_tiles(near_list, near_count, leaves, target, source_base, sources, work):
    first = lax.axis_index("leaf") * near_list.shape[0]
    pair_size, pair_at = lax.axis_size("pair"), lax.axis_index("pair")
    todo = jnp.int32(0)
    for leaf in range(leaves):
        place = target * leaves + leaf
        limit = near_count[place]
        for turn in range(near_list.shape[1]):
            source = near_list[place, turn] - first - source_base
            wanted = (turn < limit) & (source >= 0) & (source < sources)
            if pair_size > 1:
                wanted = wanted & (pair_at == turn % pair_size)
            work[todo] = leaf * sources + source
            todo = todo + wanted.astype(jnp.int32)
    return todo


def subtree_kernel(leaves, near_list, near_count, left, coefs, right, scale, out, totals, work):
    me = lax.axis_index("sub")
    vecs, width = totals.shape[1:]
    sources = left.shape[0]
    todo = list_tiles(near_list, near_count, leaves, me, 0, sources, work)
    totals[...] = jnp.zeros(totals.shape, F32)
    run_tiles((0, todo), listed(work, 0, sources), left, coefs, right, me * leaves, totals, 0)
    for leaf in range(leaves):
        out[:, leaf * width : (leaf + 1) * width] = totals[leaf] * scale[me * leaves + leaf]


def from_subtree(lists, factors, leaves):
    near_list, near_count = lists
    vecs, width = factors[1].shape[1] // 2, factors[1].shape[2]
    return pl.pallas_call(
        functools.partial(subtree_kernel, leaves),
        out_shape=jax.ShapeDtypeStruct((vecs, leaves * width), F32),
        in_specs=[SMEM, SMEM] + [VMEM] * 4,
        out_specs=VMEM,
        scratch_shapes=[
            pltpu.VMEM((leaves, vecs, width), F32),
            pltpu.SMEM((leaves * near_list.shape[1] + 1,), jnp.int32),
        ],
        compiler_params=PARAMS,
        name="near_subtree",
    )(near_list, near_count, *factors)


def interact(source, coefs, columns, target_damping):
    kernel = jnp.exp2(mxu(source_rows(source), columns))
    return product(coefs * damping(source), kernel) * target_damping


def far_kernel(place_of, leaves, subs, nears, given_far, given_parents, *refs):
    refs, (out, far_list, parent_far, found, sems) = refs[:-5], refs[-5:]
    near, refs = refs[:nears], refs[nears:]
    gathered, (skeleton, parent_skel, transfer, basis) = refs[:-4], refs[-4:]
    copies = [
        fetch(given_far, far_list, sems.at[0]),
        fetch(given_parents, parent_far, sems.at[1]),
    ]
    dim, rank = skeleton.shape[1:]
    width = basis.shape[2]
    vecs = found.shape[1]
    targets = [skeleton[leaf] for leaf in range(leaves)]
    targets.append(parent_skel[lax.axis_index("leaf")])
    columns = [(target_columns(x), damping(x) * rank**-0.5) for x in targets]
    for copy in copies:
        copy.wait()

    def block(device):
        which, *index = place_of(device)
        data = gathered[0][tuple(index)]
        for other in range(1, len(gathered)):
            data = jnp.where(which == other, gathered[other][tuple(index)], data)
        return data

    def joined(parts):
        return [jnp.concatenate(part, axis=1) for part in zip(*parts)]

    parts = []
    for turn in range(parent_far.shape[1]):
        parent = parent_far[0, turn]
        lift = block(parent * subs)[dim + vecs :]
        for sub in range(1, subs):
            lift = lift + block(parent * subs + sub)[dim + vecs :]
        pieces = [lift[:, at * rank : (at + 1) * rank] for at in range(leaves)]
        parts.append((parent_skel[parent], jnp.concatenate(pieces, axis=0)))
    upper = interact(*joined(parts), *columns[leaves])

    half = lax.broadcasted_iota(jnp.int32, (vecs, leaves * rank), 1) // rank
    fields = []
    for leaf in range(leaves):
        parts = []
        for turn in range(far_list.shape[1]):
            partner = far_list[leaf, turn]
            data = block(partner // leaves)
            coefs = jnp.where(half == partner % leaves, data[dim : dim + vecs], 0.0)
            parts.append((data[:dim], coefs))
        far = interact(*joined(parts), *columns[leaf])
        fields.append(far + product(upper, transfer[leaf], NT))

    copies = []
    for leaf in range(leaves):
        span = slice(leaf * width, (leaf + 1) * width)
        total = product(fields[leaf], basis[leaf])
        for part in near:
            total = total + part[:, span]
        found[leaf] = total
        copies.append(
            pltpu.make_async_copy(found.at[leaf], out.at[:, pl.ds(leaf * width, width)], sems.at[leaf])
        )
        copies[-1].start()
    for copy in copies:
        copy.wait()


def far_field(place_of, subs, far_list, parent_far, near, gathered, *held):
    basis = held[-1]
    leaves, rank, width = basis.shape
    vecs = near[0].shape[0]
    return pl.pallas_call(
        functools.partial(far_kernel, place_of, leaves, subs, len(near)),
        out_shape=jax.ShapeDtypeStruct((vecs, leaves * width), F32),
        in_specs=[ANY, ANY] + [VMEM] * (len(near) + len(gathered) + 4),
        out_specs=ANY,
        scratch_shapes=[
            pltpu.SMEM(far_list.shape, jnp.int32),
            pltpu.SMEM(parent_far.shape, jnp.int32),
            pltpu.VMEM((leaves, vecs, width), F32),
            pltpu.SemaphoreType.DMA((max(2, leaves),)),
        ],
        compiler_params=PARAMS,
        cost_estimate=lasts(0.5),
        name="far_field",
    )(far_list, parent_far, *near, *gathered, *held)


def swap(x, bit, axis="sub"):
    return lax.ppermute(x, axis, [(at, at ^ bit) for at in range(lax.axis_size(axis))])


def local(
    points,
    vectors,
    basis,
    transfer,
    skeleton,
    parent_skel,
    near_list,
    near_count,
    far_list,
    parent_far,
):
    leaves, _, width = basis.shape
    dim = points.shape[0]
    subs, groups = lax.axis_size("sub"), lax.axis_size("leaf")
    lists = (near_list, near_count)
    split = subs == 4 and lax.axis_size("pair") == 1 and groups in (4, 8, 16)
    packed, stack, tiles = coefficients(split, lists, points, vectors, basis, transfer, skeleton)
    if split:
        twin, cross = swap(stack, 1), swap(stack, 2)
        line = packed[None]
        step = groups
        while step > 1:
            step //= 2
            arrived = swap(line, step, "leaf")
            if step == groups // 2:
                own = with_self(stack, dim, leaves)
                arrived, own = lax.optimization_barrier((arrived, own))
            elif step == groups // 4:
                right, scale, begun, *inner = tiles_local(tiles, twin, own, leaves)
                arrived, begun = lax.optimization_barrier((arrived, begun))
            line = jnp.concatenate([line, arrived])
        beside = swap(line, 2)
        twin_near, *held, begun = tiles_cross(tiles, cross, right, scale, begun, inner)
        back = swap(twin_near, 1)
        beside, twin_near = lax.optimization_barrier((beside, twin_near))
        plane = jnp.stack([line, beside])
        gathered = (plane, swap(plane, 1))
        near = (tiles_after(tiles, inner, held, *own[2:4], begun), back)

        def place_of(device):
            away = (device % subs) ^ lax.axis_index("sub")
            apart = (device // subs) ^ lax.axis_index("leaf")
            place = 0
            for bit in range(groups.bit_length() - 1):
                place = place * 2 + (apart >> bit) % 2
            return away % 2, away // 2, place

    else:

        def place_of(device):
            return 0, device

        gathered = (lax.all_gather(packed, ("leaf", "sub")),)
        everyone = lax.all_gather(stack, "sub", axis=1, tiled=True)
        factors = prepare(everyone, dim, width)
        near = (lax.psum(from_subtree(lists, factors, leaves), "pair"),)

    return far_field(
        place_of, subs, far_list, parent_far, near, gathered, skeleton, parent_skel, transfer, basis
    )


def solution(mesh):
    placed = (
        P(None, ("groups", "leaf", "sub")),
        P(None, ("groups", "leaf", "sub")),
        P(("groups", "leaf", "sub"), None, None),
        P(("groups", "leaf", "sub"), None, None),
        P(("groups", "leaf", "sub"), None, None),
        P("groups", None, None),
        P(("groups", "leaf"), None),
        P(("groups", "leaf")),
        P(("groups", "leaf", "sub"), None),
        P(("groups", "leaf"), None),
    )
    return jax.shard_map(
        local,
        mesh=mesh,
        in_specs=placed,
        out_specs=P(None, ("groups", "leaf", "sub")),
        check_vma=False,
    )
```

```python
import functools
import math

import jax
import jax.numpy as jnp
from jax import lax
from jax.experimental import pallas as pl
from jax.experimental.pallas import tpu as pltpu
from jax.sharding import PartitionSpec as P

RATE = 0.125 * math.log2(math.e)
ROWS, COLUMNS = 256, 1024
F32, BF16 = jnp.float32, jnp.bfloat16
VMEM = pl.BlockSpec(memory_space=pltpu.VMEM)
ANY = pl.BlockSpec(memory_space=pl.ANY)
HBM = pl.BlockSpec(memory_space=pltpu.HBM)
SMEM = pl.BlockSpec(memory_space=pltpu.SMEM)
PARAMS = pltpu.CompilerParams(vmem_limit_bytes=40 * 1024 * 1024)
NN, NT = (((1,), (0,)), ((), ())), (((1,), (1,)), ((), ()))


def lasts(microseconds):
    return pl.CostEstimate(
        flops=int(1e9 * microseconds), bytes_accessed=int(3e6 * microseconds), transcendentals=0
    )


def mxu(x, y, dims=NN):
    return lax.dot_general(x, y, dims, preferred_element_type=F32)


def split2(x):
    high = x.astype(BF16)
    return high, (x - high.astype(F32)).astype(BF16)


def split3(x):
    high = x.astype(BF16).astype(F32)
    rest = x - high
    middle = rest.astype(BF16).astype(F32)
    return high, middle, (rest - middle).astype(BF16).astype(F32)


def product(x, y, dims=NN):
    rows = x.shape[0]
    x1, x2 = split2(x)
    y1, y2 = split2(y)
    top = mxu(jnp.concatenate([x1, x2], axis=0), y1, dims)
    return top[:rows] + (top[rows:] + mxu(x1, y2, dims))


def source_rows(x):
    a1, a2, a3 = split3(x * (2.0 * RATE))
    return jnp.concatenate([a1, a1, a2, a2, a1, a3], axis=0).T.astype(BF16)


def target_columns(x):
    b1, b2, b3 = split3(x)
    return jnp.concatenate([b1, b2, b1, b2, b3, b1], axis=0).astype(BF16)


def damping(x):
    return jnp.exp2(-RATE * jnp.sum(x * x, axis=0, keepdims=True))


HEAD = 9
EARLY = 2


def share_tiles(near_list, near_count, leaves, tiles):
    turns = near_list.shape[1]
    me = lax.axis_index("sub")
    core = me % 2
    many = 2 * leaves
    every = many + leaves
    first = lax.axis_index("leaf") * near_list.shape[0]
    base = me // 2 * many
    beside = (me ^ 2) * leaves
    spots = list_spots(leaves, turns)
    zero = jnp.int32(0)
    local, ahead, late, used_all, marks = zero, zero, zero, zero, []
    for index in range(many):
        side = 1 - core if index < leaves else core
        place = side * leaves + index % leaves
        limit = near_count[base + place]
        used_all = used_all + limit - 1
        for turn in range(1, turns):
            source = near_list[base + place, turn] - first
            used = turn < limit
            near = source - base
            away = source - beside
            across = place * every + many + away
            tiles[spots[0] + local] = place * every + near
            tiles[spots[1] + ahead] = across
            tiles[spots[2] + late] = across
            local = local + (used & (near >= 0) & (near < many)).astype(jnp.int32)
            ahead = ahead + (used & (away == 0)).astype(jnp.int32)
            late = late + (used & (away > 0) & (away < leaves)).astype(jnp.int32)
        if index == leaves - 1:
            marks = [local, ahead, late]
    cross = ahead + late
    other = used_all - local - cross
    mine = jnp.clip((used_all + 1 - core) // 2 - cross, 0, local)
    total, twin_total = mine + cross, local - mine + other
    own_mine = jnp.minimum(mine, local - marks[0])
    after = total - jnp.minimum(total, twin_total) + 1
    after_late = jnp.clip(after, 0, late - marks[2])
    after_early = jnp.clip(after - after_late, 0, own_mine + ahead - marks[1])
    tiles[0] = jnp.where(core == 0, marks[0] + mine - 1, local - mine)
    tiles[1] = jnp.where(core == 0, -1, 1)
    tiles[2] = mine
    tiles[3] = mine - own_mine
    tiles[4] = local
    tiles[5] = mine + ahead - after_early
    tiles[6] = mine + ahead
    tiles[7] = late - after_late
    tiles[8] = late
    tiles[spots[1] - 1] = marks[1]


def list_spots(leaves, turns):
    each = 2 * leaves * (turns - 1) + 2
    return HEAD, HEAD + each, HEAD + 2 * each


def list_size(leaves, turns):
    return HEAD + 3 * (2 * leaves * (turns - 1) + 2)


def early_pick(tiles, leaves):
    ahead_at = HEAD + (tiles.shape[0] - HEAD) // 3

    def pick(step):
        twin_local, local, twin_ahead = tiles[3], tiles[2], tiles[ahead_at - 1]
        low, high = step < twin_local, step < twin_local + twin_ahead
        is_local = low | (~high & (step < local + twin_ahead))
        at = tiles[0] + tiles[1] * jnp.where(low, step, step - twin_ahead)
        at = jnp.where(at >= tiles[4], at - tiles[4], at)
        other = jnp.where(high, step - twin_local, step - local)
        code = tiles[jnp.where(is_local, HEAD + at, ahead_at + other)]
        return code // (3 * leaves), code % (3 * leaves)

    return pick


def late_pick(tiles, leaves):
    late_at = HEAD + (tiles.shape[0] - HEAD) // 3 * 2

    def pick(step):
        code = tiles[late_at + step]
        return code // (3 * leaves), code % (3 * leaves) - (2 * leaves + 1)

    return pick


def coef_kernel(leaves, share, points, vectors, basis, transfer, skeleton, *refs):
    near_list, near_count, packed, stack, ahead, late, tiles = refs[:7]
    bases, moves, skeletons, lists, counts, sems = refs[7:]
    dim, rank = skeletons.shape[1:]
    width = bases.shape[2]
    vecs = vectors.shape[0]
    held = stack.at[dim:]
    pairs = [(near_list, lists), (near_count, counts), (vectors, held), (basis, bases)]
    pairs += [(transfer, moves), (skeleton, skeletons), (points, stack.at[:dim])]
    for part, lanes in ((ahead, pl.ds(0, width)), (late, pl.ds(width, (leaves - 1) * width))):
        pairs += [(points.at[:, lanes], part.at[:dim]), (vectors.at[:, lanes], part.at[dim:])]
    loads = [pltpu.make_async_copy(src, dst, sems.at[at]) for at, (src, dst) in enumerate(pairs)]
    for load in loads:
        load.start()
    for load in loads[:2]:
        load.wait()
    if share:
        share_tiles(lists, counts, leaves, tiles)
    else:
        tiles[0] = jnp.int32(0)
    for load in loads[2:6]:
        load.wait()
    lift = 0.0
    for leaf in range(leaves):
        lanes = slice(leaf * rank, (leaf + 1) * rank)
        coef = product(held[:, leaf * width : (leaf + 1) * width], bases[leaf], NT)
        packed[0:dim, lanes] = skeletons[leaf]
        packed[dim : dim + vecs, lanes] = coef
        lift = lift + product(coef, moves[leaf])
    rows = vecs // leaves
    for piece in range(leaves):
        packed[dim + vecs :, piece * rank : (piece + 1) * rank] = lift[
            piece * rows : (piece + 1) * rows
        ]
    for load in loads[6:]:
        load.wait()


def coefficients(share, lists, points, vectors, basis, transfer, skeleton):
    leaves, dim, rank = skeleton.shape
    vecs, width = vectors.shape[0], basis.shape[2]
    inputs = [
        pltpu.with_memory_space_constraint(x, pltpu.HBM)
        for x in (points, vectors, basis, transfer, skeleton, *lists)
    ]
    return pl.pallas_call(
        functools.partial(coef_kernel, leaves, share),
        out_shape=[
            jax.ShapeDtypeStruct((dim + vecs + vecs // leaves, leaves * rank), F32),
            jax.ShapeDtypeStruct((dim + vecs, vectors.shape[1]), F32),
            jax.ShapeDtypeStruct((dim + vecs, width), F32),
            jax.ShapeDtypeStruct((dim + vecs, (leaves - 1) * width), F32),
            jax.ShapeDtypeStruct((list_size(leaves, lists[0].shape[1]),), jnp.int32),
        ],
        in_specs=[HBM] * 7,
        out_specs=[VMEM] * 4 + [SMEM],
        scratch_shapes=[pltpu.VMEM(x.shape, F32) for x in (basis, transfer, skeleton)]
        + [pltpu.SMEM(x.shape, jnp.int32) for x in lists]
        + [pltpu.SemaphoreType.DMA((11,))],
        compiler_params=PARAMS,
        cost_estimate=lasts(0.5),
        name="coefficients",
    )(*inputs)


def write_source(points, vectors, left, coefs):
    vecs = vectors.shape[0]
    left[...] = source_rows(points)
    high, low = split2(vectors * damping(points))
    coefs[0:vecs] = high
    coefs[vecs:] = low


def write_target(points, right, scale):
    right[...] = target_columns(points)
    scale[...] = damping(points) * points.shape[1] ** -0.5


def leaf_of(stack, dim, width, leaf):
    span = slice(leaf * width, (leaf + 1) * width)
    return stack[:dim, span], stack[dim:, span]


def prepare_kernel(dim, width, stack, left, coefs, right, scale):
    for leaf in range(stack.shape[1] // width):
        points, vectors = leaf_of(stack, dim, width, leaf)
        write_source(points, vectors, left.at[leaf], coefs.at[leaf])
        write_target(points, right.at[leaf], scale.at[leaf])


def source_shapes(sources, dim, vecs, width):
    return [
        jax.ShapeDtypeStruct((sources, width, 6 * dim), BF16),
        jax.ShapeDtypeStruct((sources, 2 * vecs, width), BF16),
    ]


def target_shapes(targets, dim, width):
    return [
        jax.ShapeDtypeStruct((targets, 6 * dim, width), BF16),
        jax.ShapeDtypeStruct((targets, 1, width), F32),
    ]


def prepare(stack, dim, width):
    vecs = stack.shape[0] - dim
    count = stack.shape[1] // width
    return pl.pallas_call(
        functools.partial(prepare_kernel, dim, width),
        out_shape=source_shapes(count, dim, vecs, width) + target_shapes(count, dim, width),
        in_specs=[VMEM],
        out_specs=[VMEM] * 4,
        compiler_params=PARAMS,
        cost_estimate=lasts(0.5),
        name="prepare",
    )(stack)


def run_tiles(todo, pick, left, coefs, right, right_base, totals, totals_base):
    vecs, width = totals.shape[1:]
    chunks = [(y, x) for y in range(0, width, COLUMNS) for x in range(0, width, ROWS)]

    def tile(step, carry):
        slot, source = pick(step)

        def exponent(y, x):
            return mxu(left[source, x : x + ROWS], right[right_base + slot, :, y : y + COLUMNS])

        ahead = exponent(*chunks[0])
        for at, (y, x) in enumerate(chunks):
            power = ahead
            if at + 1 < len(chunks):
                ahead = exponent(*chunks[at + 1])
            high, low = split2(jnp.exp2(power))
            both = coefs[source, :, x : x + ROWS]
            top = mxu(both, high)
            found = top[:vecs] + (top[vecs:] + mxu(both[:vecs], low))
            strip = found if x == 0 else strip + found
            if x + ROWS == width:
                totals[totals_base + slot, :, y : y + COLUMNS] += strip
        return carry

    lax.fori_loop(*todo, tile, 0)


def listed(work, start, sources):
    return lambda step: (work[start + step] // sources, work[start + step] % sources)


def self_kernel(dim, stack, left, coefs, right, scale, totals):
    leaves, _, width = totals.shape
    prepare_kernel(dim, width, stack, left, coefs, right, scale)
    totals[...] = jnp.zeros(totals.shape, F32)
    run_tiles((0, leaves), lambda step: (step, step), left, coefs, right, 0, totals, 0)


def with_self(stack, dim, leaves):
    vecs = stack.shape[0] - dim
    width = stack.shape[1] // leaves
    return pl.pallas_call(
        functools.partial(self_kernel, dim),
        out_shape=source_shapes(leaves, dim, vecs, width)
        + target_shapes(leaves, dim, width)
        + [jax.ShapeDtypeStruct((leaves, vecs, width), F32)],
        in_specs=[VMEM],
        out_specs=[VMEM] * 5,
        compiler_params=PARAMS,
        cost_estimate=lasts(0.5),
        name="near_self",
    )(stack)


def fetch(tiles, held, sem):
    copy = pltpu.make_async_copy(tiles, held, sem)
    copy.start()
    return copy


def list_scratch(tiles):
    return [pltpu.SMEM(tiles.shape, jnp.int32), pltpu.SemaphoreType.DMA]


def early_kernel(leaves, dim, given_tiles, twin_stack, ahead_stack, *refs):
    own_left, own_coefs, own_right, own_totals = refs[:4]
    right, scale, totals, left, coefs, tiles, sem = refs[4:]
    lists = fetch(given_tiles, tiles, sem)
    many, _, width = totals.shape
    core = lax.axis_index("sub") % 2
    own, twin = core * leaves, (1 - core) * leaves
    points, vectors = leaf_of(ahead_stack, dim, width, 0)
    write_source(points, vectors, left.at[many], coefs.at[many])
    for leaf in range(leaves):
        left[own + leaf] = own_left[leaf]
        coefs[own + leaf] = own_coefs[leaf]
        right[own + leaf] = own_right[leaf]
        totals[own + leaf] = own_totals[leaf]
        totals[twin + leaf] = jnp.zeros(totals.shape[1:], F32)
        points, vectors = leaf_of(twin_stack, dim, width, leaf)
        write_source(points, vectors, left.at[twin + leaf], coefs.at[twin + leaf])
        write_target(points, right.at[twin + leaf], scale.at[leaf])
    lists.wait()
    stop = jnp.minimum(tiles[5], EARLY)
    run_tiles((0, stop), early_pick(tiles, leaves), left, coefs, right, 0, totals, 0)


def tiles_early(tiles, twin, ahead, own, leaves):
    left, coefs, right, _, totals = own
    vecs, width = totals.shape[1:]
    dim = twin.shape[0] - vecs
    many = 2 * leaves
    return pl.pallas_call(
        functools.partial(early_kernel, leaves, dim),
        out_shape=[
            jax.ShapeDtypeStruct((many, 6 * dim, width), BF16),
            jax.ShapeDtypeStruct((leaves, 1, width), F32),
            jax.ShapeDtypeStruct((many, vecs, width), F32),
        ]
        + source_shapes(many + 1, dim, vecs, width),
        in_specs=[ANY] + [VMEM] * 6,
        out_specs=[VMEM] * 5,
        scratch_shapes=list_scratch(tiles),
        compiler_params=PARAMS,
        cost_estimate=lasts(0.5),
        name="near_early",
    )(tiles, twin, ahead, left, coefs, right, totals)


def late_kernel(leaves, dim, given_tiles, late_stack, right, scale, begun, *refs):
    early_left, early_coefs, twin_out, left, coefs, own_totals, totals, tiles, sem = refs
    lists = fetch(given_tiles, tiles, sem)
    many, _, width = totals.shape
    core = lax.axis_index("sub") % 2
    own, twin = core * leaves, (1 - core) * leaves
    for leaf in range(leaves - 1):
        points, vectors = leaf_of(late_stack, dim, width, leaf)
        write_source(points, vectors, left.at[leaf], coefs.at[leaf])
    totals[...] = begun[...]
    lists.wait()
    rest = (jnp.minimum(tiles[5], EARLY), tiles[5])
    run_tiles(rest, early_pick(tiles, leaves), early_left, early_coefs, right, 0, totals, 0)
    run_tiles((0, tiles[7]), late_pick(tiles, leaves), left, coefs, right, 0, totals, 0)
    for leaf in range(leaves):
        twin_out[:, leaf * width : (leaf + 1) * width] = totals[twin + leaf] * scale[leaf]
        own_totals[leaf] = totals[own + leaf]


def tiles_late(tiles, late, right, scale, begun, early):
    many, vecs, width = begun.shape
    leaves = many // 2
    dim = late.shape[0] - vecs
    return pl.pallas_call(
        functools.partial(late_kernel, leaves, dim),
        out_shape=[jax.ShapeDtypeStruct((vecs, leaves * width), F32)]
        + source_shapes(leaves - 1, dim, vecs, width)
        + [jax.ShapeDtypeStruct((leaves, vecs, width), F32)],
        in_specs=[ANY] + [VMEM] * 6,
        out_specs=[VMEM] * 4,
        scratch_shapes=[pltpu.VMEM((many, vecs, width), F32)] + list_scratch(tiles),
        compiler_params=PARAMS,
        cost_estimate=lasts(0.5),
        name="near_late",
    )(tiles, late, right, scale, begun, *early)


def after_kernel(leaves, given_tiles, left, coefs, late_left, late_coefs, *refs):
    right, scale, begun, out, totals, tiles, sem = refs
    lists = fetch(given_tiles, tiles, sem)
    width = totals.shape[2]
    own = lax.axis_index("sub") % 2 * leaves
    totals[...] = begun[...]

    def own_place(pick):
        def picked(step):
            place, source = pick(step)
            return place - own, source

        return picked

    lists.wait()
    early, late = own_place(early_pick(tiles, leaves)), own_place(late_pick(tiles, leaves))
    run_tiles((tiles[5], tiles[6]), early, left, coefs, right, 0, totals, 0)
    run_tiles((tiles[7], tiles[8]), late, late_left, late_coefs, right, 0, totals, 0)
    for leaf in range(leaves):
        out[:, leaf * width : (leaf + 1) * width] = totals[leaf] * scale[leaf]


def tiles_after(tiles, early, late, right, scale, begun):
    leaves, vecs, width = begun.shape
    return pl.pallas_call(
        functools.partial(after_kernel, leaves),
        out_shape=jax.ShapeDtypeStruct((vecs, leaves * width), F32),
        in_specs=[ANY] + [VMEM] * 7,
        out_specs=VMEM,
        scratch_shapes=[pltpu.VMEM((leaves, vecs, width), F32)] + list_scratch(tiles),
        compiler_params=PARAMS,
        cost_estimate=lasts(0.5),
        name="near_after",
    )(tiles, *early, *late, right, scale, begun)


def list_tiles(near_list, near_count, leaves, target, source_base, sources, work):
    first = lax.axis_index("leaf") * near_list.shape[0]
    pair_size, pair_at = lax.axis_size("pair"), lax.axis_index("pair")
    todo = jnp.int32(0)
    for leaf in range(leaves):
        place = target * leaves + leaf
        limit = near_count[place]
        for turn in range(near_list.shape[1]):
            source = near_list[place, turn] - first - source_base
            wanted = (turn < limit) & (source >= 0) & (source < sources)
            if pair_size > 1:
                wanted = wanted & (pair_at == turn % pair_size)
            work[todo] = leaf * sources + source
            todo = todo + wanted.astype(jnp.int32)
    return todo


def subtree_kernel(leaves, near_list, near_count, left, coefs, right, scale, out, totals, work):
    me = lax.axis_index("sub")
    vecs, width = totals.shape[1:]
    sources = left.shape[0]
    todo = list_tiles(near_list, near_count, leaves, me, 0, sources, work)
    totals[...] = jnp.zeros(totals.shape, F32)
    run_tiles((0, todo), listed(work, 0, sources), left, coefs, right, me * leaves, totals, 0)
    for leaf in range(leaves):
        out[:, leaf * width : (leaf + 1) * width] = totals[leaf] * scale[me * leaves + leaf]


def from_subtree(lists, factors, leaves):
    near_list, near_count = lists
    vecs, width = factors[1].shape[1] // 2, factors[1].shape[2]
    return pl.pallas_call(
        functools.partial(subtree_kernel, leaves),
        out_shape=jax.ShapeDtypeStruct((vecs, leaves * width), F32),
        in_specs=[SMEM, SMEM] + [VMEM] * 4,
        out_specs=VMEM,
        scratch_shapes=[
            pltpu.VMEM((leaves, vecs, width), F32),
            pltpu.SMEM((leaves * near_list.shape[1] + 1,), jnp.int32),
        ],
        compiler_params=PARAMS,
        name="near_subtree",
    )(near_list, near_count, *factors)


def interact(source, coefs, columns, target_damping):
    kernel = jnp.exp2(mxu(source_rows(source), columns))
    return product(coefs * damping(source), kernel) * target_damping


def far_kernel(place_of, leaves, subs, nears, given_far, given_parents, *refs):
    refs, (out, far_list, parent_far, found, sems) = refs[:-5], refs[-5:]
    near, refs = refs[:nears], refs[nears:]
    gathered, (skeleton, parent_skel, transfer, basis) = refs[:-4], refs[-4:]
    copies = [
        fetch(given_far, far_list, sems.at[0]),
        fetch(given_parents, parent_far, sems.at[1]),
    ]
    dim, rank = skeleton.shape[1:]
    width = basis.shape[2]
    vecs = found.shape[1]
    targets = [skeleton[leaf] for leaf in range(leaves)]
    targets.append(parent_skel[lax.axis_index("leaf")])
    columns = [(target_columns(x), damping(x) * rank**-0.5) for x in targets]
    for copy in copies:
        copy.wait()

    def block(device):
        which, *index = place_of(device)
        data = gathered[0][tuple(index)]
        for other in range(1, len(gathered)):
            data = jnp.where(which == other, gathered[other][tuple(index)], data)
        return data

    def joined(parts):
        return [jnp.concatenate(part, axis=1) for part in zip(*parts)]

    parts = []
    for turn in range(parent_far.shape[1]):
        parent = parent_far[0, turn]
        lift = block(parent * subs)[dim + vecs :]
        for sub in range(1, subs):
            lift = lift + block(parent * subs + sub)[dim + vecs :]
        pieces = [lift[:, at * rank : (at + 1) * rank] for at in range(leaves)]
        parts.append((parent_skel[parent], jnp.concatenate(pieces, axis=0)))
    upper = interact(*joined(parts), *columns[leaves])

    half = lax.broadcasted_iota(jnp.int32, (vecs, leaves * rank), 1) // rank
    fields = []
    for leaf in range(leaves):
        parts = []
        for turn in range(far_list.shape[1]):
            partner = far_list[leaf, turn]
            data = block(partner // leaves)
            coefs = jnp.where(half == partner % leaves, data[dim : dim + vecs], 0.0)
            parts.append((data[:dim], coefs))
        far = interact(*joined(parts), *columns[leaf])
        fields.append(far + product(upper, transfer[leaf], NT))

    copies = []
    for leaf in range(leaves):
        span = slice(leaf * width, (leaf + 1) * width)
        total = product(fields[leaf], basis[leaf])
        for part in near:
            total = total + part[:, span]
        found[leaf] = total
        copies.append(
            pltpu.make_async_copy(found.at[leaf], out.at[:, pl.ds(leaf * width, width)], sems.at[leaf])
        )
        copies[-1].start()
    for copy in copies:
        copy.wait()


def far_field(place_of, subs, far_list, parent_far, near, gathered, *held):
    basis = held[-1]
    leaves, rank, width = basis.shape
    vecs = near[0].shape[0]
    return pl.pallas_call(
        functools.partial(far_kernel, place_of, leaves, subs, len(near)),
        out_shape=jax.ShapeDtypeStruct((vecs, leaves * width), F32),
        in_specs=[ANY, ANY] + [VMEM] * (len(near) + len(gathered) + 4),
        out_specs=ANY,
        scratch_shapes=[
            pltpu.SMEM(far_list.shape, jnp.int32),
            pltpu.SMEM(parent_far.shape, jnp.int32),
            pltpu.VMEM((leaves, vecs, width), F32),
            pltpu.SemaphoreType.DMA((max(2, leaves),)),
        ],
        compiler_params=PARAMS,
        cost_estimate=lasts(0.5),
        name="far_field",
    )(far_list, parent_far, *near, *gathered, *held)


def swap(x, bit, axis="sub"):
    return lax.ppermute(x, axis, [(at, at ^ bit) for at in range(lax.axis_size(axis))])


def local(
    points,
    vectors,
    basis,
    transfer,
    skeleton,
    parent_skel,
    near_list,
    near_count,
    far_list,
    parent_far,
):
    leaves, _, width = basis.shape
    dim = points.shape[0]
    subs, groups = lax.axis_size("sub"), lax.axis_size("leaf")
    lists = (near_list, near_count)
    split = leaves > 1 and subs == 4 and lax.axis_size("pair") == 1 and groups in (4, 8, 16)
    packed, stack, ahead, late, tiles = coefficients(split, lists, points, vectors, basis, transfer, skeleton)
    if split:
        twin, ahead, late = swap(stack, 1), swap(ahead, 2), swap(late, 2)
        line = packed[None]
        step = groups
        while step > 1:
            step //= 2
            arrived = swap(line, step, "leaf")
            if step == groups // 2:
                own = with_self(stack, dim, leaves)
                arrived, own = lax.optimization_barrier((arrived, own))
            elif step == groups // 4:
                right, scale, begun, *early = tiles_early(tiles, twin, ahead, own, leaves)
                arrived, begun = lax.optimization_barrier((arrived, begun))
            line = jnp.concatenate([line, arrived])
        beside = swap(line, 2)
        twin_near, *held, begun = tiles_late(tiles, late, right, scale, begun, early)
        back = swap(twin_near, 1)
        beside, twin_near = lax.optimization_barrier((beside, twin_near))
        plane = jnp.stack([line, beside])
        gathered = (plane, swap(plane, 1))
        near = (tiles_after(tiles, early, held, *own[2:4], begun), back)

        def place_of(device):
            away = (device % subs) ^ lax.axis_index("sub")
            apart = (device // subs) ^ lax.axis_index("leaf")
            place = 0
            for bit in range(groups.bit_length() - 1):
                place = place * 2 + (apart >> bit) % 2
            return away % 2, away // 2, place

    else:

        def place_of(device):
            return 0, device

        gathered = (lax.all_gather(packed, ("leaf", "sub")),)
        everyone = lax.all_gather(stack, "sub", axis=1, tiled=True)
        factors = prepare(everyone, dim, width)
        near = (lax.psum(from_subtree(lists, factors, leaves), "pair"),)

    return far_field(
        place_of, subs, far_list, parent_far, near, gathered, skeleton, parent_skel, transfer, basis
    )


def solution(mesh):
    placed = (
        P(None, ("groups", "leaf", "sub")),
        P(None, ("groups", "leaf", "sub")),
        P(("groups", "leaf", "sub"), None, None),
        P(("groups", "leaf", "sub"), None, None),
        P(("groups", "leaf", "sub"), None, None),
        P("groups", None, None),
        P(("groups", "leaf"), None),
        P(("groups", "leaf")),
        P(("groups", "leaf", "sub"), None),
        P(("groups", "leaf"), None),
    )
    return jax.shard_map(
        local,
        mesh=mesh,
        in_specs=placed,
        out_specs=P(None, ("groups", "leaf", "sub")),
        check_vma=False,
    )
```

```python
import functools
import math

import jax
import jax.numpy as jnp
from jax import lax
from jax.experimental import pallas as pl
from jax.experimental.pallas import tpu as pltpu
from jax.sharding import PartitionSpec as P

RATE = 0.125 * math.log2(math.e)
ROWS, COLUMNS = 256, 1024
F32, BF16 = jnp.float32, jnp.bfloat16
VMEM = pl.BlockSpec(memory_space=pltpu.VMEM)
ANY = pl.BlockSpec(memory_space=pl.ANY)
HBM = pl.BlockSpec(memory_space=pltpu.HBM)
SMEM = pl.BlockSpec(memory_space=pltpu.SMEM)
PARAMS = pltpu.CompilerParams(vmem_limit_bytes=40 * 1024 * 1024)
NN, NT = (((1,), (0,)), ((), ())), (((1,), (1,)), ((), ()))


def lasts(microseconds):
    return pl.CostEstimate(
        flops=int(1e9 * microseconds), bytes_accessed=int(3e6 * microseconds), transcendentals=0
    )


def mxu(x, y, dims=NN):
    return lax.dot_general(x, y, dims, preferred_element_type=F32)


def split2(x):
    high = x.astype(BF16)
    return high, (x - high.astype(F32)).astype(BF16)


def split3(x):
    high = x.astype(BF16).astype(F32)
    rest = x - high
    middle = rest.astype(BF16).astype(F32)
    return high, middle, (rest - middle).astype(BF16).astype(F32)


def product(x, y, dims=NN):
    rows = x.shape[0]
    x1, x2 = split2(x)
    y1, y2 = split2(y)
    top = mxu(jnp.concatenate([x1, x2], axis=0), y1, dims)
    return top[:rows] + (top[rows:] + mxu(x1, y2, dims))


def source_rows(x):
    a1, a2, a3 = split3(x * (2.0 * RATE))
    return jnp.concatenate([a1, a1, a2, a2, a1, a3], axis=0).T.astype(BF16)


def target_columns(x):
    b1, b2, b3 = split3(x)
    return jnp.concatenate([b1, b2, b1, b2, b3, b1], axis=0).astype(BF16)


def damping(x):
    return jnp.exp2(-RATE * jnp.sum(x * x, axis=0, keepdims=True))


HEAD = 7
EARLY = 2


def share_tiles(near_list, near_count, leaves, tiles):
    turns = near_list.shape[1]
    me = lax.axis_index("sub")
    core = me % 2
    many = 2 * leaves
    first = lax.axis_index("leaf") * near_list.shape[0]
    base = me // 2 * many
    beside = (me ^ 2) * leaves
    cross_at = HEAD + many * turns
    zero = jnp.int32(0)
    local, cross, used_all, marks = zero, zero, zero, []
    for index in range(many):
        side = 1 - core if index < leaves else core
        place = side * leaves + index % leaves
        limit = near_count[base + place]
        used_all = used_all + limit - 1
        for turn in range(1, turns):
            source = near_list[base + place, turn] - first
            used = turn < limit
            near = source - base
            away = source - beside
            tiles[HEAD + local] = place * many + near
            tiles[cross_at + cross] = place * leaves + away
            local = local + (used & (near >= 0) & (near < many)).astype(jnp.int32)
            cross = cross + (used & (away >= 0) & (away < leaves)).astype(jnp.int32)
        if index == leaves - 1:
            marks = [local, cross]
    other = used_all - local - cross
    own_local, own_cross = local - marks[0], cross - marks[1]
    mine = jnp.clip((used_all + 1 - core) // 2 - cross, 0, local)
    total, twin_total = mine + cross, local - mine + other
    after = total - jnp.minimum(total, twin_total) + 1
    after_cross = jnp.clip(after, 0, own_cross)
    after_local = jnp.clip(after - after_cross, 0, jnp.minimum(mine, own_local))
    tiles[0] = jnp.where(core == 0, marks[0] + mine - 1, local - mine)
    tiles[1] = jnp.where(core == 0, -1, 1)
    tiles[2] = local
    tiles[3] = mine - after_local
    tiles[4] = mine
    tiles[5] = cross - after_cross
    tiles[6] = cross


def walk(tiles, many):
    def pick(step):
        at = tiles[0] + tiles[1] * step
        code = tiles[HEAD + jnp.where(at >= tiles[2], at - tiles[2], at)]
        return code // many, code % many

    return pick


def walk_cross(tiles, leaves):
    cross_at = HEAD + (tiles.shape[0] - HEAD) // 2

    def pick(step):
        code = tiles[cross_at + step]
        return code // leaves, code % leaves

    return pick


def coef_kernel(leaves, share, points, vectors, basis, transfer, skeleton, *refs):
    near_list, near_count, packed, stack, tiles = refs[:5]
    bases, moves, skeletons, lists, counts, sems = refs[5:]
    dim, rank = skeletons.shape[1:]
    width = bases.shape[2]
    vecs = vectors.shape[0]
    held = stack.at[dim:]
    pairs = [(near_list, lists), (near_count, counts), (vectors, held), (basis, bases)]
    pairs += [(transfer, moves), (skeleton, skeletons), (points, stack.at[:dim])]
    loads = [pltpu.make_async_copy(src, dst, sems.at[at]) for at, (src, dst) in enumerate(pairs)]
    for load in loads:
        load.start()
    for load in loads[:2]:
        load.wait()
    if share:
        share_tiles(lists, counts, leaves, tiles)
    else:
        tiles[0] = jnp.int32(0)
    for load in loads[2:]:
        load.wait()
    lift = 0.0
    for leaf in range(leaves):
        lanes = slice(leaf * rank, (leaf + 1) * rank)
        coef = product(held[:, leaf * width : (leaf + 1) * width], bases[leaf], NT)
        packed[0:dim, lanes] = skeletons[leaf]
        packed[dim : dim + vecs, lanes] = coef
        lift = lift + product(coef, moves[leaf])
    rows = vecs // leaves
    for piece in range(leaves):
        packed[dim + vecs :, piece * rank : (piece + 1) * rank] = lift[
            piece * rows : (piece + 1) * rows
        ]


def coefficients(share, lists, points, vectors, basis, transfer, skeleton):
    leaves, dim, rank = skeleton.shape
    vecs = vectors.shape[0]
    inputs = [
        pltpu.with_memory_space_constraint(x, pltpu.HBM)
        for x in (points, vectors, basis, transfer, skeleton, *lists)
    ]
    return pl.pallas_call(
        functools.partial(coef_kernel, leaves, share),
        out_shape=[
            jax.ShapeDtypeStruct((dim + vecs + vecs // leaves, leaves * rank), F32),
            jax.ShapeDtypeStruct((dim + vecs, vectors.shape[1]), F32),
            jax.ShapeDtypeStruct((HEAD + 4 * leaves * lists[0].shape[1],), jnp.int32),
        ],
        in_specs=[HBM] * 7,
        out_specs=[VMEM, VMEM, SMEM],
        scratch_shapes=[pltpu.VMEM(x.shape, F32) for x in (basis, transfer, skeleton)]
        + [pltpu.SMEM(x.shape, jnp.int32) for x in lists]
        + [pltpu.SemaphoreType.DMA((7,))],
        compiler_params=PARAMS,
        cost_estimate=lasts(0.5),
        name="coefficients",
    )(*inputs)


def write_source(points, vectors, left, coefs):
    vecs = vectors.shape[0]
    left[...] = source_rows(points)
    high, low = split2(vectors * damping(points))
    coefs[0:vecs] = high
    coefs[vecs:] = low


def write_target(points, right, scale):
    right[...] = target_columns(points)
    scale[...] = damping(points) * points.shape[1] ** -0.5


def leaf_of(stack, dim, width, leaf):
    span = slice(leaf * width, (leaf + 1) * width)
    return stack[:dim, span], stack[dim:, span]


def prepare_kernel(dim, width, stack, left, coefs, right, scale):
    for leaf in range(stack.shape[1] // width):
        points, vectors = leaf_of(stack, dim, width, leaf)
        write_source(points, vectors, left.at[leaf], coefs.at[leaf])
        write_target(points, right.at[leaf], scale.at[leaf])


def source_shapes(sources, dim, vecs, width):
    return [
        jax.ShapeDtypeStruct((sources, width, 6 * dim), BF16),
        jax.ShapeDtypeStruct((sources, 2 * vecs, width), BF16),
    ]


def target_shapes(targets, dim, width):
    return [
        jax.ShapeDtypeStruct((targets, 6 * dim, width), BF16),
        jax.ShapeDtypeStruct((targets, 1, width), F32),
    ]


def prepare(stack, dim, width):
    vecs = stack.shape[0] - dim
    count = stack.shape[1] // width
    return pl.pallas_call(
        functools.partial(prepare_kernel, dim, width),
        out_shape=source_shapes(count, dim, vecs, width) + target_shapes(count, dim, width),
        in_specs=[VMEM],
        out_specs=[VMEM] * 4,
        compiler_params=PARAMS,
        cost_estimate=lasts(0.5),
        name="prepare",
    )(stack)


def run_tiles(todo, pick, left, coefs, right, right_base, totals, totals_base):
    vecs, width = totals.shape[1:]
    chunks = [(y, x) for y in range(0, width, COLUMNS) for x in range(0, width, ROWS)]

    def tile(step, carry):
        slot, source = pick(step)

        def exponent(y, x):
            return mxu(left[source, x : x + ROWS], right[right_base + slot, :, y : y + COLUMNS])

        ahead = exponent(*chunks[0])
        for at, (y, x) in enumerate(chunks):
            power = ahead
            if at + 1 < len(chunks):
                ahead = exponent(*chunks[at + 1])
            high, low = split2(jnp.exp2(power))
            both = coefs[source, :, x : x + ROWS]
            top = mxu(both, high)
            found = top[:vecs] + (top[vecs:] + mxu(both[:vecs], low))
            strip = found if x == 0 else strip + found
            if x + ROWS == width:
                totals[totals_base + slot, :, y : y + COLUMNS] += strip
        return carry

    lax.fori_loop(*todo, tile, 0)


def listed(work, start, sources):
    return lambda step: (work[start + step] // sources, work[start + step] % sources)


def self_kernel(dim, stack, left, coefs, right, scale, totals):
    leaves, _, width = totals.shape
    prepare_kernel(dim, width, stack, left, coefs, right, scale)
    totals[...] = jnp.zeros(totals.shape, F32)
    run_tiles((0, leaves), lambda step: (step, step), left, coefs, right, 0, totals, 0)


def with_self(stack, dim, leaves):
    vecs = stack.shape[0] - dim
    width = stack.shape[1] // leaves
    return pl.pallas_call(
        functools.partial(self_kernel, dim),
        out_shape=source_shapes(leaves, dim, vecs, width)
        + target_shapes(leaves, dim, width)
        + [jax.ShapeDtypeStruct((leaves, vecs, width), F32)],
        in_specs=[VMEM],
        out_specs=[VMEM] * 5,
        compiler_params=PARAMS,
        cost_estimate=lasts(0.5),
        name="near_self",
    )(stack)


def fetch(tiles, held, sem):
    copy = pltpu.make_async_copy(tiles, held, sem)
    copy.start()
    return copy


def list_scratch(tiles):
    return [pltpu.SMEM(tiles.shape, jnp.int32), pltpu.SemaphoreType.DMA]


def local_kernel(leaves, dim, given_tiles, twin_stack, *refs):
    own_left, own_coefs, own_right, own_totals = refs[:4]
    right, scale, totals, left, coefs, tiles, sem = refs[4:]
    lists = fetch(given_tiles, tiles, sem)
    many, _, width = totals.shape
    core = lax.axis_index("sub") % 2
    own, twin = core * leaves, (1 - core) * leaves
    for leaf in range(leaves):
        left[own + leaf] = own_left[leaf]
        coefs[own + leaf] = own_coefs[leaf]
        right[own + leaf] = own_right[leaf]
        totals[own + leaf] = own_totals[leaf]
        totals[twin + leaf] = jnp.zeros(totals.shape[1:], F32)
        points, vectors = leaf_of(twin_stack, dim, width, leaf)
        write_source(points, vectors, left.at[twin + leaf], coefs.at[twin + leaf])
        write_target(points, right.at[twin + leaf], scale.at[leaf])
    lists.wait()
    stop = jnp.minimum(tiles[3], EARLY)
    run_tiles((0, stop), walk(tiles, many), left, coefs, right, 0, totals, 0)


def tiles_local(tiles, twin, own, leaves):
    left, coefs, right, _, totals = own
    vecs, width = totals.shape[1:]
    dim = twin.shape[0] - vecs
    many = 2 * leaves
    return pl.pallas_call(
        functools.partial(local_kernel, leaves, dim),
        out_shape=[
            jax.ShapeDtypeStruct((many, 6 * dim, width), BF16),
            jax.ShapeDtypeStruct((leaves, 1, width), F32),
            jax.ShapeDtypeStruct((many, vecs, width), F32),
        ]
        + source_shapes(many, dim, vecs, width),
        in_specs=[ANY] + [VMEM] * 5,
        out_specs=[VMEM] * 5,
        scratch_shapes=list_scratch(tiles),
        compiler_params=PARAMS,
        cost_estimate=lasts(0.5),
        name="near_local",
    )(tiles, twin, left, coefs, right, totals)


def cross_kernel(leaves, dim, given_tiles, cross_stack, right, scale, begun, *refs):
    local_left, local_coefs, twin_out, left, coefs, own_totals, totals, tiles, sem = refs
    lists = fetch(given_tiles, tiles, sem)
    many, _, width = totals.shape
    core = lax.axis_index("sub") % 2
    own, twin = core * leaves, (1 - core) * leaves
    for leaf in range(leaves):
        points, vectors = leaf_of(cross_stack, dim, width, leaf)
        write_source(points, vectors, left.at[leaf], coefs.at[leaf])
    totals[...] = begun[...]
    lists.wait()
    rest = (jnp.minimum(tiles[3], EARLY), tiles[3])
    run_tiles(rest, walk(tiles, many), local_left, local_coefs, right, 0, totals, 0)
    run_tiles((0, tiles[5]), walk_cross(tiles, leaves), left, coefs, right, 0, totals, 0)
    for leaf in range(leaves):
        twin_out[:, leaf * width : (leaf + 1) * width] = totals[twin + leaf] * scale[leaf]
        own_totals[leaf] = totals[own + leaf]


def tiles_cross(tiles, cross, right, scale, begun, inner):
    many, vecs, width = begun.shape
    leaves = many // 2
    dim = cross.shape[0] - vecs
    return pl.pallas_call(
        functools.partial(cross_kernel, leaves, dim),
        out_shape=[jax.ShapeDtypeStruct((vecs, leaves * width), F32)]
        + source_shapes(leaves, dim, vecs, width)
        + [jax.ShapeDtypeStruct((leaves, vecs, width), F32)],
        in_specs=[ANY] + [VMEM] * 6,
        out_specs=[VMEM] * 4,
        scratch_shapes=[pltpu.VMEM((many, vecs, width), F32)] + list_scratch(tiles),
        compiler_params=PARAMS,
        cost_estimate=lasts(0.5),
        name="near_cross",
    )(tiles, cross, right, scale, begun, *inner)


def after_kernel(leaves, given_tiles, left, coefs, cross_left, cross_coefs, *refs):
    right, scale, begun, out, totals, tiles, sem = refs
    lists = fetch(given_tiles, tiles, sem)
    width = totals.shape[2]
    own = lax.axis_index("sub") % 2 * leaves
    totals[...] = begun[...]

    def own_place(pick):
        def picked(step):
            place, source = pick(step)
            return place - own, source

        return picked

    lists.wait()
    local, cross = own_place(walk(tiles, 2 * leaves)), own_place(walk_cross(tiles, leaves))
    run_tiles((tiles[3], tiles[4]), local, left, coefs, right, 0, totals, 0)
    run_tiles((tiles[5], tiles[6]), cross, cross_left, cross_coefs, right, 0, totals, 0)
    for leaf in range(leaves):
        out[:, leaf * width : (leaf + 1) * width] = totals[leaf] * scale[leaf]


def tiles_after(tiles, local, cross, right, scale, begun):
    leaves, vecs, width = begun.shape
    return pl.pallas_call(
        functools.partial(after_kernel, leaves),
        out_shape=jax.ShapeDtypeStruct((vecs, leaves * width), F32),
        in_specs=[ANY] + [VMEM] * 7,
        out_specs=VMEM,
        scratch_shapes=[pltpu.VMEM((leaves, vecs, width), F32)] + list_scratch(tiles),
        compiler_params=PARAMS,
        cost_estimate=lasts(0.5),
        name="near_after",
    )(tiles, *local, *cross, right, scale, begun)


def list_tiles(near_list, near_count, leaves, target, source_base, sources, work):
    first = lax.axis_index("leaf") * near_list.shape[0]
    pair_size, pair_at = lax.axis_size("pair"), lax.axis_index("pair")
    todo = jnp.int32(0)
    for leaf in range(leaves):
        place = target * leaves + leaf
        limit = near_count[place]
        for turn in range(near_list.shape[1]):
            source = near_list[place, turn] - first - source_base
            wanted = (turn < limit) & (source >= 0) & (source < sources)
            if pair_size > 1:
                wanted = wanted & (pair_at == turn % pair_size)
            work[todo] = leaf * sources + source
            todo = todo + wanted.astype(jnp.int32)
    return todo


def subtree_kernel(leaves, near_list, near_count, left, coefs, right, scale, out, totals, work):
    me = lax.axis_index("sub")
    vecs, width = totals.shape[1:]
    sources = left.shape[0]
    todo = list_tiles(near_list, near_count, leaves, me, 0, sources, work)
    totals[...] = jnp.zeros(totals.shape, F32)
    run_tiles((0, todo), listed(work, 0, sources), left, coefs, right, me * leaves, totals, 0)
    for leaf in range(leaves):
        out[:, leaf * width : (leaf + 1) * width] = totals[leaf] * scale[me * leaves + leaf]


def from_subtree(lists, factors, leaves):
    near_list, near_count = lists
    vecs, width = factors[1].shape[1] // 2, factors[1].shape[2]
    return pl.pallas_call(
        functools.partial(subtree_kernel, leaves),
        out_shape=jax.ShapeDtypeStruct((vecs, leaves * width), F32),
        in_specs=[SMEM, SMEM] + [VMEM] * 4,
        out_specs=VMEM,
        scratch_shapes=[
            pltpu.VMEM((leaves, vecs, width), F32),
            pltpu.SMEM((leaves * near_list.shape[1] + 1,), jnp.int32),
        ],
        compiler_params=PARAMS,
        name="near_subtree",
    )(near_list, near_count, *factors)


def interact(source, coefs, columns, target_damping):
    kernel = jnp.exp2(mxu(source_rows(source), columns))
    return product(coefs * damping(source), kernel) * target_damping


def far_kernel(place_of, leaves, subs, nears, given_far, given_parents, *refs):
    refs, (out, far_list, parent_far, found, sems) = refs[:-5], refs[-5:]
    near, refs = refs[:nears], refs[nears:]
    gathered, (skeleton, parent_skel, transfer, basis) = refs[:-4], refs[-4:]
    copies = [
        fetch(given_far, far_list, sems.at[0]),
        fetch(given_parents, parent_far, sems.at[1]),
    ]
    dim, rank = skeleton.shape[1:]
    width = basis.shape[2]
    vecs = found.shape[1]
    targets = [skeleton[leaf] for leaf in range(leaves)]
    targets.append(parent_skel[lax.axis_index("leaf")])
    columns = [(target_columns(x), damping(x) * rank**-0.5) for x in targets]
    both = [
        jnp.concatenate([basis[leaf], product(transfer[leaf].T, basis[leaf])], axis=0)
        for leaf in range(leaves)
    ]
    for copy in copies:
        copy.wait()

    def block(device):
        which, *index = place_of(device)
        data = gathered[0][tuple(index)]
        for other in range(1, len(gathered)):
            data = jnp.where(which == other, gathered[other][tuple(index)], data)
        return data

    def joined(parts):
        return [jnp.concatenate(part, axis=1) for part in zip(*parts)]

    parts = []
    for turn in range(parent_far.shape[1]):
        parent = parent_far[0, turn]
        lift = block(parent * subs)[dim + vecs :]
        for sub in range(1, subs):
            lift = lift + block(parent * subs + sub)[dim + vecs :]
        pieces = [lift[:, at * rank : (at + 1) * rank] for at in range(leaves)]
        parts.append((parent_skel[parent], jnp.concatenate(pieces, axis=0)))
    upper = interact(*joined(parts), *columns[leaves])

    half = lax.broadcasted_iota(jnp.int32, (vecs, leaves * rank), 1) // rank
    fields = []
    for leaf in range(leaves):
        parts = []
        for turn in range(far_list.shape[1]):
            partner = far_list[leaf, turn]
            data = block(partner // leaves)
            coefs = jnp.where(half == partner % leaves, data[dim : dim + vecs], 0.0)
            parts.append((data[:dim], coefs))
        far = interact(*joined(parts), *columns[leaf])
        fields.append(jnp.concatenate([far, upper], axis=1))

    copies = []
    for leaf in range(leaves):
        span = slice(leaf * width, (leaf + 1) * width)
        total = product(fields[leaf], both[leaf])
        for part in near:
            total = total + part[:, span]
        found[leaf] = total
        copies.append(
            pltpu.make_async_copy(found.at[leaf], out.at[:, pl.ds(leaf * width, width)], sems.at[leaf])
        )
        copies[-1].start()
    for copy in copies:
        copy.wait()


def far_field(place_of, subs, far_list, parent_far, near, gathered, *held):
    basis = held[-1]
    leaves, rank, width = basis.shape
    vecs = near[0].shape[0]
    return pl.pallas_call(
        functools.partial(far_kernel, place_of, leaves, subs, len(near)),
        out_shape=jax.ShapeDtypeStruct((vecs, leaves * width), F32),
        in_specs=[ANY, ANY] + [VMEM] * (len(near) + len(gathered) + 4),
        out_specs=ANY,
        scratch_shapes=[
            pltpu.SMEM(far_list.shape, jnp.int32),
            pltpu.SMEM(parent_far.shape, jnp.int32),
            pltpu.VMEM((leaves, vecs, width), F32),
            pltpu.SemaphoreType.DMA((max(2, leaves),)),
        ],
        compiler_params=PARAMS,
        cost_estimate=lasts(0.5),
        name="far_field",
    )(far_list, parent_far, *near, *gathered, *held)


def swap(x, bit, axis="sub"):
    return lax.ppermute(x, axis, [(at, at ^ bit) for at in range(lax.axis_size(axis))])


def local(
    points,
    vectors,
    basis,
    transfer,
    skeleton,
    parent_skel,
    near_list,
    near_count,
    far_list,
    parent_far,
):
    leaves, _, width = basis.shape
    dim = points.shape[0]
    subs, groups = lax.axis_size("sub"), lax.axis_size("leaf")
    lists = (near_list, near_count)
    split = subs == 4 and lax.axis_size("pair") == 1 and groups in (4, 8, 16)
    packed, stack, tiles = coefficients(split, lists, points, vectors, basis, transfer, skeleton)
    if split:
        twin, cross = swap(stack, 1), swap(stack, 2)
        line = packed[None]
        step = groups
        while step > 1:
            step //= 2
            arrived = swap(line, step, "leaf")
            if step == groups // 2:
                own = with_self(stack, dim, leaves)
                arrived, own = lax.optimization_barrier((arrived, own))
            elif step == groups // 4:
                right, scale, begun, *inner = tiles_local(tiles, twin, own, leaves)
                arrived, begun = lax.optimization_barrier((arrived, begun))
            line = jnp.concatenate([line, arrived])
        beside = swap(line, 2)
        twin_near, *held, begun = tiles_cross(tiles, cross, right, scale, begun, inner)
        back = swap(twin_near, 1)
        beside, twin_near = lax.optimization_barrier((beside, twin_near))
        plane = jnp.stack([line, beside])
        gathered = (plane, swap(plane, 1))
        near = (tiles_after(tiles, inner, held, *own[2:4], begun), back)

        def place_of(device):
            away = (device % subs) ^ lax.axis_index("sub")
            apart = (device // subs) ^ lax.axis_index("leaf")
            place = 0
            for bit in range(groups.bit_length() - 1):
                place = place * 2 + (apart >> bit) % 2
            return away % 2, away // 2, place

    else:

        def place_of(device):
            return 0, device

        gathered = (lax.all_gather(packed, ("leaf", "sub")),)
        everyone = lax.all_gather(stack, "sub", axis=1, tiled=True)
        factors = prepare(everyone, dim, width)
        near = (lax.psum(from_subtree(lists, factors, leaves), "pair"),)

    return far_field(
        place_of, subs, far_list, parent_far, near, gathered, skeleton, parent_skel, transfer, basis
    )


def solution(mesh):
    placed = (
        P(None, ("groups", "leaf", "sub")),
        P(None, ("groups", "leaf", "sub")),
        P(("groups", "leaf", "sub"), None, None),
        P(("groups", "leaf", "sub"), None, None),
        P(("groups", "leaf", "sub"), None, None),
        P("groups", None, None),
        P(("groups", "leaf"), None),
        P(("groups", "leaf")),
        P(("groups", "leaf", "sub"), None),
        P(("groups", "leaf"), None),
    )
    return jax.shard_map(
        local,
        mesh=mesh,
        in_specs=placed,
        out_specs=P(None, ("groups", "leaf", "sub")),
        check_vma=False,
    )
```

```python
import functools
import math

import jax
import jax.numpy as jnp
from jax import lax
from jax.experimental import pallas as pl
from jax.experimental.pallas import tpu as pltpu
from jax.sharding import PartitionSpec as P

RATE = 0.125 * math.log2(math.e)
ROWS, COLUMNS = 256, 1024
F32, BF16 = jnp.float32, jnp.bfloat16
VMEM = pl.BlockSpec(memory_space=pltpu.VMEM)
ANY = pl.BlockSpec(memory_space=pl.ANY)
HBM = pl.BlockSpec(memory_space=pltpu.HBM)
SMEM = pl.BlockSpec(memory_space=pltpu.SMEM)
PARAMS = pltpu.CompilerParams(vmem_limit_bytes=40 * 1024 * 1024)
NN, NT = (((1,), (0,)), ((), ())), (((1,), (1,)), ((), ()))


def lasts(microseconds):
    return pl.CostEstimate(
        flops=int(1e9 * microseconds), bytes_accessed=int(3e6 * microseconds), transcendentals=0
    )


def mxu(x, y, dims=NN):
    return lax.dot_general(x, y, dims, preferred_element_type=F32)


def split2(x):
    high = x.astype(BF16)
    return high, (x - high.astype(F32)).astype(BF16)


def split3(x):
    high = x.astype(BF16).astype(F32)
    rest = x - high
    middle = rest.astype(BF16).astype(F32)
    return high, middle, (rest - middle).astype(BF16).astype(F32)


def product(x, y, dims=NN):
    rows = x.shape[0]
    x1, x2 = split2(x)
    y1, y2 = split2(y)
    top = mxu(jnp.concatenate([x1, x2], axis=0), y1, dims)
    return top[:rows] + (top[rows:] + mxu(x1, y2, dims))


def source_rows(x):
    a1, a2, a3 = split3(x * (2.0 * RATE))
    return jnp.concatenate([a1, a1, a2, a2, a1, a3], axis=0).T.astype(BF16)


def target_columns(x):
    b1, b2, b3 = split3(x)
    return jnp.concatenate([b1, b2, b1, b2, b3, b1], axis=0).astype(BF16)


def damping(x):
    return jnp.exp2(-RATE * jnp.sum(x * x, axis=0, keepdims=True))


HEAD = 7
EARLY = 2


def share_tiles(near_list, near_count, leaves, tiles):
    turns = near_list.shape[1]
    me = lax.axis_index("sub")
    core = me % 2
    many = 2 * leaves
    first = lax.axis_index("leaf") * near_list.shape[0]
    base = me // 2 * many
    beside = (me ^ 2) * leaves
    cross_at = HEAD + many * turns
    zero = jnp.int32(0)
    local, cross, used_all, marks = zero, zero, zero, []
    for index in range(many):
        side = 1 - core if index < leaves else core
        place = side * leaves + index % leaves
        limit = near_count[base + place]
        used_all = used_all + limit - 1
        for turn in range(1, turns):
            source = near_list[base + place, turn] - first
            used = turn < limit
            near = source - base
            away = source - beside
            tiles[HEAD + local] = place * many + near
            tiles[cross_at + cross] = place * leaves + away
            local = local + (used & (near >= 0) & (near < many)).astype(jnp.int32)
            cross = cross + (used & (away >= 0) & (away < leaves)).astype(jnp.int32)
        if index == leaves - 1:
            marks = [local, cross]
    other = used_all - local - cross
    own_local, own_cross = local - marks[0], cross - marks[1]
    mine = jnp.clip((used_all + 1 - core) // 2 - cross, 0, local)
    total, twin_total = mine + cross, local - mine + other
    after = total - jnp.minimum(total, twin_total) + 1
    after_cross = jnp.clip(after, 0, own_cross)
    after_local = jnp.clip(after - after_cross, 0, jnp.minimum(mine, own_local))
    tiles[0] = jnp.where(core == 0, marks[0] + mine - 1, local - mine)
    tiles[1] = jnp.where(core == 0, -1, 1)
    tiles[2] = local
    tiles[3] = mine - after_local
    tiles[4] = mine
    tiles[5] = cross - after_cross
    tiles[6] = cross


def walk(tiles, many):
    def pick(step):
        at = tiles[0] + tiles[1] * step
        code = tiles[HEAD + jnp.where(at >= tiles[2], at - tiles[2], at)]
        return code // many, code % many

    return pick


def walk_cross(tiles, leaves):
    cross_at = HEAD + (tiles.shape[0] - HEAD) // 2

    def pick(step):
        code = tiles[cross_at + step]
        return code // leaves, code % leaves

    return pick


def coef_kernel(leaves, share, points, vectors, basis, transfer, skeleton, *refs):
    near_list, near_count, packed, stack, tiles = refs[:5]
    bases, moves, skeletons, lists, counts, sems = refs[5:]
    dim, rank = skeletons.shape[1:]
    width = bases.shape[2]
    vecs = vectors.shape[0]
    held = stack.at[dim:]
    pairs = [(near_list, lists), (near_count, counts), (vectors, held), (basis, bases)]
    pairs += [(transfer, moves), (skeleton, skeletons), (points, stack.at[:dim])]
    loads = [pltpu.make_async_copy(src, dst, sems.at[at]) for at, (src, dst) in enumerate(pairs)]
    for load in loads:
        load.start()
    for load in loads[:2]:
        load.wait()
    if share:
        share_tiles(lists, counts, leaves, tiles)
    else:
        tiles[0] = jnp.int32(0)
    for load in loads[2:]:
        load.wait()
    lift = 0.0
    for leaf in range(leaves):
        lanes = slice(leaf * rank, (leaf + 1) * rank)
        coef = product(held[:, leaf * width : (leaf + 1) * width], bases[leaf], NT)
        packed[0:dim, lanes] = skeletons[leaf]
        packed[dim : dim + vecs, lanes] = coef
        lift = lift + product(coef, moves[leaf])
    rows = vecs // leaves
    for piece in range(leaves):
        packed[dim + vecs :, piece * rank : (piece + 1) * rank] = lift[
            piece * rows : (piece + 1) * rows
        ]


def coefficients(share, lists, points, vectors, basis, transfer, skeleton):
    leaves, dim, rank = skeleton.shape
    vecs = vectors.shape[0]
    inputs = [
        pltpu.with_memory_space_constraint(x, pltpu.HBM)
        for x in (points, vectors, basis, transfer, skeleton, *lists)
    ]
    return pl.pallas_call(
        functools.partial(coef_kernel, leaves, share),
        out_shape=[
            jax.ShapeDtypeStruct((dim + vecs + vecs // leaves, leaves * rank), F32),
            jax.ShapeDtypeStruct((dim + vecs, vectors.shape[1]), F32),
            jax.ShapeDtypeStruct((HEAD + 4 * leaves * lists[0].shape[1],), jnp.int32),
        ],
        in_specs=[HBM] * 7,
        out_specs=[VMEM, VMEM, SMEM],
        scratch_shapes=[pltpu.VMEM(x.shape, F32) for x in (basis, transfer, skeleton)]
        + [pltpu.SMEM(x.shape, jnp.int32) for x in lists]
        + [pltpu.SemaphoreType.DMA((7,))],
        compiler_params=PARAMS,
        cost_estimate=lasts(0.5),
        name="coefficients",
    )(*inputs)


def write_source(points, vectors, left, coefs):
    vecs = vectors.shape[0]
    left[...] = source_rows(points)
    high, low = split2(vectors * damping(points))
    coefs[0:vecs] = high
    coefs[vecs:] = low


def write_target(points, right, scale):
    right[...] = target_columns(points)
    scale[...] = damping(points) * points.shape[1] ** -0.5


def leaf_of(stack, dim, width, leaf):
    span = slice(leaf * width, (leaf + 1) * width)
    return stack[:dim, span], stack[dim:, span]


def prepare_kernel(dim, width, stack, left, coefs, right, scale):
    for leaf in range(stack.shape[1] // width):
        points, vectors = leaf_of(stack, dim, width, leaf)
        write_source(points, vectors, left.at[leaf], coefs.at[leaf])
        write_target(points, right.at[leaf], scale.at[leaf])


def source_shapes(sources, dim, vecs, width):
    return [
        jax.ShapeDtypeStruct((sources, width, 6 * dim), BF16),
        jax.ShapeDtypeStruct((sources, 2 * vecs, width), BF16),
    ]


def target_shapes(targets, dim, width):
    return [
        jax.ShapeDtypeStruct((targets, 6 * dim, width), BF16),
        jax.ShapeDtypeStruct((targets, 1, width), F32),
    ]


def prepare(stack, dim, width):
    vecs = stack.shape[0] - dim
    count = stack.shape[1] // width
    return pl.pallas_call(
        functools.partial(prepare_kernel, dim, width),
        out_shape=source_shapes(count, dim, vecs, width) + target_shapes(count, dim, width),
        in_specs=[VMEM],
        out_specs=[VMEM] * 4,
        compiler_params=PARAMS,
        cost_estimate=lasts(0.5),
        name="prepare",
    )(stack)


def run_tiles(todo, pick, left, coefs, right, right_base, totals, totals_base):
    vecs, width = totals.shape[1:]
    chunks = [(y, x) for y in range(0, width, COLUMNS) for x in range(0, width, ROWS)]

    def tile(step, carry):
        slot, source = pick(step)

        def exponent(y, x):
            return mxu(left[source, x : x + ROWS], right[right_base + slot, :, y : y + COLUMNS])

        ahead = exponent(*chunks[0])
        for at, (y, x) in enumerate(chunks):
            power = ahead
            if at + 1 < len(chunks):
                ahead = exponent(*chunks[at + 1])
            high, low = split2(jnp.exp2(power))
            both = coefs[source, :, x : x + ROWS]
            top = mxu(both, high)
            found = top[:vecs] + (top[vecs:] + mxu(both[:vecs], low))
            strip = found if x == 0 else strip + found
            if x + ROWS == width:
                totals[totals_base + slot, :, y : y + COLUMNS] += strip
        return carry

    lax.fori_loop(*todo, tile, 0)


def listed(work, start, sources):
    return lambda step: (work[start + step] // sources, work[start + step] % sources)


def self_kernel(dim, stack, left, coefs, right, scale, totals):
    leaves, _, width = totals.shape
    prepare_kernel(dim, width, stack, left, coefs, right, scale)
    totals[...] = jnp.zeros(totals.shape, F32)
    run_tiles((0, leaves), lambda step: (step, step), left, coefs, right, 0, totals, 0)


def with_self(stack, dim, leaves):
    vecs = stack.shape[0] - dim
    width = stack.shape[1] // leaves
    return pl.pallas_call(
        functools.partial(self_kernel, dim),
        out_shape=source_shapes(leaves, dim, vecs, width)
        + target_shapes(leaves, dim, width)
        + [jax.ShapeDtypeStruct((leaves, vecs, width), F32)],
        in_specs=[VMEM],
        out_specs=[VMEM] * 5,
        compiler_params=PARAMS,
        cost_estimate=lasts(0.5),
        name="near_self",
    )(stack)


def fetch(tiles, held, sem):
    copy = pltpu.make_async_copy(tiles, held, sem)
    copy.start()
    return copy


def list_scratch(tiles):
    return [pltpu.SMEM(tiles.shape, jnp.int32), pltpu.SemaphoreType.DMA]


def local_kernel(leaves, dim, given_tiles, twin_stack, *refs):
    own_left, own_coefs, own_right, own_totals = refs[:4]
    right, scale, totals, left, coefs, tiles, sem = refs[4:]
    lists = fetch(given_tiles, tiles, sem)
    many, _, width = totals.shape
    core = lax.axis_index("sub") % 2
    own, twin = core * leaves, (1 - core) * leaves
    for leaf in range(leaves):
        left[own + leaf] = own_left[leaf]
        coefs[own + leaf] = own_coefs[leaf]
        right[own + leaf] = own_right[leaf]
        totals[own + leaf] = own_totals[leaf]
        totals[twin + leaf] = jnp.zeros(totals.shape[1:], F32)
        points, vectors = leaf_of(twin_stack, dim, width, leaf)
        write_source(points, vectors, left.at[twin + leaf], coefs.at[twin + leaf])
        write_target(points, right.at[twin + leaf], scale.at[leaf])
    lists.wait()
    stop = jnp.minimum(tiles[3], EARLY)
    run_tiles((0, stop), walk(tiles, many), left, coefs, right, 0, totals, 0)


def tiles_local(tiles, twin, own, leaves):
    left, coefs, right, _, totals = own
    vecs, width = totals.shape[1:]
    dim = twin.shape[0] - vecs
    many = 2 * leaves
    return pl.pallas_call(
        functools.partial(local_kernel, leaves, dim),
        out_shape=[
            jax.ShapeDtypeStruct((many, 6 * dim, width), BF16),
            jax.ShapeDtypeStruct((leaves, 1, width), F32),
            jax.ShapeDtypeStruct((many, vecs, width), F32),
        ]
        + source_shapes(many, dim, vecs, width),
        in_specs=[ANY] + [VMEM] * 5,
        out_specs=[VMEM] * 5,
        scratch_shapes=list_scratch(tiles),
        compiler_params=PARAMS,
        cost_estimate=lasts(0.5),
        name="near_local",
    )(tiles, twin, left, coefs, right, totals)


def cross_kernel(leaves, dim, given_tiles, cross_stack, right, scale, begun, *refs):
    local_left, local_coefs, twin_out, left, coefs, own_totals, totals, tiles, sem = refs
    lists = fetch(given_tiles, tiles, sem)
    many, _, width = totals.shape
    core = lax.axis_index("sub") % 2
    own, twin = core * leaves, (1 - core) * leaves
    for leaf in range(leaves):
        points, vectors = leaf_of(cross_stack, dim, width, leaf)
        write_source(points, vectors, left.at[leaf], coefs.at[leaf])
    totals[...] = begun[...]
    lists.wait()
    rest = (jnp.minimum(tiles[3], EARLY), tiles[3])
    run_tiles(rest, walk(tiles, many), local_left, local_coefs, right, 0, totals, 0)
    run_tiles((0, tiles[5]), walk_cross(tiles, leaves), left, coefs, right, 0, totals, 0)
    for leaf in range(leaves):
        twin_out[:, leaf * width : (leaf + 1) * width] = totals[twin + leaf] * scale[leaf]
        own_totals[leaf] = totals[own + leaf]


def tiles_cross(tiles, cross, right, scale, begun, inner):
    many, vecs, width = begun.shape
    leaves = many // 2
    dim = cross.shape[0] - vecs
    return pl.pallas_call(
        functools.partial(cross_kernel, leaves, dim),
        out_shape=[jax.ShapeDtypeStruct((vecs, leaves * width), F32)]
        + source_shapes(leaves, dim, vecs, width)
        + [jax.ShapeDtypeStruct((leaves, vecs, width), F32)],
        in_specs=[ANY] + [VMEM] * 6,
        out_specs=[VMEM] * 4,
        scratch_shapes=[pltpu.VMEM((many, vecs, width), F32)] + list_scratch(tiles),
        compiler_params=PARAMS,
        cost_estimate=lasts(0.5),
        name="near_cross",
    )(tiles, cross, right, scale, begun, *inner)


def after_kernel(leaves, given_tiles, left, coefs, cross_left, cross_coefs, *refs):
    right, scale, begun, out, totals, tiles, sem = refs
    lists = fetch(given_tiles, tiles, sem)
    width = totals.shape[2]
    own = lax.axis_index("sub") % 2 * leaves
    totals[...] = begun[...]

    def own_place(pick):
        def picked(step):
            place, source = pick(step)
            return place - own, source

        return picked

    lists.wait()
    local, cross = own_place(walk(tiles, 2 * leaves)), own_place(walk_cross(tiles, leaves))
    run_tiles((tiles[3], tiles[4]), local, left, coefs, right, 0, totals, 0)
    run_tiles((tiles[5], tiles[6]), cross, cross_left, cross_coefs, right, 0, totals, 0)
    for leaf in range(leaves):
        out[:, leaf * width : (leaf + 1) * width] = totals[leaf] * scale[leaf]


def tiles_after(tiles, local, cross, right, scale, begun):
    leaves, vecs, width = begun.shape
    return pl.pallas_call(
        functools.partial(after_kernel, leaves),
        out_shape=jax.ShapeDtypeStruct((vecs, leaves * width), F32),
        in_specs=[ANY] + [VMEM] * 7,
        out_specs=VMEM,
        scratch_shapes=[pltpu.VMEM((leaves, vecs, width), F32)] + list_scratch(tiles),
        compiler_params=PARAMS,
        cost_estimate=lasts(0.5),
        name="near_after",
    )(tiles, *local, *cross, right, scale, begun)


def list_tiles(near_list, near_count, leaves, target, source_base, sources, work):
    first = lax.axis_index("leaf") * near_list.shape[0]
    pair_size, pair_at = lax.axis_size("pair"), lax.axis_index("pair")
    todo = jnp.int32(0)
    for leaf in range(leaves):
        place = target * leaves + leaf
        limit = near_count[place]
        for turn in range(near_list.shape[1]):
            source = near_list[place, turn] - first - source_base
            wanted = (turn < limit) & (source >= 0) & (source < sources)
            if pair_size > 1:
                wanted = wanted & (pair_at == turn % pair_size)
            work[todo] = leaf * sources + source
            todo = todo + wanted.astype(jnp.int32)
    return todo


def subtree_kernel(leaves, near_list, near_count, left, coefs, right, scale, out, totals, work):
    me = lax.axis_index("sub")
    vecs, width = totals.shape[1:]
    sources = left.shape[0]
    todo = list_tiles(near_list, near_count, leaves, me, 0, sources, work)
    totals[...] = jnp.zeros(totals.shape, F32)
    run_tiles((0, todo), listed(work, 0, sources), left, coefs, right, me * leaves, totals, 0)
    for leaf in range(leaves):
        out[:, leaf * width : (leaf + 1) * width] = totals[leaf] * scale[me * leaves + leaf]


def from_subtree(lists, factors, leaves):
    near_list, near_count = lists
    vecs, width = factors[1].shape[1] // 2, factors[1].shape[2]
    return pl.pallas_call(
        functools.partial(subtree_kernel, leaves),
        out_shape=jax.ShapeDtypeStruct((vecs, leaves * width), F32),
        in_specs=[SMEM, SMEM] + [VMEM] * 4,
        out_specs=VMEM,
        scratch_shapes=[
            pltpu.VMEM((leaves, vecs, width), F32),
            pltpu.SMEM((leaves * near_list.shape[1] + 1,), jnp.int32),
        ],
        compiler_params=PARAMS,
        name="near_subtree",
    )(near_list, near_count, *factors)


def interact(source, coefs, rows, target_damping):
    kernel = jnp.exp2(mxu(rows, target_columns(source)))
    return product(coefs * damping(source), kernel, NT) * target_damping


def far_kernel(place_of, leaves, subs, nears, given_far, given_parents, *refs):
    refs, (out, far_list, parent_far, found, sems) = refs[:-5], refs[-5:]
    near, refs = refs[:nears], refs[nears:]
    gathered, (skeleton, parent_skel, transfer, basis) = refs[:-4], refs[-4:]
    copies = [
        fetch(given_far, far_list, sems.at[0]),
        fetch(given_parents, parent_far, sems.at[1]),
    ]
    dim, rank = skeleton.shape[1:]
    width = basis.shape[2]
    vecs = found.shape[1]
    targets = [skeleton[leaf] for leaf in range(leaves)]
    targets.append(parent_skel[lax.axis_index("leaf")])
    factors = [(source_rows(x), damping(x) * rank**-0.5) for x in targets]
    for copy in copies:
        copy.wait()

    def block(device):
        which, *index = place_of(device)
        data = gathered[0][tuple(index)]
        for other in range(1, len(gathered)):
            data = jnp.where(which == other, gathered[other][tuple(index)], data)
        return data

    def joined(parts):
        return [jnp.concatenate(part, axis=1) for part in zip(*parts)]

    parts = []
    for turn in range(parent_far.shape[1]):
        parent = parent_far[0, turn]
        lift = block(parent * subs)[dim + vecs :]
        for sub in range(1, subs):
            lift = lift + block(parent * subs + sub)[dim + vecs :]
        pieces = [lift[:, at * rank : (at + 1) * rank] for at in range(leaves)]
        parts.append((parent_skel[parent], jnp.concatenate(pieces, axis=0)))
    upper = interact(*joined(parts), *factors[leaves])

    half = lax.broadcasted_iota(jnp.int32, (vecs, leaves * rank), 1) // rank
    fields = []
    for leaf in range(leaves):
        parts = []
        for turn in range(far_list.shape[1]):
            partner = far_list[leaf, turn]
            data = block(partner // leaves)
            coefs = jnp.where(half == partner % leaves, data[dim : dim + vecs], 0.0)
            parts.append((data[:dim], coefs))
        far = interact(*joined(parts), *factors[leaf])
        fields.append(far + product(upper, transfer[leaf], NT))

    copies = []
    for leaf in range(leaves):
        span = slice(leaf * width, (leaf + 1) * width)
        total = product(fields[leaf], basis[leaf])
        for part in near:
            total = total + part[:, span]
        found[leaf] = total
        copies.append(
            pltpu.make_async_copy(found.at[leaf], out.at[:, pl.ds(leaf * width, width)], sems.at[leaf])
        )
        copies[-1].start()
    for copy in copies:
        copy.wait()


def far_field(place_of, subs, far_list, parent_far, near, gathered, *held):
    basis = held[-1]
    leaves, rank, width = basis.shape
    vecs = near[0].shape[0]
    return pl.pallas_call(
        functools.partial(far_kernel, place_of, leaves, subs, len(near)),
        out_shape=jax.ShapeDtypeStruct((vecs, leaves * width), F32),
        in_specs=[ANY, ANY] + [VMEM] * (len(near) + len(gathered) + 4),
        out_specs=ANY,
        scratch_shapes=[
            pltpu.SMEM(far_list.shape, jnp.int32),
            pltpu.SMEM(parent_far.shape, jnp.int32),
            pltpu.VMEM((leaves, vecs, width), F32),
            pltpu.SemaphoreType.DMA((max(2, leaves),)),
        ],
        compiler_params=PARAMS,
        cost_estimate=lasts(0.5),
        name="far_field",
    )(far_list, parent_far, *near, *gathered, *held)


def swap(x, bit, axis="sub"):
    return lax.ppermute(x, axis, [(at, at ^ bit) for at in range(lax.axis_size(axis))])


def local(
    points,
    vectors,
    basis,
    transfer,
    skeleton,
    parent_skel,
    near_list,
    near_count,
    far_list,
    parent_far,
):
    leaves, _, width = basis.shape
    dim = points.shape[0]
    subs, groups = lax.axis_size("sub"), lax.axis_size("leaf")
    lists = (near_list, near_count)
    split = subs == 4 and lax.axis_size("pair") == 1 and groups in (4, 8, 16)
    packed, stack, tiles = coefficients(split, lists, points, vectors, basis, transfer, skeleton)
    if split:
        twin, cross = swap(stack, 1), swap(stack, 2)
        line = packed[None]
        step = groups
        while step > 1:
            step //= 2
            arrived = swap(line, step, "leaf")
            if step == groups // 2:
                own = with_self(stack, dim, leaves)
                arrived, own = lax.optimization_barrier((arrived, own))
            elif step == groups // 4:
                right, scale, begun, *inner = tiles_local(tiles, twin, own, leaves)
                arrived, begun = lax.optimization_barrier((arrived, begun))
            line = jnp.concatenate([line, arrived])
        beside = swap(line, 2)
        twin_near, *held, begun = tiles_cross(tiles, cross, right, scale, begun, inner)
        back = swap(twin_near, 1)
        beside, twin_near = lax.optimization_barrier((beside, twin_near))
        plane = jnp.stack([line, beside])
        gathered = (plane, swap(plane, 1))
        near = (tiles_after(tiles, inner, held, *own[2:4], begun), back)

        def place_of(device):
            away = (device % subs) ^ lax.axis_index("sub")
            apart = (device // subs) ^ lax.axis_index("leaf")
            place = 0
            for bit in range(groups.bit_length() - 1):
                place = place * 2 + (apart >> bit) % 2
            return away % 2, away // 2, place

    else:

        def place_of(device):
            return 0, device

        gathered = (lax.all_gather(packed, ("leaf", "sub")),)
        everyone = lax.all_gather(stack, "sub", axis=1, tiled=True)
        factors = prepare(everyone, dim, width)
        near = (lax.psum(from_subtree(lists, factors, leaves), "pair"),)

    return far_field(
        place_of, subs, far_list, parent_far, near, gathered, skeleton, parent_skel, transfer, basis
    )


def solution(mesh):
    placed = (
        P(None, ("groups", "leaf", "sub")),
        P(None, ("groups", "leaf", "sub")),
        P(("groups", "leaf", "sub"), None, None),
        P(("groups", "leaf", "sub"), None, None),
        P(("groups", "leaf", "sub"), None, None),
        P("groups", None, None),
        P(("groups", "leaf"), None),
        P(("groups", "leaf")),
        P(("groups", "leaf", "sub"), None),
        P(("groups", "leaf"), None),
    )
    return jax.shard_map(
        local,
        mesh=mesh,
        in_specs=placed,
        out_specs=P(None, ("groups", "leaf", "sub")),
        check_vma=False,
    )
```

```python
import functools
import math

import jax
import jax.numpy as jnp
from jax import lax
from jax.experimental import pallas as pl
from jax.experimental.pallas import tpu as pltpu
from jax.sharding import PartitionSpec as P

RATE = 0.125 * math.log2(math.e)
ROWS, COLUMNS = 256, 1024
F32, BF16 = jnp.float32, jnp.bfloat16
VMEM = pl.BlockSpec(memory_space=pltpu.VMEM)
ANY = pl.BlockSpec(memory_space=pl.ANY)
HBM = pl.BlockSpec(memory_space=pltpu.HBM)
SMEM = pl.BlockSpec(memory_space=pltpu.SMEM)
PARAMS = pltpu.CompilerParams(vmem_limit_bytes=40 * 1024 * 1024)
NN, NT = (((1,), (0,)), ((), ())), (((1,), (1,)), ((), ()))


def lasts(microseconds):
    return pl.CostEstimate(
        flops=int(1e9 * microseconds), bytes_accessed=int(3e6 * microseconds), transcendentals=0
    )


def mxu(x, y, dims=NN):
    return lax.dot_general(x, y, dims, preferred_element_type=F32)


def divided(value, size):
    if size & (size - 1) == 0:
        return value >> (size.bit_length() - 1), value & (size - 1)
    return lax.div(value, jnp.int32(size)), lax.rem(value, jnp.int32(size))


def split2(x):
    high = x.astype(BF16)
    return high, (x - high.astype(F32)).astype(BF16)


def split3(x):
    high = x.astype(BF16).astype(F32)
    rest = x - high
    middle = rest.astype(BF16).astype(F32)
    return high, middle, (rest - middle).astype(BF16).astype(F32)


def product(x, y, dims=NN):
    rows = x.shape[0]
    x1, x2 = split2(x)
    y1, y2 = split2(y)
    top = mxu(jnp.concatenate([x1, x2], axis=0), y1, dims)
    return top[:rows] + (top[rows:] + mxu(x1, y2, dims))


def source_rows(x):
    a1, a2, a3 = split3(x * (2.0 * RATE))
    return jnp.concatenate([a1, a1, a2, a2, a1, a3], axis=0).T.astype(BF16)


def target_columns(x):
    b1, b2, b3 = split3(x)
    return jnp.concatenate([b1, b2, b1, b2, b3, b1], axis=0).astype(BF16)


def damping(x):
    return jnp.exp2(-RATE * jnp.sum(x * x, axis=0, keepdims=True))


HEAD = 7
EARLY = 2


def share_tiles(near_list, near_count, leaves, tiles):
    turns = near_list.shape[1]
    me = lax.axis_index("sub")
    core = me % 2
    many = 2 * leaves
    first = lax.axis_index("leaf") * near_list.shape[0]
    base = me // 2 * many
    beside = (me ^ 2) * leaves
    cross_at = HEAD + many * turns
    zero = jnp.int32(0)
    local, cross, used_all, marks = zero, zero, zero, []
    for index in range(many):
        side = 1 - core if index < leaves else core
        place = side * leaves + index % leaves
        limit = near_count[base + place]
        used_all = used_all + limit - 1
        for turn in range(1, turns):
            source = near_list[base + place, turn] - first
            used = turn < limit
            near = source - base
            away = source - beside
            tiles[HEAD + local] = place * many + near
            tiles[cross_at + cross] = place * leaves + away
            local = local + (used & (near >= 0) & (near < many)).astype(jnp.int32)
            cross = cross + (used & (away >= 0) & (away < leaves)).astype(jnp.int32)
        if index == leaves - 1:
            marks = [local, cross]
    other = used_all - local - cross
    own_local, own_cross = local - marks[0], cross - marks[1]
    mine = jnp.clip((used_all + 1 - core) // 2 - cross, 0, local)
    total, twin_total = mine + cross, local - mine + other
    after = total - jnp.minimum(total, twin_total) + 1
    after_cross = jnp.clip(after, 0, own_cross)
    after_local = jnp.clip(after - after_cross, 0, jnp.minimum(mine, own_local))
    tiles[0] = jnp.where(core == 0, marks[0] + mine - 1, local - mine)
    tiles[1] = jnp.where(core == 0, -1, 1)
    tiles[2] = local
    tiles[3] = mine - after_local
    tiles[4] = mine
    tiles[5] = cross - after_cross
    tiles[6] = cross


def walk(tiles, many):
    def pick(step):
        at = tiles[0] + tiles[1] * step
        code = tiles[HEAD + jnp.where(at >= tiles[2], at - tiles[2], at)]
        return divided(code, many)

    return pick


def walk_cross(tiles, leaves):
    cross_at = HEAD + (tiles.shape[0] - HEAD) // 2

    def pick(step):
        code = tiles[cross_at + step]
        return divided(code, leaves)

    return pick


def coef_kernel(leaves, share, points, vectors, basis, transfer, skeleton, *refs):
    near_list, near_count, packed, stack, tiles = refs[:5]
    bases, moves, skeletons, lists, counts, sems = refs[5:]
    dim, rank = skeletons.shape[1:]
    width = bases.shape[2]
    vecs = vectors.shape[0]
    held = stack.at[dim:]
    pairs = [(near_list, lists), (near_count, counts), (vectors, held), (basis, bases)]
    pairs += [(transfer, moves), (skeleton, skeletons), (points, stack.at[:dim])]
    loads = [pltpu.make_async_copy(src, dst, sems.at[at]) for at, (src, dst) in enumerate(pairs)]
    for load in loads:
        load.start()
    for load in loads[:2]:
        load.wait()
    if share:
        share_tiles(lists, counts, leaves, tiles)
    else:
        tiles[0] = jnp.int32(0)
    for load in loads[2:]:
        load.wait()
    lift = 0.0
    for leaf in range(leaves):
        lanes = slice(leaf * rank, (leaf + 1) * rank)
        coef = product(held[:, leaf * width : (leaf + 1) * width], bases[leaf], NT)
        packed[0:dim, lanes] = skeletons[leaf]
        packed[dim : dim + vecs, lanes] = coef
        lift = lift + product(coef, moves[leaf])
    rows = vecs // leaves
    for piece in range(leaves):
        packed[dim + vecs :, piece * rank : (piece + 1) * rank] = lift[
            piece * rows : (piece + 1) * rows
        ]


def coefficients(share, lists, points, vectors, basis, transfer, skeleton):
    leaves, dim, rank = skeleton.shape
    vecs = vectors.shape[0]
    inputs = [
        pltpu.with_memory_space_constraint(x, pltpu.HBM)
        for x in (points, vectors, basis, transfer, skeleton, *lists)
    ]
    return pl.pallas_call(
        functools.partial(coef_kernel, leaves, share),
        out_shape=[
            jax.ShapeDtypeStruct((dim + vecs + vecs // leaves, leaves * rank), F32),
            jax.ShapeDtypeStruct((dim + vecs, vectors.shape[1]), F32),
            jax.ShapeDtypeStruct((HEAD + 4 * leaves * lists[0].shape[1],), jnp.int32),
        ],
        in_specs=[HBM] * 7,
        out_specs=[VMEM, VMEM, SMEM],
        scratch_shapes=[pltpu.VMEM(x.shape, F32) for x in (basis, transfer, skeleton)]
        + [pltpu.SMEM(x.shape, jnp.int32) for x in lists]
        + [pltpu.SemaphoreType.DMA((7,))],
        compiler_params=PARAMS,
        cost_estimate=lasts(0.5),
        name="coefficients",
    )(*inputs)


def write_source(points, vectors, left, coefs):
    vecs = vectors.shape[0]
    left[...] = source_rows(points)
    high, low = split2(vectors * damping(points))
    coefs[0:vecs] = high
    coefs[vecs:] = low


def write_target(points, right, scale):
    right[...] = target_columns(points)
    scale[...] = damping(points) * points.shape[1] ** -0.5


def leaf_of(stack, dim, width, leaf):
    span = slice(leaf * width, (leaf + 1) * width)
    return stack[:dim, span], stack[dim:, span]


def prepare_kernel(dim, width, stack, left, coefs, right, scale):
    for leaf in range(stack.shape[1] // width):
        points, vectors = leaf_of(stack, dim, width, leaf)
        write_source(points, vectors, left.at[leaf], coefs.at[leaf])
        write_target(points, right.at[leaf], scale.at[leaf])


def source_shapes(sources, dim, vecs, width):
    return [
        jax.ShapeDtypeStruct((sources, width, 6 * dim), BF16),
        jax.ShapeDtypeStruct((sources, 2 * vecs, width), BF16),
    ]


def target_shapes(targets, dim, width):
    return [
        jax.ShapeDtypeStruct((targets, 6 * dim, width), BF16),
        jax.ShapeDtypeStruct((targets, 1, width), F32),
    ]


def prepare(stack, dim, width):
    vecs = stack.shape[0] - dim
    count = stack.shape[1] // width
    return pl.pallas_call(
        functools.partial(prepare_kernel, dim, width),
        out_shape=source_shapes(count, dim, vecs, width) + target_shapes(count, dim, width),
        in_specs=[VMEM],
        out_specs=[VMEM] * 4,
        compiler_params=PARAMS,
        cost_estimate=lasts(0.5),
        name="prepare",
    )(stack)


def run_tiles(todo, pick, left, coefs, right, right_base, totals, totals_base):
    vecs, width = totals.shape[1:]
    chunks = [(y, x) for y in range(0, width, COLUMNS) for x in range(0, width, ROWS)]

    def tile(step, carry):
        slot, source = pick(step)

        def exponent(y, x):
            return mxu(left[source, x : x + ROWS], right[right_base + slot, :, y : y + COLUMNS])

        ahead = exponent(*chunks[0])
        for at, (y, x) in enumerate(chunks):
            power = ahead
            if at + 1 < len(chunks):
                ahead = exponent(*chunks[at + 1])
            high, low = split2(jnp.exp2(power))
            both = coefs[source, :, x : x + ROWS]
            top = mxu(both, high)
            found = top[:vecs] + (top[vecs:] + mxu(both[:vecs], low))
            strip = found if x == 0 else strip + found
            if x + ROWS == width:
                totals[totals_base + slot, :, y : y + COLUMNS] += strip
        return carry

    lax.fori_loop(*todo, tile, 0)


def listed(work, start, sources):
    return lambda step: (work[start + step] // sources, work[start + step] % sources)


def self_kernel(dim, stack, left, coefs, right, scale, totals):
    leaves, _, width = totals.shape
    prepare_kernel(dim, width, stack, left, coefs, right, scale)
    totals[...] = jnp.zeros(totals.shape, F32)
    run_tiles((0, leaves), lambda step: (step, step), left, coefs, right, 0, totals, 0)


def with_self(stack, dim, leaves):
    vecs = stack.shape[0] - dim
    width = stack.shape[1] // leaves
    return pl.pallas_call(
        functools.partial(self_kernel, dim),
        out_shape=source_shapes(leaves, dim, vecs, width)
        + target_shapes(leaves, dim, width)
        + [jax.ShapeDtypeStruct((leaves, vecs, width), F32)],
        in_specs=[VMEM],
        out_specs=[VMEM] * 5,
        compiler_params=PARAMS,
        cost_estimate=lasts(0.5),
        name="near_self",
    )(stack)


def fetch(tiles, held, sem):
    copy = pltpu.make_async_copy(tiles, held, sem)
    copy.start()
    return copy


def list_scratch(tiles):
    return [pltpu.SMEM(tiles.shape, jnp.int32), pltpu.SemaphoreType.DMA]


def local_kernel(leaves, dim, given_tiles, twin_stack, *refs):
    own_left, own_coefs, own_right, own_totals = refs[:4]
    right, scale, totals, left, coefs, tiles, sem = refs[4:]
    lists = fetch(given_tiles, tiles, sem)
    many, _, width = totals.shape
    core = lax.axis_index("sub") % 2
    own, twin = core * leaves, (1 - core) * leaves
    for leaf in range(leaves):
        left[own + leaf] = own_left[leaf]
        coefs[own + leaf] = own_coefs[leaf]
        right[own + leaf] = own_right[leaf]
        totals[own + leaf] = own_totals[leaf]
        totals[twin + leaf] = jnp.zeros(totals.shape[1:], F32)
        points, vectors = leaf_of(twin_stack, dim, width, leaf)
        write_source(points, vectors, left.at[twin + leaf], coefs.at[twin + leaf])
        write_target(points, right.at[twin + leaf], scale.at[leaf])
    lists.wait()
    stop = jnp.minimum(tiles[3], EARLY)
    run_tiles((0, stop), walk(tiles, many), left, coefs, right, 0, totals, 0)


def tiles_local(tiles, twin, own, leaves):
    left, coefs, right, _, totals = own
    vecs, width = totals.shape[1:]
    dim = twin.shape[0] - vecs
    many = 2 * leaves
    return pl.pallas_call(
        functools.partial(local_kernel, leaves, dim),
        out_shape=[
            jax.ShapeDtypeStruct((many, 6 * dim, width), BF16),
            jax.ShapeDtypeStruct((leaves, 1, width), F32),
            jax.ShapeDtypeStruct((many, vecs, width), F32),
        ]
        + source_shapes(many, dim, vecs, width),
        in_specs=[ANY] + [VMEM] * 5,
        out_specs=[VMEM] * 5,
        scratch_shapes=list_scratch(tiles),
        compiler_params=PARAMS,
        cost_estimate=lasts(0.5),
        name="near_local",
    )(tiles, twin, left, coefs, right, totals)


def cross_kernel(leaves, dim, given_tiles, cross_stack, right, scale, begun, *refs):
    local_left, local_coefs, twin_out, left, coefs, own_totals, totals, tiles, sem = refs
    lists = fetch(given_tiles, tiles, sem)
    many, _, width = totals.shape
    core = lax.axis_index("sub") % 2
    own, twin = core * leaves, (1 - core) * leaves
    for leaf in range(leaves):
        points, vectors = leaf_of(cross_stack, dim, width, leaf)
        write_source(points, vectors, left.at[leaf], coefs.at[leaf])
    totals[...] = begun[...]
    lists.wait()
    rest = (jnp.minimum(tiles[3], EARLY), tiles[3])
    run_tiles(rest, walk(tiles, many), local_left, local_coefs, right, 0, totals, 0)
    run_tiles((0, tiles[5]), walk_cross(tiles, leaves), left, coefs, right, 0, totals, 0)
    for leaf in range(leaves):
        twin_out[:, leaf * width : (leaf + 1) * width] = totals[twin + leaf] * scale[leaf]
        own_totals[leaf] = totals[own + leaf]


def tiles_cross(tiles, cross, right, scale, begun, inner):
    many, vecs, width = begun.shape
    leaves = many // 2
    dim = cross.shape[0] - vecs
    return pl.pallas_call(
        functools.partial(cross_kernel, leaves, dim),
        out_shape=[jax.ShapeDtypeStruct((vecs, leaves * width), F32)]
        + source_shapes(leaves, dim, vecs, width)
        + [jax.ShapeDtypeStruct((leaves, vecs, width), F32)],
        in_specs=[ANY] + [VMEM] * 6,
        out_specs=[VMEM] * 4,
        scratch_shapes=[pltpu.VMEM((many, vecs, width), F32)] + list_scratch(tiles),
        compiler_params=PARAMS,
        cost_estimate=lasts(0.5),
        name="near_cross",
    )(tiles, cross, right, scale, begun, *inner)


def after_kernel(leaves, given_tiles, left, coefs, cross_left, cross_coefs, *refs):
    right, scale, begun, out, totals, tiles, sem = refs
    lists = fetch(given_tiles, tiles, sem)
    width = totals.shape[2]
    own = lax.axis_index("sub") % 2 * leaves
    totals[...] = begun[...]

    def own_place(pick):
        def picked(step):
            place, source = pick(step)
            return place - own, source

        return picked

    lists.wait()
    local, cross = own_place(walk(tiles, 2 * leaves)), own_place(walk_cross(tiles, leaves))
    run_tiles((tiles[3], tiles[4]), local, left, coefs, right, 0, totals, 0)
    run_tiles((tiles[5], tiles[6]), cross, cross_left, cross_coefs, right, 0, totals, 0)
    for leaf in range(leaves):
        out[:, leaf * width : (leaf + 1) * width] = totals[leaf] * scale[leaf]


def tiles_after(tiles, local, cross, right, scale, begun):
    leaves, vecs, width = begun.shape
    return pl.pallas_call(
        functools.partial(after_kernel, leaves),
        out_shape=jax.ShapeDtypeStruct((vecs, leaves * width), F32),
        in_specs=[ANY] + [VMEM] * 7,
        out_specs=VMEM,
        scratch_shapes=[pltpu.VMEM((leaves, vecs, width), F32)] + list_scratch(tiles),
        compiler_params=PARAMS,
        cost_estimate=lasts(0.5),
        name="near_after",
    )(tiles, *local, *cross, right, scale, begun)


def list_tiles(near_list, near_count, leaves, target, source_base, sources, work):
    first = lax.axis_index("leaf") * near_list.shape[0]
    pair_size, pair_at = lax.axis_size("pair"), lax.axis_index("pair")
    todo = jnp.int32(0)
    for leaf in range(leaves):
        place = target * leaves + leaf
        limit = near_count[place]
        for turn in range(near_list.shape[1]):
            source = near_list[place, turn] - first - source_base
            wanted = (turn < limit) & (source >= 0) & (source < sources)
            if pair_size > 1:
                wanted = wanted & (pair_at == turn % pair_size)
            work[todo] = leaf * sources + source
            todo = todo + wanted.astype(jnp.int32)
    return todo


def subtree_kernel(leaves, near_list, near_count, left, coefs, right, scale, out, totals, work):
    me = lax.axis_index("sub")
    vecs, width = totals.shape[1:]
    sources = left.shape[0]
    todo = list_tiles(near_list, near_count, leaves, me, 0, sources, work)
    totals[...] = jnp.zeros(totals.shape, F32)
    run_tiles((0, todo), listed(work, 0, sources), left, coefs, right, me * leaves, totals, 0)
    for leaf in range(leaves):
        out[:, leaf * width : (leaf + 1) * width] = totals[leaf] * scale[me * leaves + leaf]


def from_subtree(lists, factors, leaves):
    near_list, near_count = lists
    vecs, width = factors[1].shape[1] // 2, factors[1].shape[2]
    return pl.pallas_call(
        functools.partial(subtree_kernel, leaves),
        out_shape=jax.ShapeDtypeStruct((vecs, leaves * width), F32),
        in_specs=[SMEM, SMEM] + [VMEM] * 4,
        out_specs=VMEM,
        scratch_shapes=[
            pltpu.VMEM((leaves, vecs, width), F32),
            pltpu.SMEM((leaves * near_list.shape[1] + 1,), jnp.int32),
        ],
        compiler_params=PARAMS,
        name="near_subtree",
    )(near_list, near_count, *factors)


def interact(source, coefs, rows, target_damping):
    kernel = jnp.exp2(mxu(rows, target_columns(source)))
    return product(coefs * damping(source), kernel, NT) * target_damping


def far_kernel(place_of, leaves, subs, nears, given_far, given_parents, *refs):
    refs, (out, far_list, parent_far, found, sems) = refs[:-5], refs[-5:]
    near, refs = refs[:nears], refs[nears:]
    gathered, (skeleton, parent_skel, transfer, basis) = refs[:-4], refs[-4:]
    copies = [
        fetch(given_far, far_list, sems.at[0]),
        fetch(given_parents, parent_far, sems.at[1]),
    ]
    dim, rank = skeleton.shape[1:]
    width = basis.shape[2]
    vecs = found.shape[1]
    targets = [skeleton[leaf] for leaf in range(leaves)]
    targets.append(parent_skel[lax.axis_index("leaf")])
    factors = [(source_rows(x), damping(x) * rank**-0.5) for x in targets]
    for copy in copies:
        copy.wait()

    def block(device):
        which, *index = place_of(device)
        data = gathered[0][tuple(index)]
        for other in range(1, len(gathered)):
            data = jnp.where(which == other, gathered[other][tuple(index)], data)
        return data

    def joined(parts):
        return [jnp.concatenate(part, axis=1) for part in zip(*parts)]

    parts = []
    for turn in range(parent_far.shape[1]):
        parent = parent_far[0, turn]
        lift = block(parent * subs)[dim + vecs :]
        for sub in range(1, subs):
            lift = lift + block(parent * subs + sub)[dim + vecs :]
        pieces = [lift[:, at * rank : (at + 1) * rank] for at in range(leaves)]
        parts.append((parent_skel[parent], jnp.concatenate(pieces, axis=0)))
    upper = interact(*joined(parts), *factors[leaves])

    half = lax.broadcasted_iota(jnp.int32, (vecs, leaves * rank), 1) // rank
    fields = []
    for leaf in range(leaves):
        parts = []
        for turn in range(far_list.shape[1]):
            partner = far_list[leaf, turn]
            device, at = divided(partner, leaves)
            data = block(device)
            coefs = jnp.where(half == at, data[dim : dim + vecs], 0.0)
            parts.append((data[:dim], coefs))
        far = interact(*joined(parts), *factors[leaf])
        fields.append(far + product(upper, transfer[leaf], NT))

    copies = []
    for leaf in range(leaves):
        span = slice(leaf * width, (leaf + 1) * width)
        total = product(fields[leaf], basis[leaf])
        for part in near:
            total = total + part[:, span]
        found[leaf] = total
        copies.append(
            pltpu.make_async_copy(found.at[leaf], out.at[:, pl.ds(leaf * width, width)], sems.at[leaf])
        )
        copies[-1].start()
    for copy in copies:
        copy.wait()


def far_field(place_of, subs, far_list, parent_far, near, gathered, *held):
    basis = held[-1]
    leaves, rank, width = basis.shape
    vecs = near[0].shape[0]
    return pl.pallas_call(
        functools.partial(far_kernel, place_of, leaves, subs, len(near)),
        out_shape=jax.ShapeDtypeStruct((vecs, leaves * width), F32),
        in_specs=[ANY, ANY] + [VMEM] * (len(near) + len(gathered) + 4),
        out_specs=ANY,
        scratch_shapes=[
            pltpu.SMEM(far_list.shape, jnp.int32),
            pltpu.SMEM(parent_far.shape, jnp.int32),
            pltpu.VMEM((leaves, vecs, width), F32),
            pltpu.SemaphoreType.DMA((max(2, leaves),)),
        ],
        compiler_params=PARAMS,
        cost_estimate=lasts(0.5),
        name="far_field",
    )(far_list, parent_far, *near, *gathered, *held)


def swap(x, bit, axis="sub"):
    return lax.ppermute(x, axis, [(at, at ^ bit) for at in range(lax.axis_size(axis))])


def local(
    points,
    vectors,
    basis,
    transfer,
    skeleton,
    parent_skel,
    near_list,
    near_count,
    far_list,
    parent_far,
):
    leaves, _, width = basis.shape
    dim = points.shape[0]
    subs, groups = lax.axis_size("sub"), lax.axis_size("leaf")
    lists = (near_list, near_count)
    split = subs == 4 and lax.axis_size("pair") == 1 and groups in (4, 8, 16)
    packed, stack, tiles = coefficients(split, lists, points, vectors, basis, transfer, skeleton)
    if split:
        twin, cross = swap(stack, 1), swap(stack, 2)
        line = packed[None]
        step = groups
        while step > 1:
            step //= 2
            arrived = swap(line, step, "leaf")
            if step == groups // 2:
                own = with_self(stack, dim, leaves)
                arrived, own = lax.optimization_barrier((arrived, own))
            elif step == groups // 4:
                right, scale, begun, *inner = tiles_local(tiles, twin, own, leaves)
                arrived, begun = lax.optimization_barrier((arrived, begun))
            line = jnp.concatenate([line, arrived])
        beside = swap(line, 2)
        twin_near, *held, begun = tiles_cross(tiles, cross, right, scale, begun, inner)
        back = swap(twin_near, 1)
        beside, twin_near = lax.optimization_barrier((beside, twin_near))
        plane = jnp.stack([line, beside])
        gathered = (plane, swap(plane, 1))
        near = (tiles_after(tiles, inner, held, *own[2:4], begun), back)

        def place_of(device):
            group, sub = divided(device, subs)
            away = sub ^ lax.axis_index("sub")
            apart = group ^ lax.axis_index("leaf")
            place = 0
            for bit in range(groups.bit_length() - 1):
                place = place * 2 + ((apart >> bit) & 1)
            return away & 1, away >> 1, place

    else:

        def place_of(device):
            return 0, device

        gathered = (lax.all_gather(packed, ("leaf", "sub")),)
        everyone = lax.all_gather(stack, "sub", axis=1, tiled=True)
        factors = prepare(everyone, dim, width)
        near = (lax.psum(from_subtree(lists, factors, leaves), "pair"),)

    return far_field(
        place_of, subs, far_list, parent_far, near, gathered, skeleton, parent_skel, transfer, basis
    )


def solution(mesh):
    placed = (
        P(None, ("groups", "leaf", "sub")),
        P(None, ("groups", "leaf", "sub")),
        P(("groups", "leaf", "sub"), None, None),
        P(("groups", "leaf", "sub"), None, None),
        P(("groups", "leaf", "sub"), None, None),
        P("groups", None, None),
        P(("groups", "leaf"), None),
        P(("groups", "leaf")),
        P(("groups", "leaf", "sub"), None),
        P(("groups", "leaf"), None),
    )
    return jax.shard_map(
        local,
        mesh=mesh,
        in_specs=placed,
        out_specs=P(None, ("groups", "leaf", "sub")),
        check_vma=False,
    )
```

```python
import functools
import math

import jax
import jax.numpy as jnp
from jax import lax
from jax.experimental import pallas as pl
from jax.experimental.pallas import tpu as pltpu
from jax.sharding import PartitionSpec as P

RATE = 0.125 * math.log2(math.e)
ROWS, COLUMNS = 256, 1024
F32, BF16 = jnp.float32, jnp.bfloat16
VMEM = pl.BlockSpec(memory_space=pltpu.VMEM)
ANY = pl.BlockSpec(memory_space=pl.ANY)
HBM = pl.BlockSpec(memory_space=pltpu.HBM)
SMEM = pl.BlockSpec(memory_space=pltpu.SMEM)
PARAMS = pltpu.CompilerParams(vmem_limit_bytes=40 * 1024 * 1024)
NN, NT = (((1,), (0,)), ((), ())), (((1,), (1,)), ((), ()))


def lasts(microseconds):
    return pl.CostEstimate(
        flops=int(1e9 * microseconds), bytes_accessed=int(3e6 * microseconds), transcendentals=0
    )


def mxu(x, y, dims=NN):
    return lax.dot_general(x, y, dims, preferred_element_type=F32)


def divided(value, size):
    if size & (size - 1) == 0:
        return value >> (size.bit_length() - 1), value & (size - 1)
    return lax.div(value, jnp.int32(size)), lax.rem(value, jnp.int32(size))


def split2(x):
    high = x.astype(BF16)
    return high, (x - high.astype(F32)).astype(BF16)


def split3(x):
    high = x.astype(BF16).astype(F32)
    rest = x - high
    middle = rest.astype(BF16).astype(F32)
    return high, middle, (rest - middle).astype(BF16).astype(F32)


def product(x, y, dims=NN):
    rows = x.shape[0]
    x1, x2 = split2(x)
    y1, y2 = split2(y)
    top = mxu(jnp.concatenate([x1, x2], axis=0), y1, dims)
    return top[:rows] + (top[rows:] + mxu(x1, y2, dims))


def source_rows(x):
    a1, a2, a3 = split3(x * (2.0 * RATE))
    return jnp.concatenate([a1, a1, a2, a2, a1, a3], axis=0).T.astype(BF16)


def target_columns(x):
    b1, b2, b3 = split3(x)
    return jnp.concatenate([b1, b2, b1, b2, b3, b1], axis=0).astype(BF16)


def damping(x):
    return jnp.exp2(-RATE * jnp.sum(x * x, axis=0, keepdims=True))


HEAD = 7
EARLY = 2


def share_tiles(near_list, near_count, leaves, tiles):
    turns = near_list.shape[1]
    me = lax.axis_index("sub")
    core = me % 2
    many = 2 * leaves
    first = lax.axis_index("leaf") * near_list.shape[0]
    base = me // 2 * many
    beside = (me ^ 2) * leaves
    cross_at = HEAD + many * turns
    zero = jnp.int32(0)
    local, cross, used_all, marks = zero, zero, zero, []
    for index in range(many):
        side = 1 - core if index < leaves else core
        place = side * leaves + index % leaves
        limit = near_count[base + place]
        used_all = used_all + limit - 1
        for turn in range(1, turns):
            source = near_list[base + place, turn] - first
            used = turn < limit
            near = source - base
            away = source - beside
            tiles[HEAD + local] = place * many + near
            tiles[cross_at + cross] = place * leaves + away
            local = local + (used & (near >= 0) & (near < many)).astype(jnp.int32)
            cross = cross + (used & (away >= 0) & (away < leaves)).astype(jnp.int32)
        if index == leaves - 1:
            marks = [local, cross]
    other = used_all - local - cross
    own_local, own_cross = local - marks[0], cross - marks[1]
    mine = jnp.clip((used_all + 1 - core) // 2 - cross, 0, local)
    total, twin_total = mine + cross, local - mine + other
    after = total - jnp.minimum(total, twin_total) + 1
    after_cross = jnp.clip(after, 0, own_cross)
    after_local = jnp.clip(after - after_cross, 0, jnp.minimum(mine, own_local))
    tiles[0] = jnp.where(core == 0, marks[0] + mine - 1, local - mine)
    tiles[1] = jnp.where(core == 0, -1, 1)
    tiles[2] = local
    tiles[3] = mine - after_local
    tiles[4] = mine
    tiles[5] = cross - after_cross
    tiles[6] = cross


def walk(tiles, many):
    def pick(step):
        at = tiles[0] + tiles[1] * step
        code = tiles[HEAD + jnp.where(at >= tiles[2], at - tiles[2], at)]
        return divided(code, many)

    return pick


def walk_cross(tiles, leaves):
    cross_at = HEAD + (tiles.shape[0] - HEAD) // 2

    def pick(step):
        code = tiles[cross_at + step]
        return divided(code, leaves)

    return pick


def coef_kernel(leaves, share, points, vectors, basis, transfer, skeleton, *refs):
    near_list, near_count, packed, stack, tiles = refs[:5]
    bases, moves, skeletons, lists, counts, sems = refs[5:]
    dim, rank = skeletons.shape[1:]
    width = bases.shape[2]
    vecs = vectors.shape[0]
    held = stack.at[dim:]
    pairs = [(near_list, lists), (near_count, counts), (vectors, held), (basis, bases)]
    pairs += [(transfer, moves), (skeleton, skeletons), (points, stack.at[:dim])]
    loads = [pltpu.make_async_copy(src, dst, sems.at[at]) for at, (src, dst) in enumerate(pairs)]
    for load in loads:
        load.start()
    for load in loads[:2]:
        load.wait()
    if share:
        share_tiles(lists, counts, leaves, tiles)
    else:
        tiles[0] = jnp.int32(0)
    for load in loads[2:]:
        load.wait()
    lift = 0.0
    for leaf in range(leaves):
        lanes = slice(leaf * rank, (leaf + 1) * rank)
        coef = product(held[:, leaf * width : (leaf + 1) * width], bases[leaf], NT)
        packed[0:dim, lanes] = skeletons[leaf]
        packed[dim : dim + vecs, lanes] = coef
        lift = lift + product(coef, moves[leaf])
    rows = vecs // leaves
    for piece in range(leaves):
        packed[dim + vecs :, piece * rank : (piece + 1) * rank] = lift[
            piece * rows : (piece + 1) * rows
        ]


def coefficients(share, lists, points, vectors, basis, transfer, skeleton):
    leaves, dim, rank = skeleton.shape
    vecs = vectors.shape[0]
    inputs = [
        pltpu.with_memory_space_constraint(x, pltpu.HBM)
        for x in (points, vectors, basis, transfer, skeleton, *lists)
    ]
    return pl.pallas_call(
        functools.partial(coef_kernel, leaves, share),
        out_shape=[
            jax.ShapeDtypeStruct((dim + vecs + vecs // leaves, leaves * rank), F32),
            jax.ShapeDtypeStruct((dim + vecs, vectors.shape[1]), F32),
            jax.ShapeDtypeStruct((HEAD + 4 * leaves * lists[0].shape[1],), jnp.int32),
        ],
        in_specs=[HBM] * 7,
        out_specs=[VMEM, VMEM, SMEM],
        scratch_shapes=[pltpu.VMEM(x.shape, F32) for x in (basis, transfer, skeleton)]
        + [pltpu.SMEM(x.shape, jnp.int32) for x in lists]
        + [pltpu.SemaphoreType.DMA((7,))],
        compiler_params=PARAMS,
        cost_estimate=lasts(0.5),
        name="coefficients",
    )(*inputs)


def write_source(points, vectors, left, coefs):
    vecs = vectors.shape[0]
    left[...] = source_rows(points)
    high, low = split2(vectors * damping(points))
    coefs[0:vecs] = high
    coefs[vecs:] = low


def write_target(points, right, scale):
    right[...] = target_columns(points)
    scale[...] = damping(points) * points.shape[1] ** -0.5


def leaf_of(stack, dim, width, leaf):
    span = slice(leaf * width, (leaf + 1) * width)
    return stack[:dim, span], stack[dim:, span]


def prepare_kernel(dim, width, stack, left, coefs, right, scale):
    for leaf in range(stack.shape[1] // width):
        points, vectors = leaf_of(stack, dim, width, leaf)
        write_source(points, vectors, left.at[leaf], coefs.at[leaf])
        write_target(points, right.at[leaf], scale.at[leaf])


def source_shapes(sources, dim, vecs, width):
    return [
        jax.ShapeDtypeStruct((sources, width, 6 * dim), BF16),
        jax.ShapeDtypeStruct((sources, 2 * vecs, width), BF16),
    ]


def target_shapes(targets, dim, width):
    return [
        jax.ShapeDtypeStruct((targets, 6 * dim, width), BF16),
        jax.ShapeDtypeStruct((targets, 1, width), F32),
    ]


def prepare(stack, dim, width):
    vecs = stack.shape[0] - dim
    count = stack.shape[1] // width
    return pl.pallas_call(
        functools.partial(prepare_kernel, dim, width),
        out_shape=source_shapes(count, dim, vecs, width) + target_shapes(count, dim, width),
        in_specs=[VMEM],
        out_specs=[VMEM] * 4,
        compiler_params=PARAMS,
        cost_estimate=lasts(0.5),
        name="prepare",
    )(stack)


def run_tiles(todo, pick, left, coefs, right, right_base, totals, totals_base, unroll=1):
    vecs, width = totals.shape[1:]
    chunks = [(y, x) for y in range(0, width, COLUMNS) for x in range(0, width, ROWS)]

    def tile(step, carry):
        slot, source = pick(step)

        def exponent(y, x):
            return mxu(left[source, x : x + ROWS], right[right_base + slot, :, y : y + COLUMNS])

        ahead = exponent(*chunks[0])
        for at, (y, x) in enumerate(chunks):
            power = ahead
            if at + 1 < len(chunks):
                ahead = exponent(*chunks[at + 1])
            high, low = split2(jnp.exp2(power))
            both = coefs[source, :, x : x + ROWS]
            top = mxu(both, high)
            found = top[:vecs] + (top[vecs:] + mxu(both[:vecs], low))
            strip = found if x == 0 else strip + found
            if x + ROWS == width:
                totals[totals_base + slot, :, y : y + COLUMNS] += strip
        return carry

    lax.fori_loop(*todo, tile, 0, **({} if unroll == 1 else {"unroll": unroll}))


def listed(work, start, sources):
    return lambda step: (work[start + step] // sources, work[start + step] % sources)


def self_kernel(dim, stack, left, coefs, right, scale, totals):
    leaves, _, width = totals.shape
    prepare_kernel(dim, width, stack, left, coefs, right, scale)
    totals[...] = jnp.zeros(totals.shape, F32)
    run_tiles((0, leaves), lambda at: (at, at), left, coefs, right, 0, totals, 0, unroll=leaves)


def with_self(stack, dim, leaves):
    vecs = stack.shape[0] - dim
    width = stack.shape[1] // leaves
    return pl.pallas_call(
        functools.partial(self_kernel, dim),
        out_shape=source_shapes(leaves, dim, vecs, width)
        + target_shapes(leaves, dim, width)
        + [jax.ShapeDtypeStruct((leaves, vecs, width), F32)],
        in_specs=[VMEM],
        out_specs=[VMEM] * 5,
        compiler_params=PARAMS,
        cost_estimate=lasts(0.5),
        name="near_self",
    )(stack)


def fetch(tiles, held, sem):
    copy = pltpu.make_async_copy(tiles, held, sem)
    copy.start()
    return copy


def list_scratch(tiles):
    return [pltpu.SMEM(tiles.shape, jnp.int32), pltpu.SemaphoreType.DMA]


def local_kernel(leaves, dim, given_tiles, twin_stack, *refs):
    own_left, own_coefs, own_right, own_totals = refs[:4]
    right, scale, totals, left, coefs, tiles, sem = refs[4:]
    lists = fetch(given_tiles, tiles, sem)
    many, _, width = totals.shape
    core = lax.axis_index("sub") % 2
    own, twin = core * leaves, (1 - core) * leaves
    for leaf in range(leaves):
        left[own + leaf] = own_left[leaf]
        coefs[own + leaf] = own_coefs[leaf]
        right[own + leaf] = own_right[leaf]
        totals[own + leaf] = own_totals[leaf]
        totals[twin + leaf] = jnp.zeros(totals.shape[1:], F32)
        points, vectors = leaf_of(twin_stack, dim, width, leaf)
        write_source(points, vectors, left.at[twin + leaf], coefs.at[twin + leaf])
        write_target(points, right.at[twin + leaf], scale.at[leaf])
    lists.wait()
    stop = jnp.minimum(tiles[3], EARLY)
    run_tiles((0, stop), walk(tiles, many), left, coefs, right, 0, totals, 0)


def tiles_local(tiles, twin, own, leaves):
    left, coefs, right, _, totals = own
    vecs, width = totals.shape[1:]
    dim = twin.shape[0] - vecs
    many = 2 * leaves
    return pl.pallas_call(
        functools.partial(local_kernel, leaves, dim),
        out_shape=[
            jax.ShapeDtypeStruct((many, 6 * dim, width), BF16),
            jax.ShapeDtypeStruct((leaves, 1, width), F32),
            jax.ShapeDtypeStruct((many, vecs, width), F32),
        ]
        + source_shapes(many, dim, vecs, width),
        in_specs=[ANY] + [VMEM] * 5,
        out_specs=[VMEM] * 5,
        scratch_shapes=list_scratch(tiles),
        compiler_params=PARAMS,
        cost_estimate=lasts(0.5),
        name="near_local",
    )(tiles, twin, left, coefs, right, totals)


def cross_kernel(leaves, dim, given_tiles, cross_stack, right, scale, begun, *refs):
    local_left, local_coefs, twin_out, left, coefs, own_totals, totals, tiles, sem = refs
    lists = fetch(given_tiles, tiles, sem)
    many, _, width = totals.shape
    core = lax.axis_index("sub") % 2
    own, twin = core * leaves, (1 - core) * leaves
    for leaf in range(leaves):
        points, vectors = leaf_of(cross_stack, dim, width, leaf)
        write_source(points, vectors, left.at[leaf], coefs.at[leaf])
    totals[...] = begun[...]
    lists.wait()
    rest = (jnp.minimum(tiles[3], EARLY), tiles[3])
    run_tiles(rest, walk(tiles, many), local_left, local_coefs, right, 0, totals, 0)
    run_tiles((0, tiles[5]), walk_cross(tiles, leaves), left, coefs, right, 0, totals, 0)
    for leaf in range(leaves):
        twin_out[:, leaf * width : (leaf + 1) * width] = totals[twin + leaf] * scale[leaf]
        own_totals[leaf] = totals[own + leaf]


def tiles_cross(tiles, cross, right, scale, begun, inner):
    many, vecs, width = begun.shape
    leaves = many // 2
    dim = cross.shape[0] - vecs
    return pl.pallas_call(
        functools.partial(cross_kernel, leaves, dim),
        out_shape=[jax.ShapeDtypeStruct((vecs, leaves * width), F32)]
        + source_shapes(leaves, dim, vecs, width)
        + [jax.ShapeDtypeStruct((leaves, vecs, width), F32)],
        in_specs=[ANY] + [VMEM] * 6,
        out_specs=[VMEM] * 4,
        scratch_shapes=[pltpu.VMEM((many, vecs, width), F32)] + list_scratch(tiles),
        compiler_params=PARAMS,
        cost_estimate=lasts(0.5),
        name="near_cross",
    )(tiles, cross, right, scale, begun, *inner)


def after_kernel(leaves, given_tiles, left, coefs, cross_left, cross_coefs, *refs):
    right, scale, begun, out, totals, tiles, sem = refs
    lists = fetch(given_tiles, tiles, sem)
    width = totals.shape[2]
    own = lax.axis_index("sub") % 2 * leaves
    totals[...] = begun[...]

    def own_place(pick):
        def picked(step):
            place, source = pick(step)
            return place - own, source

        return picked

    lists.wait()
    local, cross = own_place(walk(tiles, 2 * leaves)), own_place(walk_cross(tiles, leaves))
    run_tiles((tiles[3], tiles[4]), local, left, coefs, right, 0, totals, 0)
    run_tiles((tiles[5], tiles[6]), cross, cross_left, cross_coefs, right, 0, totals, 0)
    for leaf in range(leaves):
        out[:, leaf * width : (leaf + 1) * width] = totals[leaf] * scale[leaf]


def tiles_after(tiles, local, cross, right, scale, begun):
    leaves, vecs, width = begun.shape
    return pl.pallas_call(
        functools.partial(after_kernel, leaves),
        out_shape=jax.ShapeDtypeStruct((vecs, leaves * width), F32),
        in_specs=[ANY] + [VMEM] * 7,
        out_specs=VMEM,
        scratch_shapes=[pltpu.VMEM((leaves, vecs, width), F32)] + list_scratch(tiles),
        compiler_params=PARAMS,
        cost_estimate=lasts(0.5),
        name="near_after",
    )(tiles, *local, *cross, right, scale, begun)


def list_tiles(near_list, near_count, leaves, target, source_base, sources, work):
    first = lax.axis_index("leaf") * near_list.shape[0]
    pair_size, pair_at = lax.axis_size("pair"), lax.axis_index("pair")
    todo = jnp.int32(0)
    for leaf in range(leaves):
        place = target * leaves + leaf
        limit = near_count[place]
        for turn in range(near_list.shape[1]):
            source = near_list[place, turn] - first - source_base
            wanted = (turn < limit) & (source >= 0) & (source < sources)
            if pair_size > 1:
                wanted = wanted & (pair_at == turn % pair_size)
            work[todo] = leaf * sources + source
            todo = todo + wanted.astype(jnp.int32)
    return todo


def subtree_kernel(leaves, near_list, near_count, left, coefs, right, scale, out, totals, work):
    me = lax.axis_index("sub")
    vecs, width = totals.shape[1:]
    sources = left.shape[0]
    todo = list_tiles(near_list, near_count, leaves, me, 0, sources, work)
    totals[...] = jnp.zeros(totals.shape, F32)
    run_tiles((0, todo), listed(work, 0, sources), left, coefs, right, me * leaves, totals, 0)
    for leaf in range(leaves):
        out[:, leaf * width : (leaf + 1) * width] = totals[leaf] * scale[me * leaves + leaf]


def from_subtree(lists, factors, leaves):
    near_list, near_count = lists
    vecs, width = factors[1].shape[1] // 2, factors[1].shape[2]
    return pl.pallas_call(
        functools.partial(subtree_kernel, leaves),
        out_shape=jax.ShapeDtypeStruct((vecs, leaves * width), F32),
        in_specs=[SMEM, SMEM] + [VMEM] * 4,
        out_specs=VMEM,
        scratch_shapes=[
            pltpu.VMEM((leaves, vecs, width), F32),
            pltpu.SMEM((leaves * near_list.shape[1] + 1,), jnp.int32),
        ],
        compiler_params=PARAMS,
        name="near_subtree",
    )(near_list, near_count, *factors)


def interact(source, coefs, rows, target_damping):
    kernel = jnp.exp2(mxu(rows, target_columns(source)))
    return product(coefs * damping(source), kernel, NT) * target_damping


def far_kernel(place_of, leaves, subs, nears, given_far, given_parents, *refs):
    refs, (out, far_list, parent_far, found, sems) = refs[:-5], refs[-5:]
    near, refs = refs[:nears], refs[nears:]
    gathered, (skeleton, parent_skel, transfer, basis) = refs[:-4], refs[-4:]
    copies = [
        fetch(given_far, far_list, sems.at[0]),
        fetch(given_parents, parent_far, sems.at[1]),
    ]
    dim, rank = skeleton.shape[1:]
    width = basis.shape[2]
    vecs = found.shape[1]
    targets = [skeleton[leaf] for leaf in range(leaves)]
    targets.append(parent_skel[lax.axis_index("leaf")])
    factors = [(source_rows(x), damping(x) * rank**-0.5) for x in targets]
    for copy in copies:
        copy.wait()

    def block(device):
        which, *index = place_of(device)
        data = gathered[0][tuple(index)]
        for other in range(1, len(gathered)):
            data = jnp.where(which == other, gathered[other][tuple(index)], data)
        return data

    def joined(parts):
        return [jnp.concatenate(part, axis=1) for part in zip(*parts)]

    parts = []
    for turn in range(parent_far.shape[1]):
        parent = parent_far[0, turn]
        lift = block(parent * subs)[dim + vecs :]
        for sub in range(1, subs):
            lift = lift + block(parent * subs + sub)[dim + vecs :]
        pieces = [lift[:, at * rank : (at + 1) * rank] for at in range(leaves)]
        parts.append((parent_skel[parent], jnp.concatenate(pieces, axis=0)))
    upper = interact(*joined(parts), *factors[leaves])

    half = lax.broadcasted_iota(jnp.int32, (vecs, leaves * rank), 1) // rank
    fields = []
    for leaf in range(leaves):
        parts = []
        for turn in range(far_list.shape[1]):
            partner = far_list[leaf, turn]
            device, at = divided(partner, leaves)
            data = block(device)
            coefs = jnp.where(half == at, data[dim : dim + vecs], 0.0)
            parts.append((data[:dim], coefs))
        far = interact(*joined(parts), *factors[leaf])
        fields.append(far + product(upper, transfer[leaf], NT))

    copies = []
    for leaf in range(leaves):
        span = slice(leaf * width, (leaf + 1) * width)
        total = product(fields[leaf], basis[leaf])
        for part in near:
            total = total + part[:, span]
        found[leaf] = total
        copies.append(
            pltpu.make_async_copy(found.at[leaf], out.at[:, pl.ds(leaf * width, width)], sems.at[leaf])
        )
        copies[-1].start()
    for copy in copies:
        copy.wait()


def far_field(place_of, subs, far_list, parent_far, near, gathered, *held):
    basis = held[-1]
    leaves, rank, width = basis.shape
    vecs = near[0].shape[0]
    return pl.pallas_call(
        functools.partial(far_kernel, place_of, leaves, subs, len(near)),
        out_shape=jax.ShapeDtypeStruct((vecs, leaves * width), F32),
        in_specs=[ANY, ANY] + [VMEM] * (len(near) + len(gathered) + 4),
        out_specs=ANY,
        scratch_shapes=[
            pltpu.SMEM(far_list.shape, jnp.int32),
            pltpu.SMEM(parent_far.shape, jnp.int32),
            pltpu.VMEM((leaves, vecs, width), F32),
            pltpu.SemaphoreType.DMA((max(2, leaves),)),
        ],
        compiler_params=PARAMS,
        cost_estimate=lasts(0.5),
        name="far_field",
    )(far_list, parent_far, *near, *gathered, *held)


def swap(x, bit, axis="sub"):
    return lax.ppermute(x, axis, [(at, at ^ bit) for at in range(lax.axis_size(axis))])


def local(
    points,
    vectors,
    basis,
    transfer,
    skeleton,
    parent_skel,
    near_list,
    near_count,
    far_list,
    parent_far,
):
    leaves, _, width = basis.shape
    dim = points.shape[0]
    subs, groups = lax.axis_size("sub"), lax.axis_size("leaf")
    lists = (near_list, near_count)
    split = subs == 4 and lax.axis_size("pair") == 1 and groups in (4, 8, 16)
    packed, stack, tiles = coefficients(split, lists, points, vectors, basis, transfer, skeleton)
    if split:
        twin, cross = swap(stack, 1), swap(stack, 2)
        line = packed[None]
        step = groups
        while step > 1:
            step //= 2
            arrived = swap(line, step, "leaf")
            if step == groups // 2:
                own = with_self(stack, dim, leaves)
                arrived, own = lax.optimization_barrier((arrived, own))
            elif step == groups // 4:
                right, scale, begun, *inner = tiles_local(tiles, twin, own, leaves)
                arrived, begun = lax.optimization_barrier((arrived, begun))
            line = jnp.concatenate([line, arrived])
        beside = swap(line, 2)
        twin_near, *held, begun = tiles_cross(tiles, cross, right, scale, begun, inner)
        back = swap(twin_near, 1)
        beside, twin_near = lax.optimization_barrier((beside, twin_near))
        plane = jnp.stack([line, beside])
        gathered = (plane, swap(plane, 1))
        near = (tiles_after(tiles, inner, held, *own[2:4], begun), back)

        def place_of(device):
            group, sub = divided(device, subs)
            away = sub ^ lax.axis_index("sub")
            apart = group ^ lax.axis_index("leaf")
            place = 0
            for bit in range(groups.bit_length() - 1):
                place = place * 2 + ((apart >> bit) & 1)
            return away & 1, away >> 1, place

    else:

        def place_of(device):
            return 0, device

        gathered = (lax.all_gather(packed, ("leaf", "sub")),)
        everyone = lax.all_gather(stack, "sub", axis=1, tiled=True)
        factors = prepare(everyone, dim, width)
        near = (lax.psum(from_subtree(lists, factors, leaves), "pair"),)

    return far_field(
        place_of, subs, far_list, parent_far, near, gathered, skeleton, parent_skel, transfer, basis
    )


def solution(mesh):
    placed = (
        P(None, ("groups", "leaf", "sub")),
        P(None, ("groups", "leaf", "sub")),
        P(("groups", "leaf", "sub"), None, None),
        P(("groups", "leaf", "sub"), None, None),
        P(("groups", "leaf", "sub"), None, None),
        P("groups", None, None),
        P(("groups", "leaf"), None),
        P(("groups", "leaf")),
        P(("groups", "leaf", "sub"), None),
        P(("groups", "leaf"), None),
    )
    return jax.shard_map(
        local,
        mesh=mesh,
        in_specs=placed,
        out_specs=P(None, ("groups", "leaf", "sub")),
        check_vma=False,
    )
```
